256 devices in a mesh: sub: 16 (over z_hi, x, core), tile: 16 (over y, z_lo).
Axes of the slice: x: 4, y: 4, z: 8 (z_hi: 2, z_lo: 4; z = z_hi * 4 + z_lo), core: 2. Of those that a mesh axis runs over, the one named last changes fastest.
Arguments:
- echoes: bfloat16 [8192, 2, 8192], P(('sub', 'tile')), may hold values from -6 to 6
- chirp_ref: bfloat16 [2, 2048], replicated, may hold values from -0.09375 to 0.09375
- band_starts: int32 [32, 16], P('sub'), may hold values from 0 to 8064
- doppler_rates: float32 [16, 512], P('sub'), may hold values from -4096 to 4096
- slot_pulse: int32 [16, 2, 256], P('sub'), may hold values from 0 to 255, each once within a row
- interp_weights: bfloat16 [32, 2, 128, 64, 2048], P('sub', None, None, 'tile'), may hold values from -0.00390625 to 0.00390625
Outputs:
- sar_image: float32 [2, 64, 2048], P(None, 'tile', 'sub')
The draws below stay inside these ranges and needn't reach their ends.
Inputs may be any that keep to these rules, and one draw needn't show every extreme that they name: `band_starts`: a band of 128 bins from each start lies inside the pulse of 8192 samples. `slot_pulse`: for each group and block, the 256 slots name each of the block's pulses once.
All inputs are finite; a program needn't handle non-finite values.
Results may differ from the reference program's by a relative error of at most 0.0037.
Values may be sent and summed in bfloat16 or wider, within the bound.
No kernel may reach another device: no remote copies, remote signals or barrier semaphores. Data moves between devices by JAX's collectives and lax.ppermute only.
A program may use at most 128 MiB of HBM per device.

```python
import jax
import jax.numpy as jnp
from jax import lax

NS = 8192
NC = 2048
BAND = 128
NB = 2
P_BLK_DEV = 16
ROWS = 4
PB = 256
P_GRP = 512
NPUL = 8192
NBLK = 32
COLS = 2048
IMG_ROWS = 64
N_SUB = 16
N_TILE = 16


def with_ends(entries, rng, low, high):
    extent = entries.shape
    place = [jax.random.randint(jax.random.fold_in(rng, axis), (), 0, extent[axis]) for axis in range(len(extent))]
    entries = entries.at[tuple(place)].set(low)
    longest = extent.index(max(extent))
    place[longest] = (place[longest] + 1) % extent[longest]
    return entries.at[tuple(place)].set(high)


def steps_of(own_key, shape, shards, smallest, high):
    def one(position, parts):
        draws = jax.random.uniform(jax.random.fold_in(jax.random.fold_in(own_key, 6), position), (parts,), jnp.float32, smallest / len(shards), high / len(shards))
        return jnp.repeat(jnp.exp(draws), shape[position] // parts).reshape((-1,) + (1,) * (len(shape) - position - 1))

    factor_of = one(*shards[0])
    for cut in shards[1:]:
        factor_of = factor_of * one(*cut)
    return factor_of


def scatter_about(key, shape, deviation, bound, split=(), kind=jnp.bfloat16):
    values = jax.random.normal(key, shape, jnp.float32) * deviation
    if len(split) > 0:
        values = steps_of(key, shape, split, -0.22, 0.18) * values
    return jnp.clip(values, min=-bound, max=bound).astype(kind)


def setup_inputs(seed: int = 0) -> dict:
    seeds = jax.random.split(jax.random.key(seed), 7)
    echoes = scatter_about(seeds[0], (NPUL, 2, NS), 1.0, 6.0, ((0, 256),))
    chirp_ref = scatter_about(seeds[1], (2, NC), (2 * NC) ** -0.5, 0.09375)
    band_starts = with_ends(jax.random.randint(seeds[2], (NBLK, N_TILE), 0, NS - BAND + 1), jax.random.fold_in(seeds[2], 1), 0, NS - BAND).astype(jnp.int32)
    doppler_rates = jnp.clip(jax.random.uniform(seeds[3], (N_SUB, P_GRP), jnp.float32, -4096.0, 4096.0) * steps_of(seeds[3], (N_SUB, P_GRP), ((0, 16),), -0.4, 0.0), -4096.0, 4096.0)
    slot_pulse = jax.vmap(lambda own: jax.random.permutation(own, PB))(jax.random.split(seeds[4], N_SUB * NB)).reshape((N_SUB, NB, PB)).astype(jnp.int32)
    interp_weights = scatter_about(seeds[5], (NBLK, 2, BAND, IMG_ROWS, COLS), (2 * BAND * PB * NB * N_SUB) ** -0.5, 0.00390625, ((0, 16), (3, 16)))
    return dict(echoes=echoes, chirp_ref=chirp_ref, band_starts=band_starts, doppler_rates=doppler_rates, slot_pulse=slot_pulse, interp_weights=interp_weights)


def compress_group(echo_group, chirp_ref):
    signal = lax.complex(echo_group[:, 0].astype(jnp.float32), echo_group[:, 1].astype(jnp.float32))
    chirp_sig = lax.complex(chirp_ref[0].astype(jnp.float32), chirp_ref[1].astype(jnp.float32))
    pulse_len = signal.shape[-1]
    fft_len = pulse_len + chirp_sig.shape[-1]
    spectrum = jnp.fft.fft(signal, n=fft_len, axis=-1)
    chirp_spec = jnp.fft.fft(chirp_sig, n=fft_len)
    result = jnp.fft.ifft(spectrum * jnp.conj(chirp_spec)[None, :], axis=-1)[:, :pulse_len]
    return jnp.stack([jnp.real(result), jnp.imag(result)], 1).astype(jnp.bfloat16)


def rounded(values):
    narrow = lax.optimization_barrier(values.astype(jnp.bfloat16))
    return narrow.astype(jnp.float32)


def reference(echoes, chirp_ref, band_starts, doppler_rates, slot_pulse, interp_weights):
    col_pos = (jnp.arange(COLS, dtype=jnp.float32) + 0.5) / COLS - 0.5
    high = lax.Precision.HIGHEST

    def one_group(group):
        echo_group = lax.dynamic_slice_in_dim(echoes, group * P_GRP, P_GRP, 0)
        compressed = compress_group(echo_group, chirp_ref)
        compressed = compressed.reshape(N_TILE, NB, P_BLK_DEV, 2, NS).transpose(1, 0, 2, 3, 4).reshape(NB, PB, 2, NS)
        image = jnp.zeros((2, N_TILE * ROWS, COLS), jnp.float32)
        for block in range(NB):
            pulse_ids = (slot_pulse[group, block] + block * PB).astype(jnp.int32)
            pulse_rate = doppler_rates[group][pulse_ids]
            angles = pulse_rate[:, None] * col_pos[None, :]
            cosine = rounded(jnp.cos(angles))
            sine = rounded(jnp.sin(angles))
            block_row = group * NB + block
            block_data = compressed[block]
            block_weights = interp_weights[block_row]

            def one_tile(tile):
                offset = band_starts[block_row, tile].astype(jnp.int32)
                band_cut = lax.dynamic_slice_in_dim(block_data, offset, BAND, 2).astype(jnp.float32)
                real_part = band_cut[:, 0].T
                imag_part = band_cut[:, 1].T
                acc_real = jnp.dot(real_part, cosine, precision=high) - jnp.dot(imag_part, sine, precision=high)
                acc_imag = jnp.dot(real_part, sine, precision=high) + jnp.dot(imag_part, cosine, precision=high)
                tile_weights = lax.dynamic_slice_in_dim(block_weights, (tile * ROWS).astype(jnp.int32), ROWS, 2).astype(jnp.float32)
                out_real = jnp.sum(tile_weights[0] * acc_real[:, None, :] - tile_weights[1] * acc_imag[:, None, :], 0)
                out_imag = jnp.sum(tile_weights[0] * acc_imag[:, None, :] + tile_weights[1] * acc_real[:, None, :], 0)
                return jnp.stack([out_real, out_imag])

            tiles = lax.map(one_tile, jnp.arange(N_TILE, dtype=jnp.int32))
            image = image + tiles.transpose(1, 0, 2, 3).reshape(2, N_TILE * ROWS, COLS)
        return image

    partials = lax.map(one_group, jnp.arange(N_SUB, dtype=jnp.int32))
    return jnp.sum(partials, 0)
```

```python
import functools

import jax
import jax.numpy as jnp
import numpy as np
from jax import lax
from jax.experimental import pallas as pl
from jax.experimental.pallas import tpu as pltpu
from jax.sharding import PartitionSpec as P

LANES = 128
VMEM_LIMIT = 40 * 1024 * 1024


def compress_kernel(starts_ref, chirp_ref, samples_ref, bands_ref, lhs_ref, toeplitz_ref, product_ref):
    span = toeplitz_ref.shape[1]
    blocks, tiles = starts_ref.shape
    rows = samples_ref.shape[1] // blocks
    half = rows // 2
    chunks = span // LANES
    chirp = chirp_ref[...].astype(jnp.float32)
    pad = jnp.zeros((1, span - chirp.shape[1]), jnp.float32)
    for part in range(2):
        line = jnp.concatenate([chirp[part : part + 1], pad], 1)
        shifted = pltpu.roll(
            jnp.broadcast_to(line, (LANES, span)), 0, 1, stride=1, stride_axis=0
        ).astype(jnp.bfloat16)
        base = part * 2 * LANES
        toeplitz_ref[base : base + LANES, :] = shifted
        toeplitz_ref[base + LANES : base + 2 * LANES, :LANES] = jnp.zeros((LANES, LANES), jnp.bfloat16)
        toeplitz_ref[base + LANES : base + 2 * LANES, LANES:] = shifted[:, : span - LANES]
    for block in range(blocks):
        for tile in range(tiles):
            first = starts_ref[block, tile] // LANES
            place = (block * tiles + tile) * rows
            for chunk in range(chunks):
                lhs_ref[place : place + rows, chunk * LANES : (chunk + 1) * LANES] = samples_ref[
                    first + chunk, block * rows : (block + 1) * rows, :
                ]
    product_ref[...] = lax.dot_general(
        lhs_ref[...], toeplitz_ref[...], (((1,), (1,)), ((), ())), preferred_element_type=jnp.float32
    )
    lane = lax.broadcasted_iota(jnp.int32, (half, LANES), 1)
    for block in range(blocks):
        for tile in range(tiles):
            place = (block * tiles + tile) * rows
            shift = starts_ref[block, tile] % LANES
            turn = (LANES - shift) % LANES
            keep = lane < LANES - shift

            def piece(part, column):
                top = place + part * half
                low = product_ref[top : top + half, column * 2 * LANES : column * 2 * LANES + LANES]
                high = product_ref[top : top + half, column * 2 * LANES + LANES : (column + 1) * 2 * LANES]
                return low, high

            rr, ri = piece(0, 0), piece(0, 1)
            ir, ii = piece(1, 0), piece(1, 1)
            for part, (low, high) in enumerate(
                ((rr[0] + ii[0], rr[1] + ii[1]), (ir[0] - ri[0], ir[1] - ri[1]))
            ):
                cut = jnp.where(keep, pltpu.roll(low, turn, 1), pltpu.roll(high, turn, 1))
                top = block * rows + part * half
                bands_ref[tile, top : top + half, :] = cut.astype(jnp.bfloat16)


def sine_cosine(angle):
    turns = jnp.round(angle * np.float32(2 / np.pi))
    rest = (angle - turns * np.float32(1.5703125)) - turns * np.float32(np.pi / 2 - 1.5703125)
    quarter = turns.astype(jnp.int32)
    sq = rest * rest
    sine = np.float32(1 / 362880) * sq + np.float32(-1 / 5040)
    sine = sine * sq + np.float32(1 / 120)
    sine = sine * sq + np.float32(-1 / 6)
    sine = sine * sq * rest + rest
    cosine = np.float32(1 / 40320) * sq + np.float32(-1 / 720)
    cosine = cosine * sq + np.float32(1 / 24)
    cosine = cosine * sq + np.float32(-1 / 2)
    cosine = cosine * sq + np.float32(1)
    odd = (quarter & 1) == 1
    sin_out = jnp.where(odd, cosine, sine)
    cos_out = jnp.where(odd, sine, cosine)
    sin_out = jnp.where((quarter & 2) == 2, -sin_out, sin_out)
    cos_out = jnp.where(((quarter + 1) & 2) == 2, -cos_out, cos_out)
    return sin_out, cos_out


def phase_kernel(rates_ref, slots_ref, table_ref):
    blocks, count = slots_ref.shape
    columns = table_ref.shape[2]
    row = lax.broadcasted_iota(jnp.int32, (count, count), 0)
    col = lax.broadcasted_iota(jnp.int32, (count, count), 1)
    lane = lax.broadcasted_iota(jnp.int32, (count, LANES), 1).astype(jnp.float32)
    place = (lane + 0.5) * np.float32(1 / columns) - 0.5
    for block in range(blocks):
        slots = slots_ref[block : block + 1, :].astype(jnp.float32)
        slot = jnp.sum(jnp.where(row == col, slots, 0.0), 1, keepdims=True)
        rates = rates_ref[:, block * count : (block + 1) * count]
        rate = jnp.sum(jnp.where(slot == col.astype(jnp.float32), rates, 0.0), 1, keepdims=True)
        rate = jnp.broadcast_to(rate, (count, LANES))
        for group in range(count // 32):
            span = slice(group * 32, group * 32 + 32)
            sine, cosine = sine_cosine(rate[span] * place[span])
            step_sine, step_cosine = sine_cosine(rate[span] * np.float32(LANES / columns))
            for chunk in range(columns // LANES):
                if chunk > 0:
                    sine, cosine = (
                        sine * step_cosine + cosine * step_sine,
                        cosine * step_cosine - sine * step_sine,
                    )
                lanes = slice(chunk * LANES, (chunk + 1) * LANES)
                table_ref[block, group * 32 : group * 32 + 32, lanes] = cosine.astype(jnp.bfloat16)
                table_ref[block, count + group * 32 : count + group * 32 + 32, lanes] = sine.astype(
                    jnp.bfloat16
                )


def image_kernel(bands_ref, table_ref, weights_ref, image_ref, focused_ref):
    blocks = table_ref.shape[0]
    sources, band_rows, band = bands_ref.shape
    rows = band_rows // blocks
    half = rows // 2
    count = sources * half
    columns = table_ref.shape[2]
    groups = columns // (4 * LANES)
    upper = lax.broadcasted_iota(jnp.int32, (8, LANES), 0) < 4
    zero = jnp.zeros((8, LANES), jnp.float32)
    image_rows = [[zero, zero, zero, zero] for _ in range(groups)]
    for block in range(blocks):
        real = bands_ref[:, block * rows : block * rows + half, :].reshape(count, band)
        imag = bands_ref[:, block * rows + half : (block + 1) * rows, :].reshape(count, band)
        top = jnp.concatenate([real, imag], 1)
        bottom = jnp.concatenate([-imag, real], 1)
        left = jnp.concatenate([top, bottom], 0)
        for group in range(groups):
            focused_ref[...] = lax.dot_general(
                left,
                table_ref[block, :, group * 4 * LANES : (group + 1) * 4 * LANES],
                (((0,), (0,)), ((), ())),
                preferred_element_type=jnp.float32,
            ).reshape(focused_ref.shape)

            def step(outer, sums):
                sums = list(sums)
                for inner in range(8):
                    k = outer * 8 + inner
                    weight_real = weights_ref[
                        block * 2 * band + k, group * 16 : group * 16 + 16, :
                    ].astype(jnp.float32)
                    weight_imag = weights_ref[
                        block * 2 * band + band + k, group * 16 : group * 16 + 16, :
                    ].astype(jnp.float32)
                    for pair in range(2):
                        wr = weight_real[pair * 8 : pair * 8 + 8]
                        wi = weight_imag[pair * 8 : pair * 8 + 8]

                        def value(row):
                            parts = [
                                jnp.broadcast_to(
                                    focused_ref[
                                        row,
                                        inner : inner + 1,
                                        (2 * pair + side) * LANES : (2 * pair + side + 1) * LANES,
                                    ],
                                    (8, LANES),
                                )
                                for side in range(2)
                            ]
                            return jnp.where(upper, parts[0], parts[1])

                        fr = value(outer)
                        fi = value(band // 8 + outer)
                        sums[2 * pair] = sums[2 * pair] + (wr * fr - wi * fi)
                        sums[2 * pair + 1] = sums[2 * pair + 1] + (wr * fi + wi * fr)
                return tuple(sums)

            image_rows[group] = list(
                lax.fori_loop(0, band // 8, step, tuple(image_rows[group]))
            )
    for group in range(groups):
        for pair in range(2):
            real, imag = image_rows[group][2 * pair], image_rows[group][2 * pair + 1]
            chunk = group * 4 + 2 * pair
            image_ref[chunk] = jnp.concatenate([real[:4], imag[:4]], 0)
            image_ref[chunk + 1] = jnp.concatenate([real[4:], imag[4:]], 0)


def vmem():
    return pl.BlockSpec(memory_space=pltpu.VMEM)


def partial_image(echoes, chirp_ref, band_starts, doppler_rates, slot_pulse, interp_weights):
    pulses, _, pulse_len = echoes.shape
    chirp_len = chirp_ref.shape[1]
    blocks, tiles = band_starts.shape
    _, _, band, image_rows, columns = interp_weights.shape
    count = slot_pulse.shape[2]
    chunks = pulse_len // LANES
    span = chirp_len + 2 * LANES
    params = pltpu.CompilerParams(vmem_limit_bytes=VMEM_LIMIT)
    half = pulses // blocks
    samples = echoes.reshape(blocks, half, 2, chunks, LANES).transpose(3, 0, 2, 1, 4)
    samples = samples.reshape(chunks, 2 * pulses, LANES)
    samples = jnp.pad(samples, ((0, span // LANES - 1), (0, 0), (0, 0)))
    bands = pl.pallas_call(
        compress_kernel,
        out_shape=jax.ShapeDtypeStruct((tiles, 2 * pulses, band), jnp.bfloat16),
        in_specs=[pl.BlockSpec(memory_space=pltpu.SMEM), vmem(), vmem()],
        out_specs=vmem(),
        scratch_shapes=[
            pltpu.VMEM((blocks * tiles * 2 * half, span), jnp.bfloat16),
            pltpu.VMEM((4 * LANES, span), jnp.bfloat16),
            pltpu.VMEM((blocks * tiles * 2 * half, 4 * LANES), jnp.float32),
        ],
        compiler_params=params,
        name="compress",
    )(band_starts, chirp_ref, samples)
    bands = lax.all_to_all(bands, "tile", 0, 0, tiled=True)
    table = pl.pallas_call(
        phase_kernel,
        out_shape=jax.ShapeDtypeStruct((blocks, 2 * count, columns), jnp.bfloat16),
        in_specs=[vmem(), vmem()],
        out_specs=vmem(),
        compiler_params=params,
        name="phase",
    )(doppler_rates, slot_pulse.reshape(blocks, count))
    weights = interp_weights.reshape(blocks, 2, band, image_rows, columns // LANES, LANES)
    weights = weights.transpose(0, 1, 2, 4, 3, 5).reshape(
        blocks * 2 * band, columns // LANES * image_rows, LANES
    )
    image = pl.pallas_call(
        image_kernel,
        out_shape=jax.ShapeDtypeStruct((columns // LANES, 2 * image_rows, LANES), jnp.float32),
        in_specs=[vmem(), vmem(), vmem()],
        out_specs=vmem(),
        scratch_shapes=[pltpu.VMEM((2 * band // 8, 8, 4 * LANES), jnp.float32)],
        compiler_params=params,
        name="image",
    )(bands, table, weights)
    return image


def shards(*args):
    image = partial_image(*args)
    pieces = lax.all_to_all(image, "sub", 0, 0, tiled=True)
    return jnp.sum(pieces, 0).reshape(2, -1, LANES)


def solution(mesh):
    in_specs = (
        P(("sub", "tile"), None, None),
        P(),
        P("sub", None),
        P("sub", None),
        P("sub", None, None),
        P("sub", None, None, "tile", None),
    )
    out_specs = P(None, "tile", "sub")
    return jax.shard_map(shards, mesh=mesh, in_specs=in_specs, out_specs=out_specs, check_vma=False)
```

```python
import functools

import jax
import jax.numpy as jnp
import numpy as np
from jax import lax
from jax.experimental import pallas as pl
from jax.experimental.pallas import tpu as pltpu
from jax.sharding import PartitionSpec as P

LANES = 128
VMEM_LIMIT = 60 * 1024 * 1024


def compress_kernel(
    starts_ref, chirp_ref, echoes_ref, bands_ref, raw_ref, wide_ref, samples_ref, lhs_ref, toeplitz_ref, product_ref, sem
):
    fetch = pltpu.make_async_copy(echoes_ref, raw_ref, sem)
    fetch.start()
    span = toeplitz_ref.shape[1]
    blocks, tiles = starts_ref.shape
    pulses, lines, _ = raw_ref.shape
    half = pulses // blocks
    rows = 2 * half
    chunks = span // LANES
    chirp = chirp_ref[...].astype(jnp.float32)
    pad = jnp.zeros((1, span - chirp.shape[1]), jnp.float32)
    for part in range(2):
        line = jnp.concatenate([chirp[part : part + 1], pad], 1)
        shifted = pltpu.roll(
            jnp.broadcast_to(line, (LANES, span)), 0, 1, stride=1, stride_axis=0
        ).astype(jnp.bfloat16)
        base = part * 2 * LANES
        toeplitz_ref[base : base + LANES, :] = shifted
        toeplitz_ref[base + LANES : base + 2 * LANES, :LANES] = jnp.zeros((LANES, LANES), jnp.bfloat16)
        toeplitz_ref[base + LANES : base + 2 * LANES, LANES:] = shifted[:, : span - LANES]
    samples_ref[lines // 2 :] = jnp.zeros(
        (samples_ref.shape[0] - lines // 2, 2 * pulses, LANES), jnp.bfloat16
    )
    fetch.wait()
    wide_ref[...] = raw_ref[...].astype(jnp.float32).reshape(wide_ref.shape)
    for chunk in range(lines // 2):
        for block in range(blocks):
            for part in range(2):
                line = wide_ref[
                    pl.ds(block * half * lines + 2 * chunk + part, half, stride=lines), :
                ]
                top = block * rows + part * half
                samples_ref[chunk, top : top + half, :] = line.astype(jnp.bfloat16)
    for block in range(blocks):
        for tile in range(tiles):
            first = starts_ref[block, tile] // LANES
            place = (block * tiles + tile) * rows
            for chunk in range(chunks):
                lhs_ref[place : place + rows, chunk * LANES : (chunk + 1) * LANES] = samples_ref[
                    first + chunk, block * rows : (block + 1) * rows, :
                ]
    product_ref[...] = lax.dot_general(
        lhs_ref[...], toeplitz_ref[...], (((1,), (1,)), ((), ())), preferred_element_type=jnp.float32
    )
    lane = lax.broadcasted_iota(jnp.int32, (half, LANES), 1)
    for block in range(blocks):
        for tile in range(tiles):
            place = (block * tiles + tile) * rows
            shift = starts_ref[block, tile] % LANES
            turn = (LANES - shift) % LANES
            keep = lane < LANES - shift

            def piece(part, column):
                top = place + part * half
                low = product_ref[top : top + half, column * 2 * LANES : column * 2 * LANES + LANES]
                high = product_ref[top : top + half, column * 2 * LANES + LANES : (column + 1) * 2 * LANES]
                return low, high

            rr, ri = piece(0, 0), piece(0, 1)
            ir, ii = piece(1, 0), piece(1, 1)
            for part, (low, high) in enumerate(
                ((rr[0] + ii[0], rr[1] + ii[1]), (ir[0] - ri[0], ir[1] - ri[1]))
            ):
                cut = jnp.where(keep, pltpu.roll(low, turn, 1), pltpu.roll(high, turn, 1))
                top = block * rows + part * half
                bands_ref[tile, top : top + half, :] = cut.astype(jnp.bfloat16)


def sine_cosine(angle):
    turns = jnp.round(angle * np.float32(2 / np.pi))
    rest = (angle - turns * np.float32(1.5703125)) - turns * np.float32(np.pi / 2 - 1.5703125)
    quarter = turns.astype(jnp.int32)
    sq = rest * rest
    sine = np.float32(1 / 362880) * sq + np.float32(-1 / 5040)
    sine = sine * sq + np.float32(1 / 120)
    sine = sine * sq + np.float32(-1 / 6)
    sine = sine * sq * rest + rest
    cosine = np.float32(1 / 40320) * sq + np.float32(-1 / 720)
    cosine = cosine * sq + np.float32(1 / 24)
    cosine = cosine * sq + np.float32(-1 / 2)
    cosine = cosine * sq + np.float32(1)
    odd = (quarter & 1) == 1
    sin_out = jnp.where(odd, cosine, sine)
    cos_out = jnp.where(odd, sine, cosine)
    sin_out = jnp.where((quarter & 2) == 2, -sin_out, sin_out)
    cos_out = jnp.where(((quarter + 1) & 2) == 2, -cos_out, cos_out)
    return sin_out, cos_out


def phase_kernel(rates_ref, slots_ref, table_ref):
    count = slots_ref.shape[1]
    columns = table_ref.shape[2]
    block = pl.program_id(0)
    row = lax.broadcasted_iota(jnp.int32, (count, count), 0)
    col = lax.broadcasted_iota(jnp.int32, (count, count), 1)
    lane = lax.broadcasted_iota(jnp.int32, (count, LANES), 1).astype(jnp.float32)
    place = (lane + 0.5) * np.float32(1 / columns) - 0.5
    which = lax.broadcasted_iota(jnp.int32, slots_ref.shape, 0) == block
    slots = jnp.sum(jnp.where(which, slots_ref[...], 0), 0, keepdims=True).astype(jnp.float32)
    slot = jnp.sum(jnp.where(row == col, slots, 0.0), 1, keepdims=True)
    rates = rates_ref[...]
    rate = jnp.sum(jnp.where(slot == col.astype(jnp.float32), rates, 0.0), 1, keepdims=True)
    rate = jnp.broadcast_to(rate, (count, LANES))
    for group in range(count // 32):
        span = slice(group * 32, group * 32 + 32)
        sine, cosine = sine_cosine(rate[span] * place[span])
        step_sine, step_cosine = sine_cosine(rate[span] * np.float32(LANES / columns))
        for chunk in range(columns // LANES):
            if chunk > 0:
                sine, cosine = (
                    sine * step_cosine + cosine * step_sine,
                    cosine * step_cosine - sine * step_sine,
                )
            lanes = slice(chunk * LANES, (chunk + 1) * LANES)
            table_ref[0, group * 32 : group * 32 + 32, lanes] = cosine.astype(jnp.bfloat16)
            table_ref[0, count + group * 32 : count + group * 32 + 32, lanes] = sine.astype(
                jnp.bfloat16
            )


def image_kernel(me_ref, bands_ref, table_ref, weights_ref, *rest):
    *piece_refs, left_ref, focused_ref, image_ref = rest
    step_id = pl.program_id(0)
    blocks = table_ref.shape[0]
    sources, band_rows, band = bands_ref.shape
    rows = band_rows // blocks
    half = rows // 2
    count = sources * half

    @pl.when(step_id == 0)
    def _():
        for block in range(blocks):
            real = bands_ref[:, block * rows : block * rows + half, :].reshape(count, band)
            imag = bands_ref[:, block * rows + half : (block + 1) * rows, :].reshape(count, band)
            top = jnp.concatenate([real, imag], 1)
            bottom = jnp.concatenate([-imag, real], 1)
            left_ref[block] = jnp.concatenate([top, bottom], 0).T

    for block in range(blocks):
        focused_ref[block] = jnp.dot(
            left_ref[block], table_ref[block], preferred_element_type=jnp.float32
        ).reshape(focused_ref.shape[1:])
    upper = lax.broadcasted_iota(jnp.int32, (8, LANES), 0) < 4
    zero = jnp.zeros((8, LANES), jnp.float32)
    sums = (zero, zero)
    for block in range(blocks):

        def step(outer, sums):
            real, imag = sums
            for inner in range(8):
                k = outer * 8 + inner
                wr = weights_ref[block * 2 * band + k].astype(jnp.float32)
                wi = weights_ref[block * 2 * band + band + k].astype(jnp.float32)

                def value(row):
                    parts = [
                        jnp.broadcast_to(
                            focused_ref[
                                block, row, inner : inner + 1, side * LANES : (side + 1) * LANES
                            ],
                            (8, LANES),
                        )
                        for side in range(2)
                    ]
                    return jnp.where(upper, parts[0], parts[1])

                fr = value(outer)
                fi = value(band // 8 + outer)
                real = real + (wr * fr - wi * fi)
                imag = imag + (wr * fi + wi * fr)
            return real, imag

        sums = lax.fori_loop(0, band // 8, step, sums)
    real, imag = sums
    image_ref[2 * step_id] = jnp.concatenate([real[:4], imag[:4]], 0)
    image_ref[2 * step_id + 1] = jnp.concatenate([real[4:], imag[4:]], 0)

    @pl.when(step_id == pl.num_programs(0) - 1)
    def _():
        for index, piece_ref in enumerate(piece_refs):
            piece_ref[...] = image_ref[me_ref[0] ^ index]


def vmem():
    return pl.BlockSpec(memory_space=pltpu.VMEM)


def partial_image(echoes, chirp_ref, band_starts, doppler_rates, slot_pulse, interp_weights):
    pulses, _, pulse_len = echoes.shape
    chirp_len = chirp_ref.shape[1]
    blocks, tiles = band_starts.shape
    _, _, band, image_rows, columns = interp_weights.shape
    count = slot_pulse.shape[2]
    lines = 2 * pulse_len // LANES
    span = chirp_len + 2 * LANES
    places = columns // LANES
    params = pltpu.CompilerParams(vmem_limit_bytes=VMEM_LIMIT)
    samples = echoes.reshape(pulses, 2, pulse_len // LANES, LANES).transpose(0, 2, 1, 3)
    samples = samples.reshape(pulses, lines, LANES)
    bands = pl.pallas_call(
        compress_kernel,
        out_shape=jax.ShapeDtypeStruct((tiles, 2 * pulses, band), jnp.bfloat16),
        in_specs=[
            pl.BlockSpec(memory_space=pltpu.SMEM),
            vmem(),
            pl.BlockSpec(memory_space=pl.ANY),
        ],
        out_specs=vmem(),
        scratch_shapes=[
            pltpu.VMEM((pulses, lines, LANES), jnp.bfloat16),
            pltpu.VMEM((pulses * lines, LANES), jnp.float32),
            pltpu.VMEM((lines // 2 + span // LANES - 1, 2 * pulses, LANES), jnp.bfloat16),
            pltpu.VMEM((tiles * 2 * pulses, span), jnp.bfloat16),
            pltpu.VMEM((4 * LANES, span), jnp.bfloat16),
            pltpu.VMEM((tiles * 2 * pulses, 4 * LANES), jnp.float32),
            pltpu.SemaphoreType.DMA,
        ],
        compiler_params=params,
        name="compress",
    )(band_starts, chirp_ref, samples)
    bands = lax.all_to_all(bands, "tile", 0, 0, tiled=True)
    table = pl.pallas_call(
        phase_kernel,
        grid=(blocks,),
        out_shape=jax.ShapeDtypeStruct((blocks, 2 * count, columns), jnp.bfloat16),
        in_specs=[
            pl.BlockSpec((1, count), lambda i: (0, i)),
            pl.BlockSpec((blocks, count), lambda i: (0, 0)),
        ],
        out_specs=pl.BlockSpec((1, 2 * count, columns), lambda i: (i, 0, 0)),
        compiler_params=params,
        name="phase",
    )(doppler_rates, slot_pulse.reshape(blocks, count))
    weights = interp_weights.reshape(blocks, 2, band, image_rows, places, LANES)
    weights = weights.transpose(0, 1, 2, 4, 3, 5).reshape(
        blocks * 2 * band, places * image_rows, LANES
    )
    me = lax.axis_index("sub").astype(jnp.int32).reshape(1)
    return pl.pallas_call(
        image_kernel,
        grid=(places // 2,),
        out_shape=[jax.ShapeDtypeStruct((2 * image_rows, LANES), jnp.float32)] * places,
        in_specs=[
            pl.BlockSpec(memory_space=pltpu.SMEM),
            pl.BlockSpec((tiles, 2 * pulses, band), lambda i: (0, 0, 0)),
            pl.BlockSpec((blocks, 2 * count, 2 * LANES), lambda i: (0, 0, i)),
            pl.BlockSpec((blocks * 2 * band, 2 * image_rows, LANES), lambda i: (0, i, 0)),
        ],
        out_specs=[pl.BlockSpec((2 * image_rows, LANES), lambda i: (0, 0))] * places,
        scratch_shapes=[
            pltpu.VMEM((blocks, 2 * band, 2 * count), jnp.bfloat16),
            pltpu.VMEM((blocks, 2 * band // 8, 8, 2 * LANES), jnp.float32),
            pltpu.VMEM((places, 2 * image_rows, LANES), jnp.float32),
        ],
        compiler_params=params,
        name="image",
    )(me, bands, table, weights)


def shards(*args):
    pieces = partial_image(*args)
    size = len(pieces)
    total = pieces[0]
    for index in range(1, size):
        pairs = [(source, source ^ index) for source in range(size)]
        total = total + lax.ppermute(pieces[index], "sub", pairs)
    return total.reshape(2, -1, LANES)


def solution(mesh):
    in_specs = (
        P(("sub", "tile"), None, None),
        P(),
        P("sub", None),
        P("sub", None),
        P("sub", None, None),
        P("sub", None, None, "tile", None),
    )
    out_specs = P(None, "tile", "sub")
    return jax.shard_map(shards, mesh=mesh, in_specs=in_specs, out_specs=out_specs, check_vma=False)
```

```python
import functools

import jax
import jax.numpy as jnp
import numpy as np
from jax import lax
from jax.experimental import pallas as pl
from jax.experimental.pallas import tpu as pltpu
from jax.sharding import PartitionSpec as P

LANES = 128
VMEM_LIMIT = 60 * 1024 * 1024


def compress_kernel(
    starts_ref, chirp_ref, echoes_ref, bands_ref, raw_ref, samples_ref, lhs_ref, toeplitz_ref, product_ref, sem
):
    fetch = pltpu.make_async_copy(echoes_ref, raw_ref, sem)
    fetch.start()
    span = toeplitz_ref.shape[1]
    blocks, tiles = starts_ref.shape
    pulses, lines, _ = raw_ref.shape
    half = pulses // blocks
    rows = 2 * half
    chunks = span // LANES
    chirp = chirp_ref[...].astype(jnp.float32)
    pad = jnp.zeros((1, span - chirp.shape[1]), jnp.float32)
    for part in range(2):
        line = jnp.concatenate([chirp[part : part + 1], pad], 1)
        shifted = pltpu.roll(
            jnp.broadcast_to(line, (LANES, span)), 0, 1, stride=1, stride_axis=0
        ).astype(jnp.bfloat16)
        base = part * 2 * LANES
        toeplitz_ref[base : base + LANES, :] = shifted
        toeplitz_ref[base + LANES : base + 2 * LANES, :LANES] = jnp.zeros((LANES, LANES), jnp.bfloat16)
        toeplitz_ref[base + LANES : base + 2 * LANES, LANES:] = shifted[:, : span - LANES]
    samples_ref[lines // 2 :] = jnp.zeros(
        (samples_ref.shape[0] - lines // 2, 2 * pulses, LANES), jnp.bfloat16
    )
    piece = 16
    side = half * piece
    row = lax.broadcasted_iota(jnp.int32, (side, side), 0)
    col = lax.broadcasted_iota(jnp.int32, (side, side), 1)
    order = jnp.where(col == (row % half) * piece + row // half, 1.0, 0.0).astype(jnp.bfloat16)
    fetch.wait()
    for group in range(lines // piece):
        block_rows = jnp.concatenate(
            [
                raw_ref[block * half : (block + 1) * half, group * piece : (group + 1) * piece, :].reshape(
                    side, LANES
                )
                for block in range(blocks)
            ],
            1,
        )
        moved = jnp.dot(order, block_rows, preferred_element_type=jnp.float32).astype(jnp.bfloat16)
        for block in range(blocks):
            samples_ref[
                group * piece // 2 : (group + 1) * piece // 2, block * rows : (block + 1) * rows, :
            ] = moved[:, block * LANES : (block + 1) * LANES].reshape(piece // 2, rows, LANES)
    for block in range(blocks):
        for tile in range(tiles):
            first = starts_ref[block, tile] // LANES
            place = (block * tiles + tile) * rows
            for chunk in range(chunks):
                lhs_ref[place : place + rows, chunk * LANES : (chunk + 1) * LANES] = samples_ref[
                    first + chunk, block * rows : (block + 1) * rows, :
                ]
    product_ref[...] = lax.dot_general(
        lhs_ref[...], toeplitz_ref[...], (((1,), (1,)), ((), ())), preferred_element_type=jnp.float32
    )
    lane = lax.broadcasted_iota(jnp.int32, (half, LANES), 1)
    for block in range(blocks):
        for tile in range(tiles):
            place = (block * tiles + tile) * rows
            shift = starts_ref[block, tile] % LANES
            turn = (LANES - shift) % LANES
            keep = lane < LANES - shift

            def piece(part, column):
                top = place + part * half
                low = product_ref[top : top + half, column * 2 * LANES : column * 2 * LANES + LANES]
                high = product_ref[top : top + half, column * 2 * LANES + LANES : (column + 1) * 2 * LANES]
                return low, high

            rr, ri = piece(0, 0), piece(0, 1)
            ir, ii = piece(1, 0), piece(1, 1)
            for part, (low, high) in enumerate(
                ((rr[0] + ii[0], rr[1] + ii[1]), (ir[0] - ri[0], ir[1] - ri[1]))
            ):
                cut = jnp.where(keep, pltpu.roll(low, turn, 1), pltpu.roll(high, turn, 1))
                top = block * rows + part * half
                bands_ref[tile, top : top + half, :] = cut.astype(jnp.bfloat16)


def sine_cosine(angle):
    turns = jnp.round(angle * np.float32(2 / np.pi))
    rest = (angle - turns * np.float32(1.5703125)) - turns * np.float32(np.pi / 2 - 1.5703125)
    quarter = turns.astype(jnp.int32)
    sq = rest * rest
    sine = np.float32(1 / 362880) * sq + np.float32(-1 / 5040)
    sine = sine * sq + np.float32(1 / 120)
    sine = sine * sq + np.float32(-1 / 6)
    sine = sine * sq * rest + rest
    cosine = np.float32(1 / 40320) * sq + np.float32(-1 / 720)
    cosine = cosine * sq + np.float32(1 / 24)
    cosine = cosine * sq + np.float32(-1 / 2)
    cosine = cosine * sq + np.float32(1)
    odd = (quarter & 1) == 1
    sin_out = jnp.where(odd, cosine, sine)
    cos_out = jnp.where(odd, sine, cosine)
    sin_out = jnp.where((quarter & 2) == 2, -sin_out, sin_out)
    cos_out = jnp.where(((quarter + 1) & 2) == 2, -cos_out, cos_out)
    return sin_out, cos_out


def phase_kernel(rates_ref, slots_ref, table_ref):
    count = slots_ref.shape[1]
    columns = table_ref.shape[1] * table_ref.shape[3]
    block = pl.program_id(0)
    row = lax.broadcasted_iota(jnp.int32, (count, count), 0)
    col = lax.broadcasted_iota(jnp.int32, (count, count), 1)
    lane = lax.broadcasted_iota(jnp.int32, (count, LANES), 1).astype(jnp.float32)
    place = (lane + 0.5) * np.float32(1 / columns) - 0.5
    which = lax.broadcasted_iota(jnp.int32, slots_ref.shape, 0) == block
    slots = jnp.sum(jnp.where(which, slots_ref[...], 0), 0, keepdims=True).astype(jnp.float32)
    slot = jnp.sum(jnp.where(row == col, slots, 0.0), 1, keepdims=True)
    rates = rates_ref[...]
    rate = jnp.sum(jnp.where(slot == col.astype(jnp.float32), rates, 0.0), 1, keepdims=True)
    rate = jnp.broadcast_to(rate, (count, LANES))
    for group in range(count // 32):
        span = slice(group * 32, group * 32 + 32)
        sine, cosine = sine_cosine(rate[span] * place[span])
        step_sine, step_cosine = sine_cosine(rate[span] * np.float32(LANES / columns))
        for chunk in range(columns // LANES):
            if chunk > 0:
                sine, cosine = (
                    sine * step_cosine + cosine * step_sine,
                    cosine * step_cosine - sine * step_sine,
                )
            lanes = slice(chunk % 2 * LANES, (chunk % 2 + 1) * LANES)
            table_ref[0, chunk // 2, span, lanes] = cosine.astype(jnp.bfloat16)
            table_ref[0, chunk // 2, count + group * 32 : count + group * 32 + 32, lanes] = (
                sine.astype(jnp.bfloat16)
            )


def image_kernel(
    bands_ref, table_ref, weights_ref, image_ref, left_ref, near_table_ref, near_weights_ref, focused_ref, table_sem, weights_sem
):
    blocks, parts, _, width = table_ref.shape
    sources, band_rows, band = bands_ref.shape
    rows = band_rows // blocks
    half = rows // 2
    count = sources * half
    places = image_ref.shape[0]
    depth = band // parts

    def table_copy(block, part):
        return pltpu.make_async_copy(
            table_ref.at[block, part], near_table_ref.at[block, part], table_sem.at[block, part]
        )

    def weights_copy(block, part, side):
        span = pl.ds((block * 2 + side) * band + part * depth, depth)
        return pltpu.make_async_copy(
            weights_ref.at[span], near_weights_ref.at[span], weights_sem.at[block, part, side]
        )

    for block in range(blocks):
        for part in range(parts):
            table_copy(block, part).start()
        for part in range(parts):
            for side in range(2):
                weights_copy(block, part, side).start()

    for block in range(blocks):
        real = bands_ref[:, block * rows : block * rows + half, :].reshape(count, band)
        imag = bands_ref[:, block * rows + half : (block + 1) * rows, :].reshape(count, band)
        top = jnp.concatenate([real, imag], 1)
        bottom = jnp.concatenate([-imag, real], 1)
        left_ref[block] = jnp.concatenate([top, bottom], 0).T

    def focus(block, part):
        table_copy(block, part).wait()
        focused_ref[block, part] = jnp.dot(
            left_ref[block], near_table_ref[block, part], preferred_element_type=jnp.float32
        ).reshape(focused_ref.shape[2:])

    for part in range(parts):
        focus(0, part)

    upper = lax.broadcasted_iota(jnp.int32, (8, LANES), 0) < 4
    sums = tuple(jnp.zeros((8, LANES), jnp.float32) for _ in range(places))
    for block in range(blocks):

        def step(part, sums):
            sums = list(sums)
            for side in range(2):
                weights_copy(block, part, side).wait()
            if block + 1 < blocks:
                focus(block + 1, part)
            for inner in range(depth):
                k = part * depth + inner
                for pair in range(places // 4):
                    span = slice(pair * 16, pair * 16 + 16)
                    weight_real = near_weights_ref[block * 2 * band + k, span, :].astype(jnp.float32)
                    weight_imag = near_weights_ref[
                        (block * 2 + 1) * band + k, span, :
                    ].astype(jnp.float32)
                    for one in range(2):
                        wr = weight_real[one * 8 : one * 8 + 8]
                        wi = weight_imag[one * 8 : one * 8 + 8]

                        def value(side):
                            line = side * (band // 8) + part * (depth // 8) + inner // 8
                            halves = [
                                jnp.broadcast_to(
                                    focused_ref[
                                        block,
                                        2 * pair + one,
                                        line,
                                        inner % 8 : inner % 8 + 1,
                                        place * LANES : (place + 1) * LANES,
                                    ],
                                    (8, LANES),
                                )
                                for place in range(2)
                            ]
                            return jnp.where(upper, halves[0], halves[1])

                        fr = value(0)
                        fi = value(1)
                        at = 2 * (2 * pair + one)
                        sums[at] = sums[at] + (wr * fr - wi * fi)
                        sums[at + 1] = sums[at + 1] + (wr * fi + wi * fr)
            return tuple(sums)

        sums = lax.fori_loop(0, parts, step, sums)
    for pair in range(places // 2):
        real, imag = sums[2 * pair], sums[2 * pair + 1]
        image_ref[2 * pair] = jnp.concatenate([real[:4], imag[:4]], 0)
        image_ref[2 * pair + 1] = jnp.concatenate([real[4:], imag[4:]], 0)


def vmem():
    return pl.BlockSpec(memory_space=pltpu.VMEM)


def partial_image(echoes, chirp_ref, band_starts, doppler_rates, slot_pulse, interp_weights):
    pulses, _, pulse_len = echoes.shape
    chirp_len = chirp_ref.shape[1]
    blocks, tiles = band_starts.shape
    _, _, band, image_rows, columns = interp_weights.shape
    count = slot_pulse.shape[2]
    lines = 2 * pulse_len // LANES
    span = chirp_len + 2 * LANES
    places = columns // LANES
    parts = places // 2
    params = pltpu.CompilerParams(vmem_limit_bytes=VMEM_LIMIT)
    samples = echoes.reshape(pulses, 2, pulse_len // LANES, LANES).transpose(0, 2, 1, 3)
    samples = samples.reshape(pulses, lines, LANES)
    bands = pl.pallas_call(
        compress_kernel,
        out_shape=jax.ShapeDtypeStruct((tiles, 2 * pulses, band), jnp.bfloat16),
        in_specs=[
            pl.BlockSpec(memory_space=pltpu.SMEM),
            vmem(),
            pl.BlockSpec(memory_space=pl.ANY),
        ],
        out_specs=vmem(),
        scratch_shapes=[
            pltpu.VMEM((pulses, lines, LANES), jnp.bfloat16),
            pltpu.VMEM((lines // 2 + span // LANES - 1, 2 * pulses, LANES), jnp.bfloat16),
            pltpu.VMEM((tiles * 2 * pulses, span), jnp.bfloat16),
            pltpu.VMEM((4 * LANES, span), jnp.bfloat16),
            pltpu.VMEM((tiles * 2 * pulses, 4 * LANES), jnp.float32),
            pltpu.SemaphoreType.DMA,
        ],
        compiler_params=params,
        name="compress",
    )(band_starts, chirp_ref, samples)
    bands = lax.all_to_all(bands, "tile", 0, 0, tiled=True)
    table = pl.pallas_call(
        phase_kernel,
        grid=(blocks,),
        out_shape=jax.ShapeDtypeStruct((blocks, parts, 2 * count, 2 * LANES), jnp.bfloat16),
        in_specs=[
            pl.BlockSpec((1, count), lambda i: (0, i)),
            pl.BlockSpec((blocks, count), lambda i: (0, 0)),
        ],
        out_specs=pl.BlockSpec((1, parts, 2 * count, 2 * LANES), lambda i: (i, 0, 0, 0)),
        compiler_params=params,
        name="phase",
    )(doppler_rates, slot_pulse.reshape(blocks, count))
    weights = interp_weights.reshape(blocks, 2, band, image_rows, places, LANES)
    weights = weights.transpose(0, 1, 2, 4, 3, 5).reshape(
        blocks * 2 * band, places * image_rows, LANES
    )
    return pl.pallas_call(
        image_kernel,
        out_shape=jax.ShapeDtypeStruct((places, 2 * image_rows, LANES), jnp.float32),
        in_specs=[
            vmem(),
            pl.BlockSpec(memory_space=pl.ANY),
            pl.BlockSpec(memory_space=pl.ANY),
        ],
        out_specs=vmem(),
        scratch_shapes=[
            pltpu.VMEM((blocks, 2 * band, 2 * count), jnp.bfloat16),
            pltpu.VMEM((blocks, parts, 2 * count, 2 * LANES), jnp.bfloat16),
            pltpu.VMEM((blocks * 2 * band, places * image_rows, LANES), jnp.bfloat16),
            pltpu.VMEM((blocks, parts, 2 * band // 8, 8, 2 * LANES), jnp.float32),
            pltpu.SemaphoreType.DMA((blocks, parts)),
            pltpu.SemaphoreType.DMA((blocks, parts, 2)),
        ],
        compiler_params=params,
        name="image",
    )(bands, table, weights)


def shards(*args):
    image = partial_image(*args)
    pieces = lax.all_to_all(image, "sub", 0, 0, tiled=True)
    return jnp.sum(pieces, 0).reshape(2, -1, LANES)


def solution(mesh):
    in_specs = (
        P(("sub", "tile"), None, None),
        P(),
        P("sub", None),
        P("sub", None),
        P("sub", None, None),
        P("sub", None, None, "tile", None),
    )
    out_specs = P(None, "tile", "sub")
    return jax.shard_map(shards, mesh=mesh, in_specs=in_specs, out_specs=out_specs, check_vma=False)
```

```python
import functools

import jax
import jax.numpy as jnp
import numpy as np
from jax import lax
from jax.experimental import pallas as pl
from jax.experimental.pallas import tpu as pltpu
from jax.sharding import PartitionSpec as P

LANES = 128


def compress_kernel(
    me_ref, starts_ref, chirp_ref, echoes_ref, *rest
):
    *bands_refs, raw_ref, samples_ref, lhs_ref, toeplitz_ref, product_ref, sem = rest
    fetch = pltpu.make_async_copy(echoes_ref, raw_ref, sem)
    fetch.start()
    span = toeplitz_ref.shape[1]
    blocks, tiles = starts_ref.shape
    near = tiles // len(bands_refs)
    pulses, lines, _ = raw_ref.shape
    half = pulses // blocks
    rows = 2 * half
    chunks = span // LANES
    chirp = chirp_ref[...].astype(jnp.float32)
    pad = jnp.zeros((1, span - chirp.shape[1]), jnp.float32)
    for part in range(2):
        line = jnp.concatenate([chirp[part : part + 1], pad], 1)
        shifted = pltpu.roll(
            jnp.broadcast_to(line, (LANES, span)), 0, 1, stride=1, stride_axis=0
        ).astype(jnp.bfloat16)
        base = part * 2 * LANES
        toeplitz_ref[base : base + LANES, :] = shifted
        toeplitz_ref[base + LANES : base + 2 * LANES, :LANES] = jnp.zeros((LANES, LANES), jnp.bfloat16)
        toeplitz_ref[base + LANES : base + 2 * LANES, LANES:] = shifted[:, : span - LANES]
    samples_ref[lines // 2 :] = jnp.zeros(
        (samples_ref.shape[0] - lines // 2, 2 * pulses, LANES), jnp.bfloat16
    )
    piece = 16
    side = half * piece
    row = lax.broadcasted_iota(jnp.int32, (side, side), 0)
    col = lax.broadcasted_iota(jnp.int32, (side, side), 1)
    order = jnp.where(col == (row % half) * piece + row // half, 1.0, 0.0).astype(jnp.bfloat16)
    fetch.wait()
    for group in range(lines // piece):
        block_rows = jnp.concatenate(
            [
                raw_ref[block * half : (block + 1) * half, group * piece : (group + 1) * piece, :].reshape(
                    side, LANES
                )
                for block in range(blocks)
            ],
            1,
        )
        moved = jnp.dot(order, block_rows, preferred_element_type=jnp.float32).astype(jnp.bfloat16)
        for block in range(blocks):
            samples_ref[
                group * piece // 2 : (group + 1) * piece // 2, block * rows : (block + 1) * rows, :
            ] = moved[:, block * LANES : (block + 1) * LANES].reshape(piece // 2, rows, LANES)
    for block in range(blocks):
        for tile in range(tiles):
            first = starts_ref[block, me_ref[0] ^ tile] // LANES
            place = (block * tiles + tile) * rows
            for chunk in range(chunks):
                lhs_ref[place : place + rows, chunk * LANES : (chunk + 1) * LANES] = samples_ref[
                    first + chunk, block * rows : (block + 1) * rows, :
                ]
    product_ref[...] = lax.dot_general(
        lhs_ref[...], toeplitz_ref[...], (((1,), (1,)), ((), ())), preferred_element_type=jnp.float32
    )
    lane = lax.broadcasted_iota(jnp.int32, (half, LANES), 1)
    for block in range(blocks):
        for tile in range(tiles):
            place = (block * tiles + tile) * rows
            shift = starts_ref[block, me_ref[0] ^ tile] % LANES
            turn = (LANES - shift) % LANES
            keep = lane < LANES - shift

            def piece(part, column):
                top = place + part * half
                low = product_ref[top : top + half, column * 2 * LANES : column * 2 * LANES + LANES]
                high = product_ref[top : top + half, column * 2 * LANES + LANES : (column + 1) * 2 * LANES]
                return low, high

            rr, ri = piece(0, 0), piece(0, 1)
            ir, ii = piece(1, 0), piece(1, 1)
            for part, (low, high) in enumerate(
                ((rr[0] + ii[0], rr[1] + ii[1]), (ir[0] - ri[0], ir[1] - ri[1]))
            ):
                cut = jnp.where(keep, pltpu.roll(low, turn, 1), pltpu.roll(high, turn, 1))
                top = block * rows + part * half
                bands_refs[tile // near][tile % near, top : top + half, :] = cut.astype(jnp.bfloat16)


def sine_cosine(angle):
    turns = jnp.round(angle * np.float32(2 / np.pi))
    rest = (angle - turns * np.float32(1.5703125)) - turns * np.float32(np.pi / 2 - 1.5703125)
    quarter = turns.astype(jnp.int32)
    sq = rest * rest
    sine = np.float32(1 / 362880) * sq + np.float32(-1 / 5040)
    sine = sine * sq + np.float32(1 / 120)
    sine = sine * sq + np.float32(-1 / 6)
    sine = sine * sq * rest + rest
    cosine = np.float32(1 / 40320) * sq + np.float32(-1 / 720)
    cosine = cosine * sq + np.float32(1 / 24)
    cosine = cosine * sq + np.float32(-1 / 2)
    cosine = cosine * sq + np.float32(1)
    odd = (quarter & 1) == 1
    sin_out = jnp.where(odd, cosine, sine)
    cos_out = jnp.where(odd, sine, cosine)
    sin_out = jnp.where((quarter & 2) == 2, -sin_out, sin_out)
    cos_out = jnp.where(((quarter + 1) & 2) == 2, -cos_out, cos_out)
    return sin_out, cos_out


def phase_kernel(rates_ref, slots_ref, table_ref):
    blocks, count = slots_ref.shape
    columns = table_ref.shape[1] * table_ref.shape[3]
    row = lax.broadcasted_iota(jnp.int32, (count, count), 0)
    col = lax.broadcasted_iota(jnp.int32, (count, count), 1)
    lane = lax.broadcasted_iota(jnp.int32, (count, LANES), 1).astype(jnp.float32)
    place = (lane + 0.5) * np.float32(1 / columns) - 0.5
    for block in range(blocks):
        slots = slots_ref[block : block + 1, :].astype(jnp.float32)
        slot = jnp.sum(jnp.where(row == col, slots, 0.0), 1, keepdims=True)
        rates = rates_ref[:, block * count : (block + 1) * count]
        rate = jnp.sum(jnp.where(slot == col.astype(jnp.float32), rates, 0.0), 1, keepdims=True)
        rate = jnp.broadcast_to(rate, (count, LANES))
        for group in range(count // 32):
            span = slice(group * 32, group * 32 + 32)
            sine, cosine = sine_cosine(rate[span] * place[span])
            step_sine, step_cosine = sine_cosine(rate[span] * np.float32(LANES / columns))
            for chunk in range(columns // LANES):
                if chunk > 0:
                    sine, cosine = (
                        sine * step_cosine + cosine * step_sine,
                        cosine * step_cosine - sine * step_sine,
                    )
                lanes = slice(chunk % 2 * LANES, (chunk % 2 + 1) * LANES)
                table_ref[block, chunk // 2, span, lanes] = cosine.astype(jnp.bfloat16)
                table_ref[block, chunk // 2, count + group * 32 : count + group * 32 + 32, lanes] = (
                    sine.astype(jnp.bfloat16)
                )


def relay_kernel(*refs):
    near = refs[0].shape[0]
    far = len(refs) - near + 1
    for dz in range(1, near):
        for dy in range(far):
            refs[far + dz - 1][dy] = refs[dy][dz]


def image_kernel(me_ref, table_ref, weights_ref, *rest):
    *sources_refs, image_ref, bands_ref, left_ref, near_weights_ref, first_ref, second_ref, sem = rest
    blocks, parts, _, width = table_ref.shape
    sources, band_rows, band = bands_ref.shape
    far_count = len(sources_refs) // 2 + 1
    near_refs, far_refs = sources_refs[:far_count], sources_refs[far_count:]
    near = sources // far_count
    rows = band_rows // blocks
    half = rows // 2
    count = sources * half
    places = image_ref.shape[0]
    depth = band // parts
    focused_refs = (first_ref, second_ref)
    ahead = 4

    def weights_copy(step, side):
        span = pl.ds((step // parts * 2 + side) * band + step % parts * depth, depth)
        return pltpu.make_async_copy(
            weights_ref.at[span], near_weights_ref.at[span], sem.at[step, side]
        )

    for step in range(ahead):
        for side in range(2):
            weights_copy(step, side).start()
    for dy in range(far_count):
        bands_ref[me_ref[0] ^ (dy * near)] = near_refs[dy][0]
        for dz in range(1, near):
            bands_ref[me_ref[0] ^ (dy * near + dz)] = far_refs[dz - 1][dy]

    for block in range(blocks):
        real = bands_ref[:, block * rows : block * rows + half, :].reshape(count, band)
        imag = bands_ref[:, block * rows + half : (block + 1) * rows, :].reshape(count, band)
        top = jnp.concatenate([real, imag], 1)
        bottom = jnp.concatenate([-imag, real], 1)
        left_ref[block] = jnp.concatenate([top, bottom], 0).T

    def focus(block, part):
        target_ref = focused_refs[block]
        target_ref[part] = jnp.dot(
            left_ref[block], table_ref[block, part], preferred_element_type=jnp.float32
        ).reshape(target_ref.shape[1:])

    for part in range(parts):
        focus(0, part)

    upper = lax.broadcasted_iota(jnp.int32, (8, LANES), 0) < 4
    sums = tuple(jnp.zeros((8, LANES), jnp.float32) for _ in range(places))
    for block in range(blocks):
        focused_ref = focused_refs[block]

        def step(part, sums):
            sums = list(sums)
            for side in range(2):
                weights_copy(block * parts + part, side).wait()

            @pl.when(block * parts + part + ahead < blocks * parts)
            def _():
                for side in range(2):
                    weights_copy(block * parts + part + ahead, side).start()

            if block + 1 < blocks:
                focus(block + 1, part)
            for inner in range(depth):
                k = part * depth + inner
                for pair in range(places // 4):
                    span = slice(pair * 16, pair * 16 + 16)
                    weight_real = near_weights_ref[block * 2 * band + k, span, :].astype(jnp.float32)
                    weight_imag = near_weights_ref[
                        (block * 2 + 1) * band + k, span, :
                    ].astype(jnp.float32)
                    for one in range(2):
                        wr = weight_real[one * 8 : one * 8 + 8]
                        wi = weight_imag[one * 8 : one * 8 + 8]

                        def value(side):
                            line = side * (band // 8) + part * (depth // 8) + inner // 8
                            halves = [
                                jnp.broadcast_to(
                                    focused_ref[
                                        2 * pair + one,
                                        line,
                                        inner % 8 : inner % 8 + 1,
                                        place * LANES : (place + 1) * LANES,
                                    ],
                                    (8, LANES),
                                )
                                for place in range(2)
                            ]
                            return jnp.where(upper, halves[0], halves[1])

                        fr = value(0)
                        fi = value(1)
                        at = 2 * (2 * pair + one)
                        sums[at] = sums[at] + (wr * fr - wi * fi)
                        sums[at + 1] = sums[at + 1] + (wr * fi + wi * fr)
            return tuple(sums)

        sums = lax.fori_loop(0, parts, step, sums)
    for pair in range(places // 2):
        real, imag = sums[2 * pair], sums[2 * pair + 1]
        image_ref[2 * pair] = jnp.concatenate([real[:4], imag[:4]], 0)
        image_ref[2 * pair + 1] = jnp.concatenate([real[4:], imag[4:]], 0)


def params(mib):
    return pltpu.CompilerParams(vmem_limit_bytes=mib * 1024 * 1024)


def vmem():
    return pl.BlockSpec(memory_space=pltpu.VMEM)


def partial_image(echoes, chirp_ref, band_starts, doppler_rates, slot_pulse, interp_weights):
    pulses, _, pulse_len = echoes.shape
    chirp_len = chirp_ref.shape[1]
    blocks, tiles = band_starts.shape
    _, _, band, image_rows, columns = interp_weights.shape
    count = slot_pulse.shape[2]
    lines = 2 * pulse_len // LANES
    span = chirp_len + 2 * LANES
    places = columns // LANES
    parts = places // 2
    samples = echoes.reshape(pulses, 2, pulse_len // LANES, LANES).transpose(0, 2, 1, 3)
    samples = samples.reshape(pulses, lines, LANES)
    smem = pl.BlockSpec(memory_space=pltpu.SMEM)
    me = lax.axis_index("tile").astype(jnp.int32).reshape(1)
    near = 4
    far = tiles // near
    bands = pl.pallas_call(
        compress_kernel,
        out_shape=[jax.ShapeDtypeStruct((near, 2 * pulses, band), jnp.bfloat16)] * far,
        in_specs=[
            smem,
            smem,
            vmem(),
            pl.BlockSpec(memory_space=pl.ANY),
        ],
        out_specs=[vmem()] * far,
        scratch_shapes=[
            pltpu.VMEM((pulses, lines, LANES), jnp.bfloat16),
            pltpu.VMEM((lines // 2 + span // LANES - 1, 2 * pulses, LANES), jnp.bfloat16),
            pltpu.VMEM((tiles * 2 * pulses, span), jnp.bfloat16),
            pltpu.VMEM((4 * LANES, span), jnp.bfloat16),
            pltpu.VMEM((tiles * 2 * pulses, 4 * LANES), jnp.float32),
            pltpu.SemaphoreType.DMA,
        ],
        compiler_params=params(60),
        name="compress",
    )(me, band_starts, chirp_ref, samples)

    def swap(value, distance):
        return lax.ppermute(value, "tile", [(one, one ^ distance) for one in range(tiles)])

    bands = [bands[0]] + [swap(bands[dy], dy * near) for dy in range(1, far)]
    weights = interp_weights.reshape(blocks, 2, band, image_rows, places, LANES)
    weights = weights.transpose(0, 1, 2, 4, 3, 5).reshape(
        blocks * 2 * band, places * image_rows, LANES
    )
    table = pl.pallas_call(
        phase_kernel,
        out_shape=jax.ShapeDtypeStruct((blocks, parts, 2 * count, 2 * LANES), jnp.bfloat16),
        in_specs=[vmem(), vmem()],
        out_specs=vmem(),
        compiler_params=params(16),
        name="phase",
    )(doppler_rates, slot_pulse.reshape(blocks, count))
    passed = pl.pallas_call(
        relay_kernel,
        out_shape=[jax.ShapeDtypeStruct((far, 2 * pulses, band), jnp.bfloat16)] * (near - 1),
        in_specs=[vmem()] * far,
        out_specs=[vmem()] * (near - 1),
        compiler_params=params(16),
        name="relay",
    )(*bands)
    passed = [swap(passed[dz - 1], dz) for dz in range(1, near)]
    sources = bands + passed
    return pl.pallas_call(
        image_kernel,
        out_shape=jax.ShapeDtypeStruct((places, 2 * image_rows, LANES), jnp.float32),
        in_specs=[smem, vmem(), pl.BlockSpec(memory_space=pl.ANY)] + [vmem()] * len(sources),
        out_specs=vmem(),
        scratch_shapes=[
            pltpu.VMEM((tiles, 2 * pulses, band), jnp.bfloat16),
            pltpu.VMEM((blocks, 2 * band, 2 * count), jnp.bfloat16),
            pltpu.VMEM(weights.shape, jnp.bfloat16),
            pltpu.VMEM((parts, 2 * band // 8, 8, 2 * LANES), jnp.float32),
            pltpu.VMEM((parts, 2 * band // 8, 8, 2 * LANES), jnp.float32),
            pltpu.SemaphoreType.DMA((blocks * parts, 2)),
        ],
        compiler_params=params(45),
        name="image",
    )(me, table, weights, *sources)


def shards(*args):
    image = partial_image(*args)
    pieces = lax.all_to_all(image, "sub", 0, 0, tiled=True)
    return jnp.sum(pieces, 0).reshape(2, -1, LANES)


def solution(mesh):
    in_specs = (
        P(("sub", "tile"), None, None),
        P(),
        P("sub", None),
        P("sub", None),
        P("sub", None, None),
        P("sub", None, None, "tile", None),
    )
    out_specs = P(None, "tile", "sub")
    return jax.shard_map(shards, mesh=mesh, in_specs=in_specs, out_specs=out_specs, check_vma=False)
```

```python
import jax
import jax.numpy as jnp
import numpy as np
from jax import lax
from jax.experimental import pallas as pl
from jax.experimental.pallas import tpu as pltpu
from jax.sharding import PartitionSpec as P

LANES = 128


def compress_kernel(
    me_ref, starts_ref, chirp_hbm, rates_hbm, slots_hbm, echoes_ref, *rest
):
    (
        *bands_refs, rate_ref, chirp_ref, rates_ref, slots_ref, raw_ref, samples_ref, lhs_ref, toeplitz_ref,
        product_ref, sems,
    ) = rest
    fetches = [
        pltpu.make_async_copy(source, target, sems.at[index])
        for index, (source, target) in enumerate(
            (
                (chirp_hbm, chirp_ref),
                (rates_hbm, rates_ref),
                (slots_hbm, slots_ref),
                (echoes_ref, raw_ref),
            )
        )
    ]
    for fetch in fetches:
        fetch.start()
    span = toeplitz_ref.shape[1]
    blocks, tiles = starts_ref.shape
    near = tiles // len(bands_refs)
    pulses, lines, _ = raw_ref.shape
    half = pulses // blocks
    rows = 2 * half
    chunks = span // LANES
    fetches[0].wait()
    chirp = chirp_ref[...].astype(jnp.float32)
    pad = jnp.zeros((1, span - chirp.shape[1]), jnp.float32)
    for part in range(2):
        line = jnp.concatenate([chirp[part : part + 1], pad], 1)
        shifted = pltpu.roll(
            jnp.broadcast_to(line, (LANES, span)), 0, 1, stride=1, stride_axis=0
        ).astype(jnp.bfloat16)
        base = part * 2 * LANES
        toeplitz_ref[base : base + LANES, :] = shifted
        toeplitz_ref[base + LANES : base + 2 * LANES, :LANES] = jnp.zeros((LANES, LANES), jnp.bfloat16)
        toeplitz_ref[base + LANES : base + 2 * LANES, LANES:] = shifted[:, : span - LANES]
    fetches[1].wait()
    fetches[2].wait()
    count = slots_ref.shape[1]
    row = lax.broadcasted_iota(jnp.int32, (count, count), 0)
    col = lax.broadcasted_iota(jnp.int32, (count, count), 1)
    for block in range(blocks):
        slots = slots_ref[block : block + 1, :].astype(jnp.float32)
        slot = jnp.sum(jnp.where(row == col, slots, 0.0), 1, keepdims=True)
        rates = rates_ref[:, block * count : (block + 1) * count]
        rate = jnp.sum(jnp.where(slot == col.astype(jnp.float32), rates, 0.0), 1, keepdims=True)
        rate_ref[block] = jnp.broadcast_to(rate, (count, LANES))
    samples_ref[lines // 2 :] = jnp.zeros(
        (samples_ref.shape[0] - lines // 2, 2 * pulses, LANES), jnp.bfloat16
    )
    piece = 16
    side = half * piece
    row = lax.broadcasted_iota(jnp.int32, (side, side), 0)
    col = lax.broadcasted_iota(jnp.int32, (side, side), 1)
    order = jnp.where(col == (row % half) * piece + row // half, 1.0, 0.0).astype(jnp.bfloat16)
    fetches[3].wait()
    for group in range(lines // piece):
        block_rows = jnp.concatenate(
            [
                raw_ref[block * half : (block + 1) * half, group * piece : (group + 1) * piece, :].reshape(
                    side, LANES
                )
                for block in range(blocks)
            ],
            1,
        )
        moved = jnp.dot(order, block_rows, preferred_element_type=jnp.float32).astype(jnp.bfloat16)
        for block in range(blocks):
            samples_ref[
                group * piece // 2 : (group + 1) * piece // 2, block * rows : (block + 1) * rows, :
            ] = moved[:, block * LANES : (block + 1) * LANES].reshape(piece // 2, rows, LANES)
    for block in range(blocks):
        for tile in range(tiles):
            first = starts_ref[block, me_ref[0] ^ tile] // LANES
            place = (block * tiles + tile) * rows
            for chunk in range(chunks):
                lhs_ref[place : place + rows, chunk * LANES : (chunk + 1) * LANES] = samples_ref[
                    first + chunk, block * rows : (block + 1) * rows, :
                ]
    product_ref[...] = lax.dot_general(
        lhs_ref[...], toeplitz_ref[...], (((1,), (1,)), ((), ())), preferred_element_type=jnp.float32
    )
    lane = lax.broadcasted_iota(jnp.int32, (half, LANES), 1)
    for block in range(blocks):
        for tile in range(tiles):
            place = (block * tiles + tile) * rows
            shift = starts_ref[block, me_ref[0] ^ tile] % LANES
            turn = (LANES - shift) % LANES
            keep = lane < LANES - shift

            def piece(part, column):
                top = place + part * half
                low = product_ref[top : top + half, column * 2 * LANES : column * 2 * LANES + LANES]
                high = product_ref[top : top + half, column * 2 * LANES + LANES : (column + 1) * 2 * LANES]
                return low, high

            rr, ri = piece(0, 0), piece(0, 1)
            ir, ii = piece(1, 0), piece(1, 1)
            for part, (low, high) in enumerate(
                ((rr[0] + ii[0], rr[1] + ii[1]), (ir[0] - ri[0], ir[1] - ri[1]))
            ):
                cut = jnp.where(keep, pltpu.roll(low, turn, 1), pltpu.roll(high, turn, 1))
                top = block * rows + part * half
                bands_refs[tile // near][tile % near, top : top + half, :] = cut.astype(jnp.bfloat16)


def sine_cosine(angle):
    turns = jnp.round(angle * np.float32(2 / np.pi))
    rest = (angle - turns * np.float32(1.5703125)) - turns * np.float32(np.pi / 2 - 1.5703125)
    quarter = turns.astype(jnp.int32)
    sq = rest * rest
    sine = np.float32(1 / 362880) * sq + np.float32(-1 / 5040)
    sine = sine * sq + np.float32(1 / 120)
    sine = sine * sq + np.float32(-1 / 6)
    sine = sine * sq * rest + rest
    cosine = np.float32(1 / 40320) * sq + np.float32(-1 / 720)
    cosine = cosine * sq + np.float32(1 / 24)
    cosine = cosine * sq + np.float32(-1 / 2)
    cosine = cosine * sq + np.float32(1)
    odd = (quarter & 1) == 1
    sin_out = jnp.where(odd, cosine, sine)
    cos_out = jnp.where(odd, sine, cosine)
    sin_out = jnp.where((quarter & 2) == 2, -sin_out, sin_out)
    cos_out = jnp.where(((quarter + 1) & 2) == 2, -cos_out, cos_out)
    return sin_out, cos_out


def first_phase_kernel(rate_hbm, bands_hbm, table_ref, rate_ref, bands_ref, sems):
    fetches = [
        pltpu.make_async_copy(rate_hbm, rate_ref, sems.at[0]),
        pltpu.make_async_copy(bands_hbm, bands_ref, sems.at[1]),
    ]
    for fetch in fetches:
        fetch.start()
    fetches[0].wait()
    phase_table(0, rate_ref, table_ref)
    fetches[1].wait()


def second_phase_kernel(rate_ref, after_ref, table_ref):
    phase_table(1, rate_ref, table_ref)


def phase_table(block, rate_ref, table_ref):
    count = rate_ref.shape[1]
    columns = table_ref.shape[0] * table_ref.shape[2]
    lane = lax.broadcasted_iota(jnp.int32, (32, LANES), 1).astype(jnp.float32)
    place = (lane + 0.5) * np.float32(1 / columns) - 0.5
    for group in range(count // 32):
        span = slice(group * 32, group * 32 + 32)
        rate = rate_ref[block, span]
        sine, cosine = sine_cosine(rate * place)
        step_sine, step_cosine = sine_cosine(rate * np.float32(LANES / columns))
        for chunk in range(columns // LANES):
            if chunk > 0:
                sine, cosine = (
                    sine * step_cosine + cosine * step_sine,
                    cosine * step_cosine - sine * step_sine,
                )
            lanes = slice(chunk % 2 * LANES, (chunk % 2 + 1) * LANES)
            table_ref[chunk // 2, span, lanes] = cosine.astype(jnp.bfloat16)
            table_ref[chunk // 2, count + group * 32 : count + group * 32 + 32, lanes] = (
                sine.astype(jnp.bfloat16)
            )


def relay_kernel(after_ref, *refs):
    near = refs[0].shape[0]
    far = len(refs) - near + 1
    for dz in range(1, near):
        for dy in range(far):
            refs[far + dz - 1][dy] = refs[dy][dz]


def weighted_sum(side, table_refs, weights_ref, image_ref, left_ref, near_weights_ref, first_ref, second_ref, sem):
    blocks = len(table_refs)
    places, lines, _ = image_ref.shape
    image_rows = lines // 2
    parts = places // 2
    band = weights_ref.shape[0] // (2 * blocks)
    depth = band // parts
    held = places * image_rows
    focused_refs = (first_ref, second_ref)
    ahead = 3

    def weights_copy(step, part):
        span = pl.ds((step // parts * 2 + part) * band + step % parts * depth, depth)
        rows = pl.ds(pl.multiple_of(side * held, held), held)
        return pltpu.make_async_copy(
            weights_ref.at[span, rows], near_weights_ref.at[span], sem.at[step, part]
        )

    def focus(block, part):
        target_ref = focused_refs[block]
        target_ref[part] = jnp.dot(
            left_ref[block], table_refs[block][side * parts + part], preferred_element_type=jnp.float32
        ).reshape(target_ref.shape[1:])

    for step in range(ahead):
        for part in range(2):
            weights_copy(step, part).start()
    yield
    for part in range(parts):
        focus(0, part)

    upper = lax.broadcasted_iota(jnp.int32, (8, LANES), 0) < 4
    sums = tuple(jnp.zeros((8, LANES), jnp.float32) for _ in range(places))
    for block in range(blocks):
        focused_ref = focused_refs[block]

        def step(chunk, sums):
            sums = list(sums)
            now = block * parts + chunk
            for part in range(2):
                weights_copy(now, part).wait()

            @pl.when(now + ahead < blocks * parts)
            def _():
                for part in range(2):
                    weights_copy(now + ahead, part).start()

            if block + 1 < blocks:
                focus(block + 1, chunk)
            for line in range(depth // 8):
                for quad in range(places // 4):
                    held_rows = {}
                    for one in range(2):
                        for part in range(2):
                            held_rows[one, part] = focused_ref[
                                2 * quad + one, part * (band // 8) + chunk * (depth // 8) + line, :, LANES:
                            ]
                    for inner in range(8):
                        k = chunk * depth + line * 8 + inner
                        span = slice(quad * 16, quad * 16 + 16)
                        weight_real = near_weights_ref[block * 2 * band + k, span, :].astype(jnp.float32)
                        weight_imag = near_weights_ref[
                            (block * 2 + 1) * band + k, span, :
                        ].astype(jnp.float32)
                        for one in range(2):
                            wr = weight_real[one * 8 : one * 8 + 8]
                            wi = weight_imag[one * 8 : one * 8 + 8]

                            def value(part):
                                low = focused_ref[
                                    2 * quad + one,
                                    part * (band // 8) + chunk * (depth // 8) + line,
                                    inner : inner + 1,
                                    :LANES,
                                ]
                                high = held_rows[one, part][inner : inner + 1]
                                return jnp.where(
                                    upper,
                                    jnp.broadcast_to(low, (8, LANES)),
                                    jnp.broadcast_to(high, (8, LANES)),
                                )

                            fr = value(0)
                            fi = value(1)
                            at = 2 * (2 * quad + one)
                            sums[at] = sums[at] + (wr * fr - wi * fi)
                            sums[at + 1] = sums[at + 1] + (wr * fi + wi * fr)
            return tuple(sums)

        sums = lax.fori_loop(0, parts, step, sums)
    for pair in range(places // 2):
        real, imag = sums[2 * pair], sums[2 * pair + 1]
        image_ref[2 * pair] = jnp.concatenate([real[:image_rows], imag[:image_rows]], 0)
        image_ref[2 * pair + 1] = jnp.concatenate([real[image_rows:], imag[image_rows:]], 0)
    yield


def far_image_kernel(me_ref, sub_ref, first_table_ref, second_table_ref, weights_ref, *rest):
    *sources_refs, image_ref, left_ref, bands_ref, near_weights_ref, first_ref, second_ref, sem = rest
    work = weighted_sum(
        1 - (sub_ref[0] >> 3), (first_table_ref, second_table_ref), weights_ref, image_ref, left_ref,
        near_weights_ref, first_ref, second_ref, sem,
    )
    next(work)
    sources, band_rows, band = bands_ref.shape
    far_count = len(sources_refs) // 2 + 1
    near_refs, far_refs = sources_refs[:far_count], sources_refs[far_count:]
    near = sources // far_count
    blocks = left_ref.shape[0]
    rows = band_rows // blocks
    half = rows // 2
    count = sources * half
    for dy in range(far_count):
        bands_ref[me_ref[0] ^ (dy * near)] = near_refs[dy][0]
        for dz in range(1, near):
            bands_ref[me_ref[0] ^ (dy * near + dz)] = far_refs[dz - 1][dy]
    for block in range(blocks):
        real = bands_ref[:, block * rows : block * rows + half, :].reshape(count, band)
        imag = bands_ref[:, block * rows + half : (block + 1) * rows, :].reshape(count, band)
        top = jnp.concatenate([real, imag], 1)
        bottom = jnp.concatenate([-imag, real], 1)
        left_ref[block] = jnp.concatenate([top, bottom], 0).T
    next(work)


def near_image_kernel(
    sub_ref, first_table_ref, second_table_ref, weights_ref, left_ref, after_ref, image_ref,
    near_weights_ref, first_ref, second_ref, sem,
):
    work = weighted_sum(
        sub_ref[0] >> 3, (first_table_ref, second_table_ref), weights_ref, image_ref, left_ref,
        near_weights_ref, first_ref, second_ref, sem,
    )
    next(work)
    next(work)


def split_kernel(sub_ref, mine_ref, came_ref, *out_refs):
    width = out_refs[0].shape[0]
    for dx, out_ref in enumerate(out_refs):
        first = ((sub_ref[0] >> 1 & 3) ^ dx) * width
        for core in range(width):
            out_ref[core] = mine_ref[first + core] + came_ref[first + core]


def join_kernel(sub_ref, *refs):
    *piece_refs, keep_ref, send_ref = refs
    for out_ref, core in ((keep_ref, sub_ref[0] & 1), (send_ref, 1 - (sub_ref[0] & 1))):
        out_ref[...] = (piece_refs[0][core] + piece_refs[1][core]) + (
            piece_refs[2][core] + piece_refs[3][core]
        )


def params(mib):
    return pltpu.CompilerParams(vmem_limit_bytes=mib * 1024 * 1024)


def vmem():
    return pl.BlockSpec(memory_space=pltpu.VMEM)


def call(kernel, name, mib, out_shape, in_specs, scratch=()):
    multiple = isinstance(out_shape, list)
    return pl.pallas_call(
        kernel,
        out_shape=out_shape,
        in_specs=in_specs,
        out_specs=[vmem()] * len(out_shape) if multiple else vmem(),
        scratch_shapes=list(scratch),
        compiler_params=params(mib),
        name=name,
    )


def partial_image(echoes, chirp_ref, band_starts, doppler_rates, slot_pulse, interp_weights):
    pulses, _, pulse_len = echoes.shape
    chirp_len = chirp_ref.shape[1]
    blocks, tiles = band_starts.shape
    _, _, band, image_rows, columns = interp_weights.shape
    count = slot_pulse.shape[2]
    lines = 2 * pulse_len // LANES
    span = chirp_len + 2 * LANES
    places = columns // LANES
    parts = places // 2
    near = 4
    far = tiles // near
    smem = pl.BlockSpec(memory_space=pltpu.SMEM)
    anywhere = pl.BlockSpec(memory_space=pl.ANY)
    shape = jax.ShapeDtypeStruct
    sub = lax.axis_index("sub").astype(jnp.int32).reshape(1)
    me = lax.axis_index("tile").astype(jnp.int32).reshape(1)

    samples = echoes.reshape(pulses, 2, pulse_len // LANES, LANES).transpose(0, 2, 1, 3)
    samples = samples.reshape(pulses, lines, LANES)
    weights = interp_weights.reshape(blocks, 2, band, image_rows, places, LANES)
    weights = weights.transpose(0, 1, 2, 4, 3, 5).reshape(
        blocks * 2 * band, places * image_rows, LANES
    )
    own = shape((near, 2 * pulses, band), jnp.bfloat16)
    rates = shape((blocks, count, LANES), jnp.float32)
    *bands, rate = call(
        compress_kernel,
        "compress",
        60,
        [own] * far + [rates],
        [smem, smem] + [anywhere] * 4,
        [
            pltpu.VMEM((2, chirp_len), jnp.bfloat16),
            pltpu.VMEM((1, blocks * count), jnp.float32),
            pltpu.VMEM((blocks, count), jnp.int32),
            pltpu.VMEM((pulses, lines, LANES), jnp.bfloat16),
            pltpu.VMEM((lines // 2 + span // LANES - 1, 2 * pulses, LANES), jnp.bfloat16),
            pltpu.VMEM((tiles * 2 * pulses, span), jnp.bfloat16),
            pltpu.VMEM((4 * LANES, span), jnp.bfloat16),
            pltpu.VMEM((tiles * 2 * pulses, 4 * LANES), jnp.float32),
            pltpu.SemaphoreType.DMA((4,)),
        ],
    )(me, band_starts, chirp_ref, doppler_rates, slot_pulse.reshape(blocks, count), samples)

    def swap(value, distance):
        return lax.ppermute(value, "tile", [(one, one ^ distance) for one in range(tiles)])

    table = shape((parts, 2 * count, 2 * LANES), jnp.bfloat16)
    first_table, rate, mine = call(
        first_phase_kernel,
        "phase",
        16,
        [table, rates, own],
        [anywhere] * 2,
        [pltpu.SemaphoreType.DMA((2,))],
    )(rate, bands[0])
    bands = [mine] + [swap(bands[dy], dy * near) for dy in range(1, far)]
    passed = call(
        relay_kernel,
        "relay",
        16,
        [shape((far, 2 * pulses, band), jnp.bfloat16)] * (near - 1),
        [anywhere] + [vmem()] * far,
    )(first_table, *bands)
    second_table = call(second_phase_kernel, "phase", 16, table, [vmem(), anywhere])(rate, passed[0])
    passed = [swap(passed[dz - 1], dz) for dz in range(1, near)]
    sources = bands + passed
    half = shape((places // 2, 2 * image_rows, LANES), jnp.float32)
    near_weights = pltpu.VMEM((blocks * 2 * band, places // 2 * image_rows, LANES), jnp.bfloat16)
    focused = pltpu.VMEM((parts // 2, 2 * band // 8, 8, 2 * LANES), jnp.float32)
    sems = pltpu.SemaphoreType.DMA((blocks * parts // 2, 2))
    far_image, left = call(
        far_image_kernel,
        "far_image",
        45,
        [half, shape((blocks, 2 * band, 2 * count), jnp.bfloat16)],
        [smem, smem, vmem(), vmem(), anywhere] + [vmem()] * len(sources),
        [
            pltpu.VMEM((tiles, 2 * pulses, band), jnp.bfloat16),
            near_weights,
            focused,
            focused,
            sems,
        ],
    )(me, sub, first_table, second_table, weights, *sources)
    near_image = call(
        near_image_kernel,
        "near_image",
        45,
        half,
        [smem, vmem(), vmem(), anywhere, vmem(), anywhere],
        [near_weights, focused, focused, sems],
    )(sub, first_table, second_table, weights, left, far_image)
    return sub, far_image, near_image


def shards(*args):
    sub, far_image, near_image = partial_image(*args)
    smem = pl.BlockSpec(memory_space=pltpu.SMEM)
    size = 16

    def swap(value, distance):
        return lax.ppermute(value, "sub", [(one, one ^ distance) for one in range(size)])

    came = swap(far_image, 8)
    _, lines, _ = far_image.shape
    pair = jax.ShapeDtypeStruct((2, lines, LANES), jnp.float32)
    one = jax.ShapeDtypeStruct((lines, LANES), jnp.float32)
    pieces = call(split_kernel, "split", 16, [pair] * 4, [smem, vmem(), vmem()])(sub, near_image, came)
    pieces = [pieces[0]] + [swap(pieces[dx], 2 * dx) for dx in range(1, 4)]
    keep, send = call(join_kernel, "join", 16, [one, one], [smem] + [vmem()] * 4)(sub, *pieces)
    return (keep + swap(send, 1)).reshape(2, -1, LANES)


def solution(mesh):
    in_specs = (
        P(("sub", "tile"), None, None),
        P(),
        P("sub", None),
        P("sub", None),
        P("sub", None, None),
        P("sub", None, None, "tile", None),
    )
    out_specs = P(None, "tile", "sub")
    return jax.shard_map(shards, mesh=mesh, in_specs=in_specs, out_specs=out_specs, check_vma=False)
```

```python
import jax
import jax.numpy as jnp
import numpy as np
from jax import lax
from jax.experimental import pallas as pl
from jax.experimental.pallas import tpu as pltpu
from jax.sharding import PartitionSpec as P

LANES = 128


def compress_kernel(
    me_ref, starts_ref, chirp_hbm, rates_hbm, slots_hbm, echoes_ref, *rest
):
    (
        *bands_refs, extra_ref, chirp_ref, rates_ref, slots_ref, raw_ref, samples_ref, lhs_ref, toeplitz_ref,
        product_ref, sems,
    ) = rest
    fetches = [
        pltpu.make_async_copy(source, target, sems.at[index])
        for index, (source, target) in enumerate(
            (
                (chirp_hbm, chirp_ref),
                (rates_hbm, rates_ref),
                (slots_hbm, slots_ref),
                (echoes_ref, raw_ref),
            )
        )
    ]
    for fetch in fetches:
        fetch.start()
    span = toeplitz_ref.shape[1]
    blocks, tiles = starts_ref.shape
    near = tiles // (len(bands_refs) + 1)
    pulses, lines, _ = raw_ref.shape
    half = pulses // blocks
    rows = 2 * half
    chunks = span // LANES
    fetches[0].wait()
    chirp = chirp_ref[...].astype(jnp.float32)
    pad = jnp.zeros((1, span - chirp.shape[1]), jnp.float32)
    for part in range(2):
        line = jnp.concatenate([chirp[part : part + 1], pad], 1)
        shifted = pltpu.roll(
            jnp.broadcast_to(line, (LANES, span)), 0, 1, stride=1, stride_axis=0
        ).astype(jnp.bfloat16)
        base = part * 2 * LANES
        toeplitz_ref[base : base + LANES, :] = shifted
        toeplitz_ref[base + LANES : base + 2 * LANES, :LANES] = jnp.zeros((LANES, LANES), jnp.bfloat16)
        toeplitz_ref[base + LANES : base + 2 * LANES, LANES:] = shifted[:, : span - LANES]
    fetches[1].wait()
    fetches[2].wait()
    count = slots_ref.shape[1]
    row = lax.broadcasted_iota(jnp.int32, (count, count), 0)
    col = lax.broadcasted_iota(jnp.int32, (count, count), 1)
    for block in range(blocks):
        slots = slots_ref[block : block + 1, :].astype(jnp.float32)
        slot = jnp.sum(jnp.where(row == col, slots, 0.0), 1, keepdims=True)
        rates = rates_ref[:, block * count : (block + 1) * count]
        rate = jnp.sum(jnp.where(slot == col.astype(jnp.float32), rates, 0.0), 1, keepdims=True)
        extra_ref[block * count : (block + 1) * count, :] = jnp.broadcast_to(rate, (count, LANES))
    samples_ref[lines // 2 :] = jnp.zeros(
        (samples_ref.shape[0] - lines // 2, 2 * pulses, LANES), jnp.bfloat16
    )
    piece = 16
    side = half * piece
    row = lax.broadcasted_iota(jnp.int32, (side, side), 0)
    col = lax.broadcasted_iota(jnp.int32, (side, side), 1)
    order = jnp.where(col == (row % half) * piece + row // half, 1.0, 0.0).astype(jnp.bfloat16)
    fetches[3].wait()
    for group in range(lines // piece):
        block_rows = jnp.concatenate(
            [
                raw_ref[block * half : (block + 1) * half, group * piece : (group + 1) * piece, :].reshape(
                    side, LANES
                )
                for block in range(blocks)
            ],
            1,
        )
        moved = jnp.dot(order, block_rows, preferred_element_type=jnp.float32).astype(jnp.bfloat16)
        for block in range(blocks):
            samples_ref[
                group * piece // 2 : (group + 1) * piece // 2, block * rows : (block + 1) * rows, :
            ] = moved[:, block * LANES : (block + 1) * LANES].reshape(piece // 2, rows, LANES)
    for block in range(blocks):
        for tile in range(tiles):
            first = starts_ref[block, me_ref[0] ^ tile] // LANES
            place = (block * tiles + tile) * rows
            for chunk in range(chunks):
                lhs_ref[place : place + rows, chunk * LANES : (chunk + 1) * LANES] = samples_ref[
                    first + chunk, block * rows : (block + 1) * rows, :
                ]
    product_ref[...] = lax.dot_general(
        lhs_ref[...], toeplitz_ref[...], (((1,), (1,)), ((), ())), preferred_element_type=jnp.float32
    )
    lane = lax.broadcasted_iota(jnp.int32, (half, LANES), 1)
    for block in range(blocks):
        for tile in range(tiles):
            place = (block * tiles + tile) * rows
            shift = starts_ref[block, me_ref[0] ^ tile] % LANES
            turn = (LANES - shift) % LANES
            keep = lane < LANES - shift

            def piece(part, column):
                top = place + part * half
                low = product_ref[top : top + half, column * 2 * LANES : column * 2 * LANES + LANES]
                high = product_ref[top : top + half, column * 2 * LANES + LANES : (column + 1) * 2 * LANES]
                return low, high

            rr, ri = piece(0, 0), piece(0, 1)
            ir, ii = piece(1, 0), piece(1, 1)
            for part, (low, high) in enumerate(
                ((rr[0] + ii[0], rr[1] + ii[1]), (ir[0] - ri[0], ir[1] - ri[1]))
            ):
                cut = jnp.where(keep, pltpu.roll(low, turn, 1), pltpu.roll(high, turn, 1))
                top = block * rows + part * half
                cut = cut.astype(jnp.bfloat16)
                if tile < near:
                    top += blocks * count + tile * 2 * pulses
                    extra_ref[top : top + half, :] = cut.astype(jnp.float32)
                else:
                    bands_refs[tile // near - 1][tile % near, top : top + half, :] = cut


def sine_cosine(angle):
    turns = jnp.round(angle * np.float32(2 / np.pi))
    rest = (angle - turns * np.float32(1.5703125)) - turns * np.float32(np.pi / 2 - 1.5703125)
    quarter = turns.astype(jnp.int32)
    sq = rest * rest
    sine = np.float32(1 / 362880) * sq + np.float32(-1 / 5040)
    sine = sine * sq + np.float32(1 / 120)
    sine = sine * sq + np.float32(-1 / 6)
    sine = sine * sq * rest + rest
    cosine = np.float32(1 / 40320) * sq + np.float32(-1 / 720)
    cosine = cosine * sq + np.float32(1 / 24)
    cosine = cosine * sq + np.float32(-1 / 2)
    cosine = cosine * sq + np.float32(1)
    odd = (quarter & 1) == 1
    sin_out = jnp.where(odd, cosine, sine)
    cos_out = jnp.where(odd, sine, cosine)
    sin_out = jnp.where((quarter & 2) == 2, -sin_out, sin_out)
    cos_out = jnp.where(((quarter + 1) & 2) == 2, -cos_out, cos_out)
    return sin_out, cos_out


def phase_kernel(extra_ref, first_table_ref, second_table_ref, bands_ref):
    count = first_table_ref.shape[1] // 2
    bands_ref[...] = extra_ref[2 * count :].astype(jnp.bfloat16).reshape(bands_ref.shape)
    phase_table(0, extra_ref, first_table_ref)
    phase_table(1, extra_ref, second_table_ref)


def turn_kernel(weights_ref, after_ref, first_ref, second_ref):
    band = first_ref.shape[2]
    lines = first_ref.shape[1]
    size = 16
    side = size * size
    row = lax.broadcasted_iota(jnp.int32, (side, side), 0)
    col = lax.broadcasted_iota(jnp.int32, (side, side), 1)
    order = jnp.where(col == (row % size) * size + row // size, 1.0, 0.0).astype(jnp.bfloat16)
    for block, out_ref in enumerate((first_ref, second_ref)):
        for part in range(2):

            def step(chunk, carry, block=block, part=part, out_ref=out_ref):
                first = pl.multiple_of(chunk * size, size)
                for pair in range(lines // (2 * size)):
                    tops = [(2 * pair + one) * size for one in range(2)]
                    block_rows = jnp.concatenate(
                        [
                            weights_ref[
                                pl.ds((block * 2 + part) * band + first, size), top : top + size, :
                            ].reshape(side, LANES)
                            for top in tops
                        ],
                        1,
                    )
                    moved = jnp.dot(order, block_rows, preferred_element_type=jnp.float32).astype(
                        jnp.bfloat16
                    )
                    for one, top in enumerate(tops):
                        out_ref[part, top : top + size, pl.ds(first, size), :] = moved[
                            :, one * LANES : (one + 1) * LANES
                        ].reshape(size, size, LANES)
                return carry

            lax.fori_loop(0, band // size, step, 0, unroll=True)


def phase_table(block, rate_ref, table_ref):
    count = table_ref.shape[1] // 2
    columns = table_ref.shape[0] * table_ref.shape[2]
    lane = lax.broadcasted_iota(jnp.int32, (32, LANES), 1).astype(jnp.float32)
    place = (lane + 0.5) * np.float32(1 / columns) - 0.5
    for group in range(count // 32):
        span = slice(group * 32, group * 32 + 32)
        rate = rate_ref[block * count + group * 32 : block * count + group * 32 + 32, :]
        sine, cosine = sine_cosine(rate * place)
        step_sine, step_cosine = sine_cosine(rate * np.float32(LANES / columns))
        for chunk in range(columns // LANES):
            if chunk > 0:
                sine, cosine = (
                    sine * step_cosine + cosine * step_sine,
                    cosine * step_cosine - sine * step_sine,
                )
            lanes = slice(chunk % 2 * LANES, (chunk % 2 + 1) * LANES)
            table_ref[chunk // 2, span, lanes] = cosine.astype(jnp.bfloat16)
            table_ref[chunk // 2, count + group * 32 : count + group * 32 + 32, lanes] = (
                sine.astype(jnp.bfloat16)
            )


def relay_kernel(after_ref, *refs):
    near = refs[0].shape[0]
    far = len(refs) - near + 1
    for dz in range(1, near):
        for dy in range(far):
            refs[far + dz - 1][dy] = refs[dy][dz]


def weighted_sum(side, table_refs, weights_refs, image_ref, left_ref, focused_refs):
    blocks = len(table_refs)
    places, lines, _ = image_ref.shape
    image_rows = lines // 2
    pairs = places // 2
    band = weights_refs[0].shape[2]

    def focus(pair):
        for block in range(blocks):
            focused_refs[pair % 2 * blocks + block][...] = jnp.dot(
                left_ref[block], table_refs[block][side * pairs + pair], preferred_element_type=jnp.float32
            )

    focus(0)
    for pair in range(pairs):
        if pair + 1 < pairs:
            focus(pair + 1)
        for place in range(2):
            lanes = slice(place * LANES, (place + 1) * LANES)
            real = [jnp.zeros((8, LANES), jnp.float32)] * image_rows
            imag = [jnp.zeros((8, LANES), jnp.float32)] * image_rows
            for block in range(blocks):
                focused_ref = focused_refs[pair % 2 * blocks + block]
                for k in range(0, band, 16):
                    focus_real = focused_ref[k : k + 16, lanes]
                    focus_imag = focused_ref[band + k : band + k + 16, lanes]
                    for row in range(image_rows):
                        line = (side * places + 2 * pair + place) * image_rows + row
                        weight_real = weights_refs[block][0, line, k : k + 16, :].astype(jnp.float32)
                        weight_imag = weights_refs[block][1, line, k : k + 16, :].astype(jnp.float32)
                        for first in (0, 8):
                            part = slice(first, first + 8)
                            wr, wi = weight_real[part], weight_imag[part]
                            fr, fi = focus_real[part], focus_imag[part]
                            real[row] = real[row] + (wr * fr - wi * fi)
                            imag[row] = imag[row] + (wr * fi + wi * fr)
            image_ref[2 * pair + place] = jnp.concatenate(
                [jnp.sum(one, 0, keepdims=True) for one in real + imag], 0
            )


def far_image_kernel(
    me_ref, sub_ref, first_table_ref, second_table_ref, first_weights_ref, second_weights_ref, *rest
):
    *sources_refs, image_ref, left_ref, bands_ref, one_ref, two_ref, three_ref, four_ref = rest
    sources, band_rows, band = bands_ref.shape
    far_count = len(sources_refs) // 2 + 1
    near_refs, far_refs = sources_refs[:far_count], sources_refs[far_count:]
    near = sources // far_count
    blocks = left_ref.shape[0]
    rows = band_rows // blocks
    half = rows // 2
    count = sources * half
    for dy in range(far_count):
        bands_ref[me_ref[0] ^ (dy * near)] = near_refs[dy][0]
        for dz in range(1, near):
            bands_ref[me_ref[0] ^ (dy * near + dz)] = far_refs[dz - 1][dy]
    for block in range(blocks):
        real = bands_ref[:, block * rows : block * rows + half, :].reshape(count, band)
        imag = bands_ref[:, block * rows + half : (block + 1) * rows, :].reshape(count, band)
        top = jnp.concatenate([real, imag], 1)
        bottom = jnp.concatenate([-imag, real], 1)
        left_ref[block] = jnp.concatenate([top, bottom], 0).T
    weighted_sum(
        1 - (sub_ref[0] >> 3),
        (first_table_ref, second_table_ref),
        (first_weights_ref, second_weights_ref),
        image_ref,
        left_ref,
        (one_ref, two_ref, three_ref, four_ref),
    )


def near_image_kernel(
    sub_ref, first_table_ref, second_table_ref, first_weights_ref, second_weights_ref, left_ref, after_ref,
    image_ref, one_ref, two_ref, three_ref, four_ref,
):
    weighted_sum(
        sub_ref[0] >> 3,
        (first_table_ref, second_table_ref),
        (first_weights_ref, second_weights_ref),
        image_ref,
        left_ref,
        (one_ref, two_ref, three_ref, four_ref),
    )


def params(mib):
    return pltpu.CompilerParams(vmem_limit_bytes=mib * 1024 * 1024)


def vmem():
    return pl.BlockSpec(memory_space=pltpu.VMEM)


def call(kernel, name, mib, out_shape, in_specs, scratch=(), flops=0):
    multiple = isinstance(out_shape, list)
    return pl.pallas_call(
        kernel,
        out_shape=out_shape,
        in_specs=in_specs,
        out_specs=[vmem()] * len(out_shape) if multiple else vmem(),
        scratch_shapes=list(scratch),
        compiler_params=params(mib),
        cost_estimate=pl.CostEstimate(flops=flops, bytes_accessed=0, transcendentals=0),
        name=name,
    )


def partial_image(echoes, chirp_ref, band_starts, doppler_rates, slot_pulse, interp_weights):
    pulses, _, pulse_len = echoes.shape
    chirp_len = chirp_ref.shape[1]
    blocks, tiles = band_starts.shape
    _, _, band, image_rows, columns = interp_weights.shape
    count = slot_pulse.shape[2]
    lines = 2 * pulse_len // LANES
    span = chirp_len + 2 * LANES
    places = columns // LANES
    parts = places // 2
    near = 4
    far = tiles // near
    smem = pl.BlockSpec(memory_space=pltpu.SMEM)
    anywhere = pl.BlockSpec(memory_space=pl.ANY)
    shape = jax.ShapeDtypeStruct
    sub = lax.axis_index("sub").astype(jnp.int32).reshape(1)
    me = lax.axis_index("tile").astype(jnp.int32).reshape(1)

    samples = echoes.reshape(pulses, 2, pulse_len // LANES, LANES).transpose(0, 2, 1, 3)
    samples = samples.reshape(pulses, lines, LANES)
    weights = interp_weights.reshape(blocks, 2, band, image_rows, places, LANES)
    weights = weights.transpose(0, 1, 2, 4, 3, 5).reshape(
        blocks * 2 * band, places * image_rows, LANES
    )
    own = shape((near, 2 * pulses, band), jnp.bfloat16)
    extras = shape((blocks * count + near * 2 * pulses, LANES), jnp.float32)
    *bands, extra = call(
        compress_kernel,
        "compress",
        60,
        [own] * (far - 1) + [extras],
        [smem, smem] + [anywhere] * 4,
        [
            pltpu.VMEM((2, chirp_len), jnp.bfloat16),
            pltpu.VMEM((1, blocks * count), jnp.float32),
            pltpu.VMEM((blocks, count), jnp.int32),
            pltpu.VMEM((pulses, lines, LANES), jnp.bfloat16),
            pltpu.VMEM((lines // 2 + span // LANES - 1, 2 * pulses, LANES), jnp.bfloat16),
            pltpu.VMEM((tiles * 2 * pulses, span), jnp.bfloat16),
            pltpu.VMEM((4 * LANES, span), jnp.bfloat16),
            pltpu.VMEM((tiles * 2 * pulses, 4 * LANES), jnp.float32),
            pltpu.SemaphoreType.DMA((4,)),
        ],
        flops=6 * 10**9,
    )(me, band_starts, chirp_ref, doppler_rates, slot_pulse.reshape(blocks, count), samples)

    def swap(value, distance):
        return lax.ppermute(value, "tile", [(one, one ^ distance) for one in range(tiles)])

    table = shape((parts, 2 * count, 2 * LANES), jnp.bfloat16)
    turned = shape((2, places * image_rows, band, LANES), jnp.bfloat16)
    first_table, second_table, mine = call(phase_kernel, "phase", 12, [table, table, own], [vmem()], flops=4 * 10**9)(extra)
    bands = [mine] + [swap(bands[dy - 1], dy * near) for dy in range(1, far)]
    passed = call(
        relay_kernel,
        "relay",
        16,
        [shape((far, 2 * pulses, band), jnp.bfloat16)] * (near - 1),
        [anywhere] + [vmem()] * far,
    )(first_table, *bands)
    first_weights, second_weights = call(turn_kernel, "turn", 12, [turned, turned], [vmem(), anywhere], flops=4 * 10**9)(
        weights, passed[0]
    )
    passed = [swap(passed[dz - 1], dz) for dz in range(1, near)]
    sources = bands + passed
    half = shape((places // 2, 2 * image_rows, LANES), jnp.float32)
    focused = [pltpu.VMEM((2 * band, 2 * LANES), jnp.float32)] * (2 * blocks)
    far_image, left = call(
        far_image_kernel,
        "far_image",
        12,
        [half, shape((blocks, 2 * band, 2 * count), jnp.bfloat16)],
        [smem, smem] + [vmem()] * (4 + len(sources)),
        [pltpu.VMEM((tiles, 2 * pulses, band), jnp.bfloat16)] + focused,
        flops=3 * 10**9,
    )(me, sub, first_table, second_table, first_weights, second_weights, *sources)
    near_image = call(
        near_image_kernel, "near_image", 12, half, [smem] + [vmem()] * 5 + [anywhere], focused, flops=3 * 10**9
    )(sub, first_table, second_table, first_weights, second_weights, left, far_image)
    return sub, far_image, near_image


def shards(*args):
    _, far_image, near_image = partial_image(*args)
    size = 16
    half = size // 2
    came = lax.ppermute(far_image, "sub", [(one, one ^ half) for one in range(size)])
    groups = [list(range(half)), list(range(half, size))]
    pieces = lax.all_to_all(near_image + came, "sub", 0, 0, axis_index_groups=groups, tiled=True)
    return jnp.sum(pieces, 0).reshape(2, -1, LANES)


def solution(mesh):
    in_specs = (
        P(("sub", "tile"), None, None),
        P(),
        P("sub", None),
        P("sub", None),
        P("sub", None, None),
        P("sub", None, None, "tile", None),
    )
    out_specs = P(None, "tile", "sub")
    return jax.shard_map(shards, mesh=mesh, in_specs=in_specs, out_specs=out_specs, check_vma=False)
```

```python
import jax
import jax.numpy as jnp
import numpy as np
from jax import lax
from jax.experimental import pallas as pl
from jax.experimental.pallas import tpu as pltpu
from jax.sharding import PartitionSpec as P

LANES = 128


def compress_kernel(
    me_ref, sub_ref, starts_ref, chirp_hbm, rates_hbm, slots_hbm, echoes_ref, *rest
):
    (
        *bands_refs, extra_ref, chirp_ref, rates_ref, slots_ref, raw_ref, samples_ref, toeplitz_ref,
        lhs_a, lhs_b, lhs_c, lhs_d, sems,
    ) = rest
    fetches = [
        pltpu.make_async_copy(source, target, sems.at[index])
        for index, (source, target) in enumerate(
            (
                (chirp_hbm, chirp_ref),
                (rates_hbm, rates_ref),
                (slots_hbm, slots_ref),
                (echoes_ref, raw_ref),
            )
        )
    ]
    for fetch in fetches:
        fetch.start()
    span = toeplitz_ref.shape[1]
    blocks, tiles = starts_ref.shape
    near = tiles // (len(bands_refs) + 1)
    pulses, lines, _ = raw_ref.shape
    half = pulses // blocks
    rows = 2 * half
    chunks = span // LANES
    samples_ref[lines // 2 :] = jnp.zeros(
        (samples_ref.shape[0] - lines // 2, 2 * pulses, LANES), jnp.bfloat16
    )
    piece = 16
    side = half * piece
    row = lax.broadcasted_iota(jnp.int32, (side, side), 0)
    col = lax.broadcasted_iota(jnp.int32, (side, side), 1)
    order = jnp.where(col == (row % half) * piece + row // half, 1.0, 0.0).astype(jnp.bfloat16)
    fetches[0].wait()
    chirp = chirp_ref[...].astype(jnp.float32)
    pad = jnp.zeros((1, span - chirp.shape[1]), jnp.float32)
    for part in range(2):
        line = jnp.concatenate([chirp[part : part + 1], pad], 1)
        shifted = pltpu.roll(
            jnp.broadcast_to(line, (LANES, span)), 0, 1, stride=1, stride_axis=0
        ).astype(jnp.bfloat16)
        base = part * 2 * LANES
        toeplitz_ref[base : base + LANES, :] = shifted
        toeplitz_ref[base + LANES : base + 2 * LANES, :LANES] = jnp.zeros((LANES, LANES), jnp.bfloat16)
        toeplitz_ref[base + LANES : base + 2 * LANES, LANES:] = shifted[:, : span - LANES]
    fetches[1].wait()
    fetches[2].wait()
    count = slots_ref.shape[1]
    row = lax.broadcasted_iota(jnp.int32, (count, count), 0)
    col = lax.broadcasted_iota(jnp.int32, (count, count), 1)
    for block in range(blocks):
        slots = slots_ref[block : block + 1, :].astype(jnp.float32)
        slot = jnp.sum(jnp.where(row == col, slots, 0.0), 1, keepdims=True)
        rates = rates_ref[:, block * count : (block + 1) * count]
        rate = jnp.sum(jnp.where(slot == col.astype(jnp.float32), rates, 0.0), 1, keepdims=True)
        extra_ref[block * count : (block + 1) * count, :] = jnp.broadcast_to(rate, (count, LANES))
    fetches[3].wait()
    for group in range(lines // piece):
        block_rows = jnp.concatenate(
            [
                raw_ref[block * half : (block + 1) * half, group * piece : (group + 1) * piece, :].reshape(
                    side, LANES
                )
                for block in range(blocks)
            ],
            1,
        )
        moved = jnp.dot(order, block_rows, preferred_element_type=jnp.float32).astype(jnp.bfloat16)
        for block in range(blocks):
            samples_ref[
                group * piece // 2 : (group + 1) * piece // 2, block * rows : (block + 1) * rows, :
            ] = moved[:, block * LANES : (block + 1) * LANES].reshape(piece // 2, rows, LANES)
    lane = lax.broadcasted_iota(jnp.int32, (half, LANES), 1)
    lhs_refs = (lhs_a, lhs_b, lhs_c, lhs_d)

    def gather(dy):
        for dz in range(near):
            for block in range(blocks):
                first = starts_ref[block, me_ref[0] ^ (dy * near + dz)] // LANES
                place = (dz * blocks + block) * rows
                for chunk in range(chunks):
                    lhs_refs[dy][place : place + rows, chunk * LANES : (chunk + 1) * LANES] = samples_ref[
                        first + chunk, block * rows : (block + 1) * rows, :
                    ]

    def correlate(dy):
        return lax.dot_general(
            lhs_refs[dy][...],
            toeplitz_ref[...],
            (((1,), (1,)), ((), ())),
            preferred_element_type=jnp.float32,
        )

    def cut(dy, product):
        for dz in range(near):
            for block in range(blocks):
                place = (dz * blocks + block) * rows
                shift = starts_ref[block, me_ref[0] ^ (dy * near + dz)] % LANES
                turn = (LANES - shift) % LANES
                keep = lane < LANES - shift

                def piece(part, column):
                    rows_of = product[place + part * half : place + (part + 1) * half]
                    left = column * 2 * LANES
                    return rows_of[:, left : left + LANES], rows_of[:, left + LANES : left + 2 * LANES]

                rr, ri = piece(0, 0), piece(0, 1)
                ir, ii = piece(1, 0), piece(1, 1)
                for part, (low, high) in enumerate(
                    ((rr[0] + ii[0], rr[1] + ii[1]), (ir[0] - ri[0], ir[1] - ri[1]))
                ):
                    band = jnp.where(keep, pltpu.roll(low, turn, 1), pltpu.roll(high, turn, 1))
                    band = band.astype(jnp.bfloat16)
                    top = block * rows + part * half
                    if dy == 0:
                        top += blocks * count + dz * 2 * pulses
                        extra_ref[top : top + half, :] = band.astype(jnp.float32)
                    else:
                        bands_refs[dy - 1][dz, top : top + half, :] = band

    gather(0)
    for dy in range(len(lhs_refs)):
        if dy + 1 < len(lhs_refs):
            gather(dy + 1)
        cut(dy, correlate(dy))


def sine_cosine(angle):
    turns = jnp.round(angle * np.float32(2 / np.pi))
    rest = (angle - turns * np.float32(1.5703125)) - turns * np.float32(np.pi / 2 - 1.5703125)
    quarter = turns.astype(jnp.int32)
    sq = rest * rest
    sine = np.float32(1 / 362880) * sq + np.float32(-1 / 5040)
    sine = sine * sq + np.float32(1 / 120)
    sine = sine * sq + np.float32(-1 / 6)
    sine = sine * sq * rest + rest
    cosine = np.float32(1 / 40320) * sq + np.float32(-1 / 720)
    cosine = cosine * sq + np.float32(1 / 24)
    cosine = cosine * sq + np.float32(-1 / 2)
    cosine = cosine * sq + np.float32(1)
    odd = (quarter & 1) == 1
    sin_out = jnp.where(odd, cosine, sine)
    cos_out = jnp.where(odd, sine, cosine)
    sin_out = jnp.where((quarter & 2) == 2, -sin_out, sin_out)
    cos_out = jnp.where(((quarter + 1) & 2) == 2, -cos_out, cos_out)
    return sin_out, cos_out


def phase_kernel(extra_ref, first_table_ref, second_table_ref, bands_ref):
    count = first_table_ref.shape[1] // 2
    bands_ref[...] = extra_ref[2 * count :].astype(jnp.bfloat16).reshape(bands_ref.shape)
    phase_table(0, extra_ref, first_table_ref)
    phase_table(1, extra_ref, second_table_ref)


def turn_kernel(weights_ref, after_ref, first_ref, second_ref):
    band = first_ref.shape[2]
    lines = first_ref.shape[1]
    size = 16
    side = size * size
    row = lax.broadcasted_iota(jnp.int32, (side, side), 0)
    col = lax.broadcasted_iota(jnp.int32, (side, side), 1)
    order = jnp.where(col == (row % size) * size + row // size, 1.0, 0.0).astype(jnp.bfloat16)
    for block, out_ref in enumerate((first_ref, second_ref)):
        for part in range(2):

            def step(chunk, carry, block=block, part=part, out_ref=out_ref):
                first = pl.multiple_of(chunk * size, size)
                for pair in range(lines // (2 * size)):
                    tops = [(2 * pair + one) * size for one in range(2)]
                    block_rows = jnp.concatenate(
                        [
                            weights_ref[
                                pl.ds((block * 2 + part) * band + first, size), top : top + size, :
                            ].reshape(side, LANES)
                            for top in tops
                        ],
                        1,
                    )
                    moved = jnp.dot(order, block_rows, preferred_element_type=jnp.float32).astype(
                        jnp.bfloat16
                    )
                    for one, top in enumerate(tops):
                        out_ref[part, top : top + size, pl.ds(first, size), :] = moved[
                            :, one * LANES : (one + 1) * LANES
                        ].reshape(size, size, LANES)
                return carry

            lax.fori_loop(0, band // size, step, 0, unroll=True)


def phase_table(block, rate_ref, table_ref):
    count = table_ref.shape[1] // 2
    columns = table_ref.shape[0] * table_ref.shape[2]
    lane = lax.broadcasted_iota(jnp.int32, (32, LANES), 1).astype(jnp.float32)
    place = (lane + 0.5) * np.float32(1 / columns) - 0.5
    for group in range(count // 32):
        span = slice(group * 32, group * 32 + 32)
        rate = rate_ref[block * count + group * 32 : block * count + group * 32 + 32, :]
        sine, cosine = sine_cosine(rate * place)
        step_sine, step_cosine = sine_cosine(rate * np.float32(LANES / columns))
        for chunk in range(columns // LANES):
            if chunk > 0:
                sine, cosine = (
                    sine * step_cosine + cosine * step_sine,
                    cosine * step_cosine - sine * step_sine,
                )
            lanes = slice(chunk % 2 * LANES, (chunk % 2 + 1) * LANES)
            table_ref[chunk // 2, span, lanes] = cosine.astype(jnp.bfloat16)
            table_ref[chunk // 2, count + group * 32 : count + group * 32 + 32, lanes] = (
                sine.astype(jnp.bfloat16)
            )


def relay_kernel(after_ref, *refs):
    near = refs[0].shape[0]
    far = len(refs) - near + 1
    for dz in range(1, near):
        for dy in range(far):
            refs[far + dz - 1][dy] = refs[dy][dz]


def weighted_sum(side, table_refs, weights_refs, image_ref, left_ref, focused_refs):
    blocks = len(table_refs)
    places, lines, _ = image_ref.shape
    image_rows = lines // 2
    pairs = places // 2
    band = weights_refs[0].shape[2]

    def focus(pair):
        for block in range(blocks):
            focused_refs[pair % 2 * blocks + block][...] = jnp.dot(
                left_ref[block], table_refs[block][side * pairs + pair], preferred_element_type=jnp.float32
            )

    focus(0)
    for pair in range(pairs):
        if pair + 1 < pairs:
            focus(pair + 1)
        for place in range(2):
            lanes = slice(place * LANES, (place + 1) * LANES)
            real = [jnp.zeros((8, LANES), jnp.float32)] * image_rows
            imag = [jnp.zeros((8, LANES), jnp.float32)] * image_rows
            for block in range(blocks):
                focused_ref = focused_refs[pair % 2 * blocks + block]
                for k in range(0, band, 16):
                    focus_real = focused_ref[k : k + 16, lanes]
                    focus_imag = focused_ref[band + k : band + k + 16, lanes]
                    for row in range(image_rows):
                        line = (side * places + 2 * pair + place) * image_rows + row
                        weight_real = weights_refs[block][0, line, k : k + 16, :].astype(jnp.float32)
                        weight_imag = weights_refs[block][1, line, k : k + 16, :].astype(jnp.float32)
                        for first in (0, 8):
                            part = slice(first, first + 8)
                            wr, wi = weight_real[part], weight_imag[part]
                            fr, fi = focus_real[part], focus_imag[part]
                            real[row] = real[row] + (wr * fr - wi * fi)
                            imag[row] = imag[row] + (wr * fi + wi * fr)
            image_ref[2 * pair + place] = jnp.concatenate(
                [jnp.sum(one, 0, keepdims=True) for one in real + imag], 0
            )


def far_image_kernel(
    me_ref, sub_ref, first_table_ref, second_table_ref, first_weights_ref, second_weights_ref, *rest
):
    *sources_refs, image_ref, left_ref, bands_ref, one_ref, two_ref, three_ref, four_ref = rest
    sources, band_rows, band = bands_ref.shape
    far_count = len(sources_refs) // 2 + 1
    near_refs, far_refs = sources_refs[:far_count], sources_refs[far_count:]
    near = sources // far_count
    blocks = left_ref.shape[0]
    rows = band_rows // blocks
    half = rows // 2
    count = sources * half
    for dy in range(far_count):
        bands_ref[me_ref[0] ^ (dy * near)] = near_refs[dy][0]
        for dz in range(1, near):
            bands_ref[me_ref[0] ^ (dy * near + dz)] = far_refs[dz - 1][dy]
    for block in range(blocks):
        real = bands_ref[:, block * rows : block * rows + half, :].reshape(count, band)
        imag = bands_ref[:, block * rows + half : (block + 1) * rows, :].reshape(count, band)
        top = jnp.concatenate([real, imag], 1)
        bottom = jnp.concatenate([-imag, real], 1)
        left_ref[block] = jnp.concatenate([top, bottom], 0).T
    weighted_sum(
        1 - (sub_ref[0] >> 3),
        (first_table_ref, second_table_ref),
        (first_weights_ref, second_weights_ref),
        image_ref,
        left_ref,
        (one_ref, two_ref, three_ref, four_ref),
    )


def near_image_kernel(
    sub_ref, first_table_ref, second_table_ref, first_weights_ref, second_weights_ref, left_ref, after_ref,
    image_ref, one_ref, two_ref, three_ref, four_ref,
):
    weighted_sum(
        sub_ref[0] >> 3,
        (first_table_ref, second_table_ref),
        (first_weights_ref, second_weights_ref),
        image_ref,
        left_ref,
        (one_ref, two_ref, three_ref, four_ref),
    )


def params(mib):
    return pltpu.CompilerParams(vmem_limit_bytes=mib * 1024 * 1024)


def vmem():
    return pl.BlockSpec(memory_space=pltpu.VMEM)


def call(kernel, name, mib, out_shape, in_specs, scratch=(), flops=0):
    multiple = isinstance(out_shape, list)
    return pl.pallas_call(
        kernel,
        out_shape=out_shape,
        in_specs=in_specs,
        out_specs=[vmem()] * len(out_shape) if multiple else vmem(),
        scratch_shapes=list(scratch),
        compiler_params=params(mib),
        cost_estimate=pl.CostEstimate(flops=flops, bytes_accessed=0, transcendentals=0),
        name=name,
    )


def partial_image(echoes, chirp_ref, band_starts, doppler_rates, slot_pulse, interp_weights):
    pulses, _, pulse_len = echoes.shape
    chirp_len = chirp_ref.shape[1]
    blocks, tiles = band_starts.shape
    _, _, band, image_rows, columns = interp_weights.shape
    count = slot_pulse.shape[2]
    lines = 2 * pulse_len // LANES
    span = chirp_len + 2 * LANES
    places = columns // LANES
    parts = places // 2
    near = 4
    far = tiles // near
    smem = pl.BlockSpec(memory_space=pltpu.SMEM)
    anywhere = pl.BlockSpec(memory_space=pl.ANY)
    shape = jax.ShapeDtypeStruct
    sub = lax.axis_index("sub").astype(jnp.int32).reshape(1)
    me = lax.axis_index("tile").astype(jnp.int32).reshape(1)

    samples = echoes.reshape(pulses, 2, pulse_len // LANES, LANES).transpose(0, 2, 1, 3)
    samples = samples.reshape(pulses, lines, LANES)
    weights = interp_weights.reshape(blocks, 2, band, image_rows, places, LANES)
    weights = weights.transpose(0, 1, 2, 4, 3, 5).reshape(
        blocks * 2 * band, places * image_rows, LANES
    )
    own = shape((near, 2 * pulses, band), jnp.bfloat16)
    extras = shape((blocks * count + near * 2 * pulses, LANES), jnp.float32)
    *bands, extra = call(
        compress_kernel,
        "compress",
        60,
        [own] * (far - 1) + [extras],
        [smem] * 3 + [anywhere] * 4,
        [
            pltpu.VMEM((2, chirp_len), jnp.bfloat16),
            pltpu.VMEM((1, blocks * count), jnp.float32),
            pltpu.VMEM((blocks, count), jnp.int32),
            pltpu.VMEM((pulses, lines, LANES), jnp.bfloat16),
            pltpu.VMEM((lines // 2 + span // LANES - 1, 2 * pulses, LANES), jnp.bfloat16),
            pltpu.VMEM((4 * LANES, span), jnp.bfloat16),
        ]
        + [pltpu.VMEM((near * 2 * pulses, span), jnp.bfloat16)] * far
        + [
            pltpu.SemaphoreType.DMA((4,)),
        ],
        flops=6 * 10**9,
    )(me, sub, band_starts, chirp_ref, doppler_rates, slot_pulse.reshape(blocks, count), samples)

    def swap(value, distance):
        return lax.ppermute(value, "tile", [(one, one ^ distance) for one in range(tiles)])

    table = shape((parts, 2 * count, 2 * LANES), jnp.bfloat16)
    turned = shape((2, places * image_rows, band, LANES), jnp.bfloat16)
    first_table, second_table, mine = call(phase_kernel, "phase", 12, [table, table, own], [vmem()], flops=4 * 10**9)(extra)
    bands = [mine] + [swap(bands[dy - 1], dy * near) for dy in range(1, far)]
    passed = call(
        relay_kernel,
        "relay",
        16,
        [shape((far, 2 * pulses, band), jnp.bfloat16)] * (near - 1),
        [anywhere] + [vmem()] * far,
    )(first_table, *bands)
    first_weights, second_weights = call(turn_kernel, "turn", 12, [turned, turned], [vmem(), anywhere], flops=4 * 10**9)(
        weights, passed[0]
    )
    passed = [swap(passed[dz - 1], dz) for dz in range(1, near)]
    sources = bands + passed
    half = shape((places // 2, 2 * image_rows, LANES), jnp.float32)
    focused = [pltpu.VMEM((2 * band, 2 * LANES), jnp.float32)] * (2 * blocks)
    far_image, left = call(
        far_image_kernel,
        "far_image",
        12,
        [half, shape((blocks, 2 * band, 2 * count), jnp.bfloat16)],
        [smem, smem] + [vmem()] * (4 + len(sources)),
        [pltpu.VMEM((tiles, 2 * pulses, band), jnp.bfloat16)] + focused,
        flops=3 * 10**9,
    )(me, sub, first_table, second_table, first_weights, second_weights, *sources)
    near_image = call(
        near_image_kernel, "near_image", 12, half, [smem] + [vmem()] * 5 + [anywhere], focused, flops=3 * 10**9
    )(sub, first_table, second_table, first_weights, second_weights, left, far_image)
    return sub, far_image, near_image


def shards(*args):
    _, far_image, near_image = partial_image(*args)
    size = 16
    half = size // 2
    came = lax.ppermute(far_image, "sub", [(one, one ^ half) for one in range(size)])
    groups = [list(range(half)), list(range(half, size))]
    pieces = lax.all_to_all(near_image + came, "sub", 0, 0, axis_index_groups=groups, tiled=True)
    return jnp.sum(pieces, 0).reshape(2, -1, LANES)


def solution(mesh):
    in_specs = (
        P(("sub", "tile"), None, None),
        P(),
        P("sub", None),
        P("sub", None),
        P("sub", None, None),
        P("sub", None, None, "tile", None),
    )
    out_specs = P(None, "tile", "sub")
    return jax.shard_map(shards, mesh=mesh, in_specs=in_specs, out_specs=out_specs, check_vma=False)
```

```python
import jax
import jax.numpy as jnp
import numpy as np
from jax import lax
from jax.experimental import pallas as pl
from jax.experimental.pallas import tpu as pltpu
from jax.sharding import PartitionSpec as P

LANES = 128


def compress_kernel(
    me_ref, sub_ref, starts_ref, chirp_hbm, rates_hbm, slots_hbm, echoes_ref, *rest
):
    (
        *bands_refs, extra_ref, chirp_ref, rates_ref, slots_ref, raw_ref, samples_ref, toeplitz_ref,
        lhs_a, lhs_b, lhs_c, lhs_d, sems,
    ) = rest
    fetches = [
        pltpu.make_async_copy(source, target, sems.at[index])
        for index, (source, target) in enumerate(
            (
                (chirp_hbm, chirp_ref),
                (rates_hbm, rates_ref),
                (slots_hbm, slots_ref),
                (echoes_ref, raw_ref),
            )
        )
    ]
    for fetch in fetches:
        fetch.start()
    span = toeplitz_ref.shape[1]
    blocks, tiles = starts_ref.shape
    near = tiles // (len(bands_refs) + 1)
    pulses, lines, _ = raw_ref.shape
    half = pulses // blocks
    rows = 2 * half
    chunks = span // LANES
    samples_ref[lines // 2 :] = jnp.zeros(
        (samples_ref.shape[0] - lines // 2, 2 * pulses, LANES), jnp.bfloat16
    )
    piece = 16
    side = half * piece
    row = lax.broadcasted_iota(jnp.int32, (side, side), 0)
    col = lax.broadcasted_iota(jnp.int32, (side, side), 1)
    order = jnp.where(col == (row & (half - 1)) * piece + (row >> 4), 1.0, 0.0).astype(jnp.bfloat16)
    for fetch in fetches[:3]:
        fetch.wait()
    chirp = chirp_ref[...].astype(jnp.float32)
    pad = jnp.zeros((1, span - chirp.shape[1]), jnp.float32)
    for part in range(2):
        line = jnp.concatenate([chirp[part : part + 1], pad], 1)
        shifted = pltpu.roll(
            jnp.broadcast_to(line, (LANES, span)), 0, 1, stride=1, stride_axis=0
        ).astype(jnp.bfloat16)
        toeplitz_ref[part * LANES : (part + 1) * LANES, :] = shifted
    count = slots_ref.shape[1]
    row = lax.broadcasted_iota(jnp.int32, (count, count), 0)
    col = lax.broadcasted_iota(jnp.int32, (count, count), 1)
    for block in range(blocks):
        slots = slots_ref[block : block + 1, :].astype(jnp.float32)
        slot = jnp.sum(jnp.where(row == col, slots, 0.0), 1, keepdims=True)
        rates = rates_ref[:, block * count : (block + 1) * count]
        rate = jnp.sum(jnp.where(slot == col.astype(jnp.float32), rates, 0.0), 1, keepdims=True)
        extra_ref[block * count : (block + 1) * count, :] = jnp.broadcast_to(rate, (count, LANES))
    fetches[3].wait()
    for group in range(lines // piece):
        block_rows = jnp.concatenate(
            [
                raw_ref[block * half : (block + 1) * half, group * piece : (group + 1) * piece, :].reshape(
                    side, LANES
                )
                for block in range(blocks)
            ],
            1,
        )
        moved = jnp.dot(order, block_rows, preferred_element_type=jnp.float32).astype(jnp.bfloat16)
        for block in range(blocks):
            samples_ref[
                group * piece // 2 : (group + 1) * piece // 2, block * rows : (block + 1) * rows, :
            ] = moved[:, block * LANES : (block + 1) * LANES].reshape(piece // 2, rows, LANES)
    lane = lax.broadcasted_iota(jnp.int32, (rows, LANES), 1)
    lhs_refs = (lhs_a, lhs_b, lhs_c, lhs_d)

    def gather(dy):
        for dz in range(near):
            for block in range(blocks):
                start = starts_ref[block, me_ref[0] ^ (dy * near + dz)]
                first = start >> 7
                shift = start & (LANES - 1)
                turn = (LANES - shift) & (LANES - 1)
                keep = lane < LANES - shift
                place = (dz * blocks + block) * rows

                def rolled(chunk):
                    line = samples_ref[first + chunk, block * rows : (block + 1) * rows, :]
                    return pltpu.roll(line, turn, 1)

                low = rolled(0)
                for chunk in range(chunks):
                    high = rolled(chunk + 1)
                    lhs_refs[dy][place : place + rows, chunk * LANES : (chunk + 1) * LANES] = jnp.where(
                        keep, low, high
                    )
                    low = high

    def correlate(dy):
        return lax.dot_general(
            lhs_refs[dy][...],
            toeplitz_ref[...],
            (((1,), (1,)), ((), ())),
            preferred_element_type=jnp.float32,
        )

    def cut(dy, product):
        for dz in range(near):
            for block in range(blocks):
                place = (dz * blocks + block) * rows
                real = product[place : place + half]
                imag = product[place + half : place + rows]
                for part, band in enumerate(
                    (real[:, :LANES] + imag[:, LANES:], imag[:, :LANES] - real[:, LANES:])
                ):
                    band = band.astype(jnp.bfloat16)
                    top = block * rows + part * half
                    if dy == 0:
                        top += blocks * count + dz * 2 * pulses
                        extra_ref[top : top + half, :] = band.astype(jnp.float32)
                    else:
                        bands_refs[dy - 1][dz, top : top + half, :] = band

    gather(0)
    for dy in range(len(lhs_refs)):
        if dy + 1 < len(lhs_refs):
            gather(dy + 1)
        cut(dy, correlate(dy))


def sine_cosine(angle):
    turns = jnp.round(angle * np.float32(2 / np.pi))
    rest = (angle - turns * np.float32(1.5703125)) - turns * np.float32(np.pi / 2 - 1.5703125)
    quarter = turns.astype(jnp.int32)
    sq = rest * rest
    sine = np.float32(1 / 362880) * sq + np.float32(-1 / 5040)
    sine = sine * sq + np.float32(1 / 120)
    sine = sine * sq + np.float32(-1 / 6)
    sine = sine * sq * rest + rest
    cosine = np.float32(1 / 40320) * sq + np.float32(-1 / 720)
    cosine = cosine * sq + np.float32(1 / 24)
    cosine = cosine * sq + np.float32(-1 / 2)
    cosine = cosine * sq + np.float32(1)
    odd = (quarter & 1) == 1
    sin_out = jnp.where(odd, cosine, sine)
    cos_out = jnp.where(odd, sine, cosine)
    sin_out = jnp.where((quarter & 2) == 2, -sin_out, sin_out)
    cos_out = jnp.where(((quarter + 1) & 2) == 2, -cos_out, cos_out)
    return sin_out, cos_out


def phase_kernel(extra_ref, first_table_ref, second_table_ref, bands_ref):
    count = first_table_ref.shape[1] // 2
    bands_ref[...] = extra_ref[2 * count :].astype(jnp.bfloat16).reshape(bands_ref.shape)
    phase_table(0, extra_ref, first_table_ref)
    phase_table(1, extra_ref, second_table_ref)


def turn_kernel(weights_ref, after_ref, first_ref, second_ref):
    band = first_ref.shape[2]
    lines = first_ref.shape[1]
    size = 16
    side = size * size
    row = lax.broadcasted_iota(jnp.int32, (side, side), 0)
    col = lax.broadcasted_iota(jnp.int32, (side, side), 1)
    order = jnp.where(col == (row & (size - 1)) * size + (row >> 4), 1.0, 0.0).astype(jnp.bfloat16)
    for block, out_ref in enumerate((first_ref, second_ref)):
        for part in range(2):

            def step(chunk, carry, block=block, part=part, out_ref=out_ref):
                first = pl.multiple_of(chunk * size, size)
                for pair in range(lines // (2 * size)):
                    tops = [(2 * pair + one) * size for one in range(2)]
                    block_rows = jnp.concatenate(
                        [
                            weights_ref[
                                pl.ds((block * 2 + part) * band + first, size), top : top + size, :
                            ].reshape(side, LANES)
                            for top in tops
                        ],
                        1,
                    )
                    moved = jnp.dot(order, block_rows, preferred_element_type=jnp.float32).astype(
                        jnp.bfloat16
                    )
                    for one, top in enumerate(tops):
                        out_ref[part, top : top + size, pl.ds(first, size), :] = moved[
                            :, one * LANES : (one + 1) * LANES
                        ].reshape(size, size, LANES)
                return carry

            lax.fori_loop(0, band // size, step, 0, unroll=True)


def phase_table(block, rate_ref, table_ref):
    count = table_ref.shape[1] // 2
    columns = table_ref.shape[0] * table_ref.shape[2]
    lane = lax.broadcasted_iota(jnp.int32, (32, LANES), 1).astype(jnp.float32)
    place = (lane + 0.5) * np.float32(1 / columns) - 0.5
    for group in range(count // 32):
        span = slice(group * 32, group * 32 + 32)
        rate = rate_ref[block * count + group * 32 : block * count + group * 32 + 32, :]
        sine, cosine = sine_cosine(rate * place)
        step_sine, step_cosine = sine_cosine(rate * np.float32(LANES / columns))
        for chunk in range(columns // LANES):
            if chunk > 0:
                sine, cosine = (
                    sine * step_cosine + cosine * step_sine,
                    cosine * step_cosine - sine * step_sine,
                )
            lanes = slice(chunk % 2 * LANES, (chunk % 2 + 1) * LANES)
            table_ref[chunk // 2, span, lanes] = cosine.astype(jnp.bfloat16)
            table_ref[chunk // 2, count + group * 32 : count + group * 32 + 32, lanes] = (
                sine.astype(jnp.bfloat16)
            )


def relay_kernel(after_ref, *refs):
    near = refs[0].shape[0]
    far = len(refs) - near + 1
    for dz in range(1, near):
        for dy in range(far):
            refs[far + dz - 1][dy] = refs[dy][dz]


def weighted_sum(side, table_refs, weights_refs, image_ref, left_ref, focused_refs):
    blocks = len(table_refs)
    places, lines, _ = image_ref.shape
    image_rows = lines // 2
    pairs = places // 2
    band = weights_refs[0].shape[2]

    def focus(pair):
        for block in range(blocks):
            focused_refs[pair % 2 * blocks + block][...] = jnp.dot(
                left_ref[block], table_refs[block][side * pairs + pair], preferred_element_type=jnp.float32
            )

    focus(0)
    for pair in range(pairs):
        if pair + 1 < pairs:
            focus(pair + 1)
        for place in range(2):
            lanes = slice(place * LANES, (place + 1) * LANES)
            real = [jnp.zeros((8, LANES), jnp.float32)] * image_rows
            imag = [jnp.zeros((8, LANES), jnp.float32)] * image_rows
            for block in range(blocks):
                focused_ref = focused_refs[pair % 2 * blocks + block]
                for k in range(0, band, 16):
                    focus_real = focused_ref[k : k + 16, lanes]
                    focus_imag = focused_ref[band + k : band + k + 16, lanes]
                    for row in range(image_rows):
                        line = (side * places + 2 * pair + place) * image_rows + row
                        weight_real = weights_refs[block][0, line, k : k + 16, :].astype(jnp.float32)
                        weight_imag = weights_refs[block][1, line, k : k + 16, :].astype(jnp.float32)
                        for first in (0, 8):
                            part = slice(first, first + 8)
                            wr, wi = weight_real[part], weight_imag[part]
                            fr, fi = focus_real[part], focus_imag[part]
                            real[row] = real[row] + (wr * fr - wi * fi)
                            imag[row] = imag[row] + (wr * fi + wi * fr)
            image_ref[2 * pair + place] = jnp.concatenate(
                [jnp.sum(one, 0, keepdims=True) for one in real + imag], 0
            )


def far_image_kernel(
    me_ref, sub_ref, first_table_ref, second_table_ref, first_weights_ref, second_weights_ref, *rest
):
    *sources_refs, image_ref, left_ref, bands_ref, one_ref, two_ref, three_ref, four_ref = rest
    sources, band_rows, band = bands_ref.shape
    far_count = len(sources_refs) // 2 + 1
    near_refs, far_refs = sources_refs[:far_count], sources_refs[far_count:]
    near = sources // far_count
    blocks = left_ref.shape[0]
    rows = band_rows // blocks
    half = rows // 2
    count = sources * half
    for dy in range(far_count):
        bands_ref[me_ref[0] ^ (dy * near)] = near_refs[dy][0]
        for dz in range(1, near):
            bands_ref[me_ref[0] ^ (dy * near + dz)] = far_refs[dz - 1][dy]
    for block in range(blocks):
        real = bands_ref[:, block * rows : block * rows + half, :].reshape(count, band)
        imag = bands_ref[:, block * rows + half : (block + 1) * rows, :].reshape(count, band)
        top = jnp.concatenate([real, imag], 1)
        bottom = jnp.concatenate([-imag, real], 1)
        left_ref[block] = jnp.concatenate([top, bottom], 0).T
    weighted_sum(
        1 - (sub_ref[0] >> 3),
        (first_table_ref, second_table_ref),
        (first_weights_ref, second_weights_ref),
        image_ref,
        left_ref,
        (one_ref, two_ref, three_ref, four_ref),
    )


def near_image_kernel(
    sub_ref, first_table_ref, second_table_ref, first_weights_ref, second_weights_ref, left_ref, after_ref,
    image_ref, one_ref, two_ref, three_ref, four_ref,
):
    weighted_sum(
        sub_ref[0] >> 3,
        (first_table_ref, second_table_ref),
        (first_weights_ref, second_weights_ref),
        image_ref,
        left_ref,
        (one_ref, two_ref, three_ref, four_ref),
    )


def params(mib):
    return pltpu.CompilerParams(vmem_limit_bytes=mib * 1024 * 1024)


def vmem():
    return pl.BlockSpec(memory_space=pltpu.VMEM)


def call(kernel, name, mib, out_shape, in_specs, scratch=(), flops=0):
    multiple = isinstance(out_shape, list)
    return pl.pallas_call(
        kernel,
        out_shape=out_shape,
        in_specs=in_specs,
        out_specs=[vmem()] * len(out_shape) if multiple else vmem(),
        scratch_shapes=list(scratch),
        compiler_params=params(mib),
        cost_estimate=pl.CostEstimate(flops=flops, bytes_accessed=0, transcendentals=0),
        name=name,
    )


def partial_image(echoes, chirp_ref, band_starts, doppler_rates, slot_pulse, interp_weights):
    pulses, _, pulse_len = echoes.shape
    chirp_len = chirp_ref.shape[1]
    blocks, tiles = band_starts.shape
    _, _, band, image_rows, columns = interp_weights.shape
    count = slot_pulse.shape[2]
    lines = 2 * pulse_len // LANES
    span = chirp_len + LANES
    places = columns // LANES
    parts = places // 2
    near = 4
    far = tiles // near
    smem = pl.BlockSpec(memory_space=pltpu.SMEM)
    anywhere = pl.BlockSpec(memory_space=pl.ANY)
    shape = jax.ShapeDtypeStruct
    sub = lax.axis_index("sub").astype(jnp.int32).reshape(1)
    me = lax.axis_index("tile").astype(jnp.int32).reshape(1)

    samples = echoes.reshape(pulses, 2, pulse_len // LANES, LANES).transpose(0, 2, 1, 3)
    samples = samples.reshape(pulses, lines, LANES)
    weights = interp_weights.reshape(blocks, 2, band, image_rows, places, LANES)
    weights = weights.transpose(0, 1, 2, 4, 3, 5).reshape(
        blocks * 2 * band, places * image_rows, LANES
    )
    own = shape((near, 2 * pulses, band), jnp.bfloat16)
    extras = shape((blocks * count + near * 2 * pulses, LANES), jnp.float32)
    *bands, extra = call(
        compress_kernel,
        "compress",
        60,
        [own] * (far - 1) + [extras],
        [smem] * 3 + [anywhere] * 4,
        [
            pltpu.VMEM((2, chirp_len), jnp.bfloat16),
            pltpu.VMEM((1, blocks * count), jnp.float32),
            pltpu.VMEM((blocks, count), jnp.int32),
            pltpu.VMEM((pulses, lines, LANES), jnp.bfloat16),
            pltpu.VMEM((lines // 2 + span // LANES, 2 * pulses, LANES), jnp.bfloat16),
            pltpu.VMEM((2 * LANES, span), jnp.bfloat16),
        ]
        + [pltpu.VMEM((near * 2 * pulses, span), jnp.bfloat16)] * far
        + [
            pltpu.SemaphoreType.DMA((4,)),
        ],
        flops=6 * 10**9,
    )(me, sub, band_starts, chirp_ref, doppler_rates, slot_pulse.reshape(blocks, count), samples)

    def swap(value, distance):
        return lax.ppermute(value, "tile", [(one, one ^ distance) for one in range(tiles)])

    table = shape((parts, 2 * count, 2 * LANES), jnp.bfloat16)
    turned = shape((2, places * image_rows, band, LANES), jnp.bfloat16)
    first_table, second_table, mine = call(phase_kernel, "phase", 12, [table, table, own], [vmem()], flops=4 * 10**9)(extra)
    bands = [mine] + [swap(bands[dy - 1], dy * near) for dy in range(1, far)]
    passed = call(
        relay_kernel,
        "relay",
        16,
        [shape((far, 2 * pulses, band), jnp.bfloat16)] * (near - 1),
        [anywhere] + [vmem()] * far,
    )(first_table, *bands)
    first_weights, second_weights = call(turn_kernel, "turn", 12, [turned, turned], [vmem(), anywhere], flops=4 * 10**9)(
        weights, passed[0]
    )
    passed = [swap(passed[dz - 1], dz) for dz in range(1, near)]
    sources = bands + passed
    half = shape((places // 2, 2 * image_rows, LANES), jnp.float32)
    focused = [pltpu.VMEM((2 * band, 2 * LANES), jnp.float32)] * (2 * blocks)
    far_image, left = call(
        far_image_kernel,
        "far_image",
        12,
        [half, shape((blocks, 2 * band, 2 * count), jnp.bfloat16)],
        [smem, smem] + [vmem()] * (4 + len(sources)),
        [pltpu.VMEM((tiles, 2 * pulses, band), jnp.bfloat16)] + focused,
        flops=3 * 10**9,
    )(me, sub, first_table, second_table, first_weights, second_weights, *sources)
    near_image = call(
        near_image_kernel, "near_image", 12, half, [smem] + [vmem()] * 5 + [anywhere], focused, flops=3 * 10**9
    )(sub, first_table, second_table, first_weights, second_weights, left, far_image)
    return sub, far_image, near_image


def shards(*args):
    _, far_image, near_image = partial_image(*args)
    size = 16
    half = size // 2
    came = lax.ppermute(far_image, "sub", [(one, one ^ half) for one in range(size)])
    groups = [list(range(half)), list(range(half, size))]
    pieces = lax.all_to_all(near_image + came, "sub", 0, 0, axis_index_groups=groups, tiled=True)
    return jnp.sum(pieces, 0).reshape(2, -1, LANES)


def solution(mesh):
    in_specs = (
        P(("sub", "tile"), None, None),
        P(),
        P("sub", None),
        P("sub", None),
        P("sub", None, None),
        P("sub", None, None, "tile", None),
    )
    out_specs = P(None, "tile", "sub")
    return jax.shard_map(shards, mesh=mesh, in_specs=in_specs, out_specs=out_specs, check_vma=False)
```

```python
import jax
import jax.numpy as jnp
import numpy as np
from jax import lax
from jax.experimental import pallas as pl
from jax.experimental.pallas import tpu as pltpu
from jax.sharding import PartitionSpec as P

LANES = 128


def compress_kernel(
    me_ref, sub_ref, starts_ref, chirp_hbm, rates_hbm, slots_hbm, echoes_ref, *rest
):
    (
        *bands_refs, extra_ref, chirp_ref, rates_ref, slots_ref, raw_ref, samples_ref, toeplitz_ref,
        lhs_a, lhs_b, lhs_c, lhs_d, sems,
    ) = rest
    fetches = [
        pltpu.make_async_copy(source, target, sems.at[index])
        for index, (source, target) in enumerate(
            (
                (chirp_hbm, chirp_ref),
                (rates_hbm, rates_ref),
                (slots_hbm, slots_ref),
                (echoes_ref, raw_ref),
            )
        )
    ]
    for fetch in fetches:
        fetch.start()
    span = toeplitz_ref.shape[1]
    blocks, tiles = starts_ref.shape
    near = tiles // (len(bands_refs) + 1)
    pulses, lines, _ = raw_ref.shape
    half = pulses // blocks
    rows = 2 * half
    chunks = span // LANES
    samples_ref[lines // 2 :] = jnp.zeros(
        (samples_ref.shape[0] - lines // 2, 2 * pulses, LANES), jnp.bfloat16
    )
    piece = 16
    side = half * piece
    row = lax.broadcasted_iota(jnp.int32, (side, side), 0)
    col = lax.broadcasted_iota(jnp.int32, (side, side), 1)
    order = jnp.where(col == (row & (half - 1)) * piece + (row >> 4), 1.0, 0.0).astype(jnp.bfloat16)
    for fetch in fetches[:3]:
        fetch.wait()
    chirp = chirp_ref[...].astype(jnp.float32)
    pad = jnp.zeros((1, span - chirp.shape[1]), jnp.float32)
    for part in range(2):
        line = jnp.concatenate([chirp[part : part + 1], pad], 1)
        shifted = pltpu.roll(
            jnp.broadcast_to(line, (LANES, span)), 0, 1, stride=1, stride_axis=0
        ).astype(jnp.bfloat16)
        toeplitz_ref[part * LANES : (part + 1) * LANES, :] = shifted
    count = slots_ref.shape[1]
    row = lax.broadcasted_iota(jnp.int32, (count, count), 0)
    col = lax.broadcasted_iota(jnp.int32, (count, count), 1)
    for block in range(blocks):
        slots = slots_ref[block : block + 1, :].astype(jnp.float32)
        slot = jnp.sum(jnp.where(row == col, slots, 0.0), 1, keepdims=True)
        rates = rates_ref[:, block * count : (block + 1) * count]
        rate = jnp.sum(jnp.where(slot == col.astype(jnp.float32), rates, 0.0), 1, keepdims=True)
        extra_ref[block * count : (block + 1) * count, :] = jnp.broadcast_to(rate, (count, LANES))
    fetches[3].wait()
    for group in range(lines // piece):
        block_rows = jnp.concatenate(
            [
                raw_ref[block * half : (block + 1) * half, group * piece : (group + 1) * piece, :].reshape(
                    side, LANES
                )
                for block in range(blocks)
            ],
            1,
        )
        moved = jnp.dot(order, block_rows, preferred_element_type=jnp.float32).astype(jnp.bfloat16)
        for block in range(blocks):
            samples_ref[
                group * piece // 2 : (group + 1) * piece // 2, block * rows : (block + 1) * rows, :
            ] = moved[:, block * LANES : (block + 1) * LANES].reshape(piece // 2, rows, LANES)
    lane = lax.broadcasted_iota(jnp.int32, (rows, LANES), 1)
    lhs_refs = (lhs_a, lhs_b, lhs_c, lhs_d)

    def gather(dy):
        for dz in range(near):
            for block in range(blocks):
                start = starts_ref[block, me_ref[0] ^ distance_of(sub_ref[0], dy, dz, near)]
                first = start >> 7
                shift = start & (LANES - 1)
                turn = (LANES - shift) & (LANES - 1)
                keep = lane < LANES - shift
                place = (dz * blocks + block) * rows

                def rolled(chunk):
                    line = samples_ref[first + chunk, block * rows : (block + 1) * rows, :]
                    return pltpu.roll(line, turn, 1)

                low = rolled(0)
                for chunk in range(chunks):
                    high = rolled(chunk + 1)
                    lhs_refs[dy][place : place + rows, chunk * LANES : (chunk + 1) * LANES] = jnp.where(
                        keep, low, high
                    )
                    low = high

    def correlate(dy):
        return lax.dot_general(
            lhs_refs[dy][...],
            toeplitz_ref[...],
            (((1,), (1,)), ((), ())),
            preferred_element_type=jnp.float32,
        )

    def cut(dy, product):
        for dz in range(near):
            for block in range(blocks):
                place = (dz * blocks + block) * rows
                real = product[place : place + half]
                imag = product[place + half : place + rows]
                for part, band in enumerate(
                    (real[:, :LANES] + imag[:, LANES:], imag[:, :LANES] - real[:, LANES:])
                ):
                    band = band.astype(jnp.bfloat16)
                    top = block * rows + part * half
                    if dy == 0:
                        top += blocks * count + dz * 2 * pulses
                        extra_ref[top : top + half, :] = band.astype(jnp.float32)
                    else:
                        bands_refs[dy - 1][dz, top : top + half, :] = band

    gather(0)
    for dy in range(len(lhs_refs)):
        if dy + 1 < len(lhs_refs):
            gather(dy + 1)
        cut(dy, correlate(dy))


def distance_of(sub, first, second, near):
    return jnp.where((sub & 1) == 1, first * near + second, second * near + first)


def sine_cosine(angle):
    turns = jnp.round(angle * np.float32(2 / np.pi))
    rest = (angle - turns * np.float32(1.5703125)) - turns * np.float32(np.pi / 2 - 1.5703125)
    quarter = turns.astype(jnp.int32)
    sq = rest * rest
    sine = np.float32(1 / 362880) * sq + np.float32(-1 / 5040)
    sine = sine * sq + np.float32(1 / 120)
    sine = sine * sq + np.float32(-1 / 6)
    sine = sine * sq * rest + rest
    cosine = np.float32(1 / 40320) * sq + np.float32(-1 / 720)
    cosine = cosine * sq + np.float32(1 / 24)
    cosine = cosine * sq + np.float32(-1 / 2)
    cosine = cosine * sq + np.float32(1)
    odd = (quarter & 1) == 1
    sin_out = jnp.where(odd, cosine, sine)
    cos_out = jnp.where(odd, sine, cosine)
    sin_out = jnp.where((quarter & 2) == 2, -sin_out, sin_out)
    cos_out = jnp.where(((quarter + 1) & 2) == 2, -cos_out, cos_out)
    return sin_out, cos_out


def phase_kernel(extra_ref, first_table_ref, second_table_ref, bands_ref):
    count = first_table_ref.shape[1] // 2
    bands_ref[...] = extra_ref[2 * count :].astype(jnp.bfloat16).reshape(bands_ref.shape)
    phase_table(0, extra_ref, first_table_ref)
    phase_table(1, extra_ref, second_table_ref)


def turn_kernel(weights_ref, after_ref, first_ref, second_ref):
    band = first_ref.shape[2]
    lines = first_ref.shape[1]
    size = 16
    side = size * size
    row = lax.broadcasted_iota(jnp.int32, (side, side), 0)
    col = lax.broadcasted_iota(jnp.int32, (side, side), 1)
    order = jnp.where(col == (row & (size - 1)) * size + (row >> 4), 1.0, 0.0).astype(jnp.bfloat16)
    for block, out_ref in enumerate((first_ref, second_ref)):
        for part in range(2):

            def step(chunk, carry, block=block, part=part, out_ref=out_ref):
                first = pl.multiple_of(chunk * size, size)
                for pair in range(lines // (2 * size)):
                    tops = [(2 * pair + one) * size for one in range(2)]
                    block_rows = jnp.concatenate(
                        [
                            weights_ref[
                                pl.ds((block * 2 + part) * band + first, size), top : top + size, :
                            ].reshape(side, LANES)
                            for top in tops
                        ],
                        1,
                    )
                    moved = jnp.dot(order, block_rows, preferred_element_type=jnp.float32).astype(
                        jnp.bfloat16
                    )
                    for one, top in enumerate(tops):
                        out_ref[part, top : top + size, pl.ds(first, size), :] = moved[
                            :, one * LANES : (one + 1) * LANES
                        ].reshape(size, size, LANES)
                return carry

            lax.fori_loop(0, band // size, step, 0, unroll=True)


def phase_table(block, rate_ref, table_ref):
    count = table_ref.shape[1] // 2
    columns = table_ref.shape[0] * table_ref.shape[2]
    lane = lax.broadcasted_iota(jnp.int32, (32, LANES), 1).astype(jnp.float32)
    place = (lane + 0.5) * np.float32(1 / columns) - 0.5
    for group in range(count // 32):
        span = slice(group * 32, group * 32 + 32)
        rate = rate_ref[block * count + group * 32 : block * count + group * 32 + 32, :]
        sine, cosine = sine_cosine(rate * place)
        step_sine, step_cosine = sine_cosine(rate * np.float32(LANES / columns))
        for chunk in range(columns // LANES):
            if chunk > 0:
                sine, cosine = (
                    sine * step_cosine + cosine * step_sine,
                    cosine * step_cosine - sine * step_sine,
                )
            lanes = slice(chunk % 2 * LANES, (chunk % 2 + 1) * LANES)
            table_ref[chunk // 2, span, lanes] = cosine.astype(jnp.bfloat16)
            table_ref[chunk // 2, count + group * 32 : count + group * 32 + 32, lanes] = (
                sine.astype(jnp.bfloat16)
            )


def relay_kernel(after_ref, *refs):
    near = refs[0].shape[0]
    far = len(refs) - near + 1
    for dz in range(1, near):
        for dy in range(far):
            refs[far + dz - 1][dy] = refs[dy][dz]


def weighted_sum(side, table_refs, weights_refs, image_ref, left_ref, focused_refs):
    blocks = len(table_refs)
    places, lines, _ = image_ref.shape
    image_rows = lines // 2
    pairs = places // 2
    band = weights_refs[0].shape[2]

    def focus(pair):
        for block in range(blocks):
            focused_refs[pair % 2 * blocks + block][...] = jnp.dot(
                left_ref[block], table_refs[block][side * pairs + pair], preferred_element_type=jnp.float32
            )

    focus(0)
    for pair in range(pairs):
        if pair + 1 < pairs:
            focus(pair + 1)
        for place in range(2):
            lanes = slice(place * LANES, (place + 1) * LANES)
            real = [jnp.zeros((8, LANES), jnp.float32)] * image_rows
            imag = [jnp.zeros((8, LANES), jnp.float32)] * image_rows
            for block in range(blocks):
                focused_ref = focused_refs[pair % 2 * blocks + block]
                for k in range(0, band, 16):
                    focus_real = focused_ref[k : k + 16, lanes]
                    focus_imag = focused_ref[band + k : band + k + 16, lanes]
                    for row in range(image_rows):
                        line = (side * places + 2 * pair + place) * image_rows + row
                        weight_real = weights_refs[block][0, line, k : k + 16, :].astype(jnp.float32)
                        weight_imag = weights_refs[block][1, line, k : k + 16, :].astype(jnp.float32)
                        for first in (0, 8):
                            part = slice(first, first + 8)
                            wr, wi = weight_real[part], weight_imag[part]
                            fr, fi = focus_real[part], focus_imag[part]
                            real[row] = real[row] + (wr * fr - wi * fi)
                            imag[row] = imag[row] + (wr * fi + wi * fr)
            image_ref[2 * pair + place] = jnp.concatenate(
                [jnp.sum(one, 0, keepdims=True) for one in real + imag], 0
            )


def far_image_kernel(
    me_ref, sub_ref, first_table_ref, second_table_ref, first_weights_ref, second_weights_ref, *rest
):
    *sources_refs, image_ref, left_ref, bands_ref, one_ref, two_ref, three_ref, four_ref = rest
    sources, band_rows, band = bands_ref.shape
    far_count = len(sources_refs) // 2 + 1
    near_refs, far_refs = sources_refs[:far_count], sources_refs[far_count:]
    near = sources // far_count
    blocks = left_ref.shape[0]
    rows = band_rows // blocks
    half = rows // 2
    count = sources * half
    for dy in range(far_count):
        bands_ref[me_ref[0] ^ distance_of(sub_ref[0], dy, 0, near)] = near_refs[dy][0]
        for dz in range(1, near):
            bands_ref[me_ref[0] ^ distance_of(sub_ref[0], dy, dz, near)] = far_refs[dz - 1][dy]
    for block in range(blocks):
        real = bands_ref[:, block * rows : block * rows + half, :].reshape(count, band)
        imag = bands_ref[:, block * rows + half : (block + 1) * rows, :].reshape(count, band)
        top = jnp.concatenate([real, imag], 1)
        bottom = jnp.concatenate([-imag, real], 1)
        left_ref[block] = jnp.concatenate([top, bottom], 0).T
    weighted_sum(
        1 - (sub_ref[0] >> 3),
        (first_table_ref, second_table_ref),
        (first_weights_ref, second_weights_ref),
        image_ref,
        left_ref,
        (one_ref, two_ref, three_ref, four_ref),
    )


def near_image_kernel(
    sub_ref, first_table_ref, second_table_ref, first_weights_ref, second_weights_ref, left_ref, after_ref,
    image_ref, one_ref, two_ref, three_ref, four_ref,
):
    weighted_sum(
        sub_ref[0] >> 3,
        (first_table_ref, second_table_ref),
        (first_weights_ref, second_weights_ref),
        image_ref,
        left_ref,
        (one_ref, two_ref, three_ref, four_ref),
    )


def params(mib):
    return pltpu.CompilerParams(vmem_limit_bytes=mib * 1024 * 1024)


def vmem():
    return pl.BlockSpec(memory_space=pltpu.VMEM)


def call(kernel, name, mib, out_shape, in_specs, scratch=(), flops=0):
    multiple = isinstance(out_shape, list)
    return pl.pallas_call(
        kernel,
        out_shape=out_shape,
        in_specs=in_specs,
        out_specs=[vmem()] * len(out_shape) if multiple else vmem(),
        scratch_shapes=list(scratch),
        compiler_params=params(mib),
        cost_estimate=pl.CostEstimate(flops=flops, bytes_accessed=0, transcendentals=0),
        name=name,
    )


def partial_image(echoes, chirp_ref, band_starts, doppler_rates, slot_pulse, interp_weights):
    pulses, _, pulse_len = echoes.shape
    chirp_len = chirp_ref.shape[1]
    blocks, tiles = band_starts.shape
    _, _, band, image_rows, columns = interp_weights.shape
    count = slot_pulse.shape[2]
    lines = 2 * pulse_len // LANES
    span = chirp_len + LANES
    places = columns // LANES
    parts = places // 2
    near = 4
    far = tiles // near
    smem = pl.BlockSpec(memory_space=pltpu.SMEM)
    anywhere = pl.BlockSpec(memory_space=pl.ANY)
    shape = jax.ShapeDtypeStruct
    sub = lax.axis_index("sub").astype(jnp.int32).reshape(1)
    me = lax.axis_index("tile").astype(jnp.int32).reshape(1)

    samples = echoes.reshape(pulses, 2, pulse_len // LANES, LANES).transpose(0, 2, 1, 3)
    samples = samples.reshape(pulses, lines, LANES)
    weights = interp_weights.reshape(blocks, 2, band, image_rows, places, LANES)
    weights = weights.transpose(0, 1, 2, 4, 3, 5).reshape(
        blocks * 2 * band, places * image_rows, LANES
    )
    own = shape((near, 2 * pulses, band), jnp.bfloat16)
    extras = shape((blocks * count + near * 2 * pulses, LANES), jnp.float32)
    *bands, extra = call(
        compress_kernel,
        "compress",
        60,
        [own] * (far - 1) + [extras],
        [smem] * 3 + [anywhere] * 4,
        [
            pltpu.VMEM((2, chirp_len), jnp.bfloat16),
            pltpu.VMEM((1, blocks * count), jnp.float32),
            pltpu.VMEM((blocks, count), jnp.int32),
            pltpu.VMEM((pulses, lines, LANES), jnp.bfloat16),
            pltpu.VMEM((lines // 2 + span // LANES, 2 * pulses, LANES), jnp.bfloat16),
            pltpu.VMEM((2 * LANES, span), jnp.bfloat16),
        ]
        + [pltpu.VMEM((near * 2 * pulses, span), jnp.bfloat16)] * far
        + [
            pltpu.SemaphoreType.DMA((4,)),
        ],
        flops=6 * 10**9,
    )(me, sub, band_starts, chirp_ref, doppler_rates, slot_pulse.reshape(blocks, count), samples)

    subs = lax.axis_size("sub")

    def swap(value, by_core):
        pairs = [
            (one * tiles + tile, one * tiles + (tile ^ by_core[one & 1]))
            for one in range(subs)
            for tile in range(tiles)
        ]
        return lax.ppermute(value, ("sub", "tile"), pairs)

    table = shape((parts, 2 * count, 2 * LANES), jnp.bfloat16)
    turned = shape((2, places * image_rows, band, LANES), jnp.bfloat16)
    first_table, second_table, mine = call(phase_kernel, "phase", 12, [table, table, own], [vmem()], flops=4 * 10**9)(extra)
    bands = [mine] + [swap(bands[dy - 1], (dy, dy * near)) for dy in range(1, far)]
    passed = call(
        relay_kernel,
        "relay",
        16,
        [shape((far, 2 * pulses, band), jnp.bfloat16)] * (near - 1),
        [anywhere] + [vmem()] * far,
    )(first_table, *bands)
    first_weights, second_weights = call(turn_kernel, "turn", 12, [turned, turned], [vmem(), anywhere], flops=4 * 10**9)(
        weights, passed[0]
    )
    passed = [swap(passed[dz - 1], (dz * near, dz)) for dz in range(1, near)]
    sources = bands + passed
    half = shape((places // 2, 2 * image_rows, LANES), jnp.float32)
    focused = [pltpu.VMEM((2 * band, 2 * LANES), jnp.float32)] * (2 * blocks)
    far_image, left = call(
        far_image_kernel,
        "far_image",
        12,
        [half, shape((blocks, 2 * band, 2 * count), jnp.bfloat16)],
        [smem, smem] + [vmem()] * (4 + len(sources)),
        [pltpu.VMEM((tiles, 2 * pulses, band), jnp.bfloat16)] + focused,
        flops=3 * 10**9,
    )(me, sub, first_table, second_table, first_weights, second_weights, *sources)
    near_image = call(
        near_image_kernel, "near_image", 12, half, [smem] + [vmem()] * 5 + [anywhere], focused, flops=3 * 10**9
    )(sub, first_table, second_table, first_weights, second_weights, left, far_image)
    return sub, far_image, near_image


def shards(*args):
    _, far_image, near_image = partial_image(*args)
    size = 16
    half = size // 2
    came = lax.ppermute(far_image, "sub", [(one, one ^ half) for one in range(size)])
    groups = [list(range(half)), list(range(half, size))]
    pieces = lax.all_to_all(near_image + came, "sub", 0, 0, axis_index_groups=groups, tiled=True)
    return jnp.sum(pieces, 0).reshape(2, -1, LANES)


def solution(mesh):
    in_specs = (
        P(("sub", "tile"), None, None),
        P(),
        P("sub", None),
        P("sub", None),
        P("sub", None, None),
        P("sub", None, None, "tile", None),
    )
    out_specs = P(None, "tile", "sub")
    return jax.shard_map(shards, mesh=mesh, in_specs=in_specs, out_specs=out_specs, check_vma=False)
```

```python
import functools

import jax
import jax.numpy as jnp
import numpy as np
from jax import lax
from jax.experimental import pallas as pl
from jax.experimental.pallas import tpu as pltpu
from jax.sharding import PartitionSpec as P

LANES = 128


def compress_kernel(
    me_ref, sub_ref, starts_ref, chirp_hbm, rates_hbm, slots_hbm, echoes_ref, *rest
):
    (
        *bands_refs, extra_ref, chirp_ref, rates_ref, slots_ref, raw_ref, samples_ref, toeplitz_ref,
        lhs_a, lhs_b, lhs_c, lhs_d, sems,
    ) = rest
    fetches = [
        pltpu.make_async_copy(source, target, sems.at[index])
        for index, (source, target) in enumerate(
            (
                (chirp_hbm, chirp_ref),
                (rates_hbm, rates_ref),
                (slots_hbm, slots_ref),
                (echoes_ref, raw_ref),
            )
        )
    ]
    for fetch in fetches:
        fetch.start()
    span = toeplitz_ref.shape[1]
    blocks, tiles = starts_ref.shape
    near = tiles // (len(bands_refs) + 1)
    pulses, lines, _ = raw_ref.shape
    half = pulses // blocks
    rows = 2 * half
    chunks = span // LANES
    samples_ref[lines // 2 :] = jnp.zeros(
        (samples_ref.shape[0] - lines // 2, 2 * pulses, LANES), jnp.bfloat16
    )
    piece = 16
    side = half * piece
    row = lax.broadcasted_iota(jnp.int32, (side, side), 0)
    col = lax.broadcasted_iota(jnp.int32, (side, side), 1)
    order = jnp.where(col == (row & (half - 1)) * piece + (row >> 4), 1.0, 0.0).astype(jnp.bfloat16)
    for fetch in fetches[:3]:
        fetch.wait()
    chirp = chirp_ref[...].astype(jnp.float32)
    pad = jnp.zeros((1, span - chirp.shape[1]), jnp.float32)
    for part in range(2):
        line = jnp.concatenate([chirp[part : part + 1], pad], 1)
        shifted = pltpu.roll(
            jnp.broadcast_to(line, (LANES, span)), 0, 1, stride=1, stride_axis=0
        ).astype(jnp.bfloat16)
        toeplitz_ref[part * LANES : (part + 1) * LANES, :] = shifted
    count = slots_ref.shape[1]
    row = lax.broadcasted_iota(jnp.int32, (count, count), 0)
    col = lax.broadcasted_iota(jnp.int32, (count, count), 1)
    for block in range(blocks):
        slots = slots_ref[block : block + 1, :].astype(jnp.float32)
        slot = jnp.sum(jnp.where(row == col, slots, 0.0), 1, keepdims=True)
        rates = rates_ref[:, block * count : (block + 1) * count]
        rate = jnp.sum(jnp.where(slot == col.astype(jnp.float32), rates, 0.0), 1, keepdims=True)
        extra_ref[block * count : (block + 1) * count, :] = jnp.broadcast_to(rate, (count, LANES))
    fetches[3].wait()
    for group in range(lines // piece):
        block_rows = jnp.concatenate(
            [
                raw_ref[block * half : (block + 1) * half, group * piece : (group + 1) * piece, :].reshape(
                    side, LANES
                )
                for block in range(blocks)
            ],
            1,
        )
        moved = jnp.dot(order, block_rows, preferred_element_type=jnp.float32).astype(jnp.bfloat16)
        for block in range(blocks):
            samples_ref[
                group * piece // 2 : (group + 1) * piece // 2, block * rows : (block + 1) * rows, :
            ] = moved[:, block * LANES : (block + 1) * LANES].reshape(piece // 2, rows, LANES)
    lane = lax.broadcasted_iota(jnp.int32, (rows, LANES), 1)
    lhs_refs = (lhs_a, lhs_b, lhs_c, lhs_d)

    def gather(dy):
        for dz in range(near):
            for block in range(blocks):
                start = starts_ref[block, me_ref[0] ^ distance_of(sub_ref[0], dy, dz, near)]
                first = start >> 7
                shift = start & (LANES - 1)
                turn = (LANES - shift) & (LANES - 1)
                keep = lane < LANES - shift
                place = (dz * blocks + block) * rows

                def rolled(chunk):
                    line = samples_ref[first + chunk, block * rows : (block + 1) * rows, :]
                    return pltpu.roll(line, turn, 1)

                low = rolled(0)
                for chunk in range(chunks):
                    high = rolled(chunk + 1)
                    lhs_refs[dy][place : place + rows, chunk * LANES : (chunk + 1) * LANES] = jnp.where(
                        keep, low, high
                    )
                    low = high

    def correlate(dy):
        return lax.dot_general(
            lhs_refs[dy][...],
            toeplitz_ref[...],
            (((1,), (1,)), ((), ())),
            preferred_element_type=jnp.float32,
        )

    def cut(dy, product):
        for dz in range(near):
            for block in range(blocks):
                place = (dz * blocks + block) * rows
                real = product[place : place + half]
                imag = product[place + half : place + rows]
                for part, band in enumerate(
                    (real[:, :LANES] + imag[:, LANES:], imag[:, :LANES] - real[:, LANES:])
                ):
                    band = band.astype(jnp.bfloat16)
                    top = block * rows + part * half
                    if dy == 0:
                        top += blocks * count + dz * 2 * pulses
                        extra_ref[top : top + half, :] = band.astype(jnp.float32)
                    else:
                        bands_refs[dy - 1][dz, top : top + half, :] = band

    gather(0)
    for dy in range(len(lhs_refs)):
        if dy + 1 < len(lhs_refs):
            gather(dy + 1)
        cut(dy, correlate(dy))


FIRST_Z, FIRST_Y = (0, 3, 2, 1), (0, 2, 1, 3)
SECOND_Z, SECOND_Y = (0, 1, 3, 2), (0, 3, 2, 1)


def distance_of(sub, first, second, near):
    return jnp.where(
        (sub & 1) == 1,
        FIRST_Y[first] * near + SECOND_Z[second],
        SECOND_Y[second] * near + FIRST_Z[first],
    )


def sine_cosine(angle):
    turns = jnp.round(angle * np.float32(2 / np.pi))
    rest = (angle - turns * np.float32(1.5703125)) - turns * np.float32(np.pi / 2 - 1.5703125)
    quarter = turns.astype(jnp.int32)
    sq = rest * rest
    sine = np.float32(1 / 362880) * sq + np.float32(-1 / 5040)
    sine = sine * sq + np.float32(1 / 120)
    sine = sine * sq + np.float32(-1 / 6)
    sine = sine * sq * rest + rest
    cosine = np.float32(1 / 40320) * sq + np.float32(-1 / 720)
    cosine = cosine * sq + np.float32(1 / 24)
    cosine = cosine * sq + np.float32(-1 / 2)
    cosine = cosine * sq + np.float32(1)
    odd = (quarter & 1) == 1
    sin_out = jnp.where(odd, cosine, sine)
    cos_out = jnp.where(odd, sine, cosine)
    sin_out = jnp.where((quarter & 2) == 2, -sin_out, sin_out)
    cos_out = jnp.where(((quarter + 1) & 2) == 2, -cos_out, cos_out)
    return sin_out, cos_out


def phase_kernel(extra_ref, first_table_ref, second_table_ref, bands_ref):
    count = first_table_ref.shape[1] // 2
    bands_ref[...] = extra_ref[2 * count :].astype(jnp.bfloat16).reshape(bands_ref.shape)
    phase_table(0, extra_ref, first_table_ref)
    phase_table(1, extra_ref, second_table_ref)


def turn_kernel(far, sub_ref, weights_ref, after_ref, first_ref, second_ref):
    band = first_ref.shape[2]
    lines = first_ref.shape[1]
    offset = ((sub_ref[0] >> 3) ^ far) * lines
    size = 16
    side = size * size
    row = lax.broadcasted_iota(jnp.int32, (side, side), 0)
    col = lax.broadcasted_iota(jnp.int32, (side, side), 1)
    order = jnp.where(col == (row & (size - 1)) * size + (row >> 4), 1.0, 0.0).astype(jnp.bfloat16)
    for block, out_ref in enumerate((first_ref, second_ref)):
        for part in range(2):

            def step(chunk, carry, block=block, part=part, out_ref=out_ref):
                first = pl.multiple_of(chunk * size, size)
                for pair in range(lines // (2 * size)):
                    tops = [(2 * pair + one) * size for one in range(2)]
                    block_rows = jnp.concatenate(
                        [
                            weights_ref[
                                pl.ds((block * 2 + part) * band + first, size),
                                pl.ds(pl.multiple_of(offset + top, size), size),
                                :,
                            ].reshape(side, LANES)
                            for top in tops
                        ],
                        1,
                    )
                    moved = jnp.dot(order, block_rows, preferred_element_type=jnp.float32).astype(
                        jnp.bfloat16
                    )
                    for one, top in enumerate(tops):
                        out_ref[part, top : top + size, pl.ds(first, size), :] = moved[
                            :, one * LANES : (one + 1) * LANES
                        ].reshape(size, size, LANES)
                return carry

            lax.fori_loop(0, band // size, step, 0, unroll=True)


def phase_table(block, rate_ref, table_ref):
    count = table_ref.shape[1] // 2
    columns = table_ref.shape[0] * table_ref.shape[2]
    lane = lax.broadcasted_iota(jnp.int32, (32, LANES), 1).astype(jnp.float32)
    place = (lane + 0.5) * np.float32(1 / columns) - 0.5
    for group in range(count // 32):
        span = slice(group * 32, group * 32 + 32)
        rate = rate_ref[block * count + group * 32 : block * count + group * 32 + 32, :]
        sine, cosine = sine_cosine(rate * place)
        step_sine, step_cosine = sine_cosine(rate * np.float32(LANES / columns))
        for chunk in range(columns // LANES):
            if chunk > 0:
                sine, cosine = (
                    sine * step_cosine + cosine * step_sine,
                    cosine * step_cosine - sine * step_sine,
                )
            lanes = slice(chunk % 2 * LANES, (chunk % 2 + 1) * LANES)
            table_ref[chunk // 2, span, lanes] = cosine.astype(jnp.bfloat16)
            table_ref[chunk // 2, count + group * 32 : count + group * 32 + 32, lanes] = (
                sine.astype(jnp.bfloat16)
            )


def relay_kernel(after_ref, *refs):
    near = refs[0].shape[0]
    far = len(refs) - near + 1
    for dz in range(1, near):
        for dy in range(far):
            refs[far + dz - 1][dy] = refs[dy][dz]


def weighted_sum(side, table_refs, weights_refs, image_ref, left_ref, focused_refs):
    blocks = len(table_refs)
    places, lines, _ = image_ref.shape
    image_rows = lines // 2
    pairs = places // 2
    band = weights_refs[0].shape[2]

    def focus(pair):
        for block in range(blocks):
            focused_refs[pair % 2 * blocks + block][...] = jnp.dot(
                left_ref[block], table_refs[block][side * pairs + pair], preferred_element_type=jnp.float32
            )

    focus(0)
    for pair in range(pairs):
        if pair + 1 < pairs:
            focus(pair + 1)
        for place in range(2):
            lanes = slice(place * LANES, (place + 1) * LANES)
            real = [jnp.zeros((8, LANES), jnp.float32)] * image_rows
            imag = [jnp.zeros((8, LANES), jnp.float32)] * image_rows
            for block in range(blocks):
                focused_ref = focused_refs[pair % 2 * blocks + block]
                for k in range(0, band, 16):
                    focus_real = focused_ref[k : k + 16, lanes]
                    focus_imag = focused_ref[band + k : band + k + 16, lanes]
                    for row in range(image_rows):
                        line = (2 * pair + place) * image_rows + row
                        weight_real = weights_refs[block][0, line, k : k + 16, :].astype(jnp.float32)
                        weight_imag = weights_refs[block][1, line, k : k + 16, :].astype(jnp.float32)
                        for first in (0, 8):
                            part = slice(first, first + 8)
                            wr, wi = weight_real[part], weight_imag[part]
                            fr, fi = focus_real[part], focus_imag[part]
                            real[row] = real[row] + (wr * fr - wi * fi)
                            imag[row] = imag[row] + (wr * fi + wi * fr)
            image_ref[2 * pair + place] = jnp.concatenate(
                [jnp.sum(one, 0, keepdims=True) for one in real + imag], 0
            )


def far_image_kernel(
    me_ref, sub_ref, first_table_ref, second_table_ref, first_weights_ref, second_weights_ref, *rest
):
    *sources_refs, image_ref, left_ref, bands_ref, one_ref, two_ref, three_ref, four_ref = rest
    sources, band_rows, band = bands_ref.shape
    far_count = len(sources_refs) // 2 + 1
    near_refs, far_refs = sources_refs[:far_count], sources_refs[far_count:]
    near = sources // far_count
    blocks = left_ref.shape[0]
    rows = band_rows // blocks
    half = rows // 2
    count = sources * half
    for dy in range(far_count):
        bands_ref[me_ref[0] ^ distance_of(sub_ref[0], dy, 0, near)] = near_refs[dy][0]
        for dz in range(1, near):
            bands_ref[me_ref[0] ^ distance_of(sub_ref[0], dy, dz, near)] = far_refs[dz - 1][dy]
    for block in range(blocks):
        real = bands_ref[:, block * rows : block * rows + half, :].reshape(count, band)
        imag = bands_ref[:, block * rows + half : (block + 1) * rows, :].reshape(count, band)
        top = jnp.concatenate([real, imag], 1)
        bottom = jnp.concatenate([-imag, real], 1)
        left_ref[block] = jnp.concatenate([top, bottom], 0).T
    weighted_sum(
        1 - (sub_ref[0] >> 3),
        (first_table_ref, second_table_ref),
        (first_weights_ref, second_weights_ref),
        image_ref,
        left_ref,
        (one_ref, two_ref, three_ref, four_ref),
    )


def near_image_kernel(
    sub_ref, first_table_ref, second_table_ref, first_weights_ref, second_weights_ref, left_ref, after_ref,
    image_ref, one_ref, two_ref, three_ref, four_ref,
):
    weighted_sum(
        sub_ref[0] >> 3,
        (first_table_ref, second_table_ref),
        (first_weights_ref, second_weights_ref),
        image_ref,
        left_ref,
        (one_ref, two_ref, three_ref, four_ref),
    )


def params(mib):
    return pltpu.CompilerParams(vmem_limit_bytes=mib * 1024 * 1024)


def vmem():
    return pl.BlockSpec(memory_space=pltpu.VMEM)


def call(kernel, name, mib, out_shape, in_specs, scratch=(), flops=0):
    multiple = isinstance(out_shape, list)
    return pl.pallas_call(
        kernel,
        out_shape=out_shape,
        in_specs=in_specs,
        out_specs=[vmem()] * len(out_shape) if multiple else vmem(),
        scratch_shapes=list(scratch),
        compiler_params=params(mib),
        cost_estimate=pl.CostEstimate(flops=flops, bytes_accessed=0, transcendentals=0),
        name=name,
    )


def partial_image(echoes, chirp_ref, band_starts, doppler_rates, slot_pulse, interp_weights):
    pulses, _, pulse_len = echoes.shape
    chirp_len = chirp_ref.shape[1]
    blocks, tiles = band_starts.shape
    _, _, band, image_rows, columns = interp_weights.shape
    count = slot_pulse.shape[2]
    lines = 2 * pulse_len // LANES
    span = chirp_len + LANES
    places = columns // LANES
    parts = places // 2
    near = 4
    far = tiles // near
    smem = pl.BlockSpec(memory_space=pltpu.SMEM)
    anywhere = pl.BlockSpec(memory_space=pl.ANY)
    shape = jax.ShapeDtypeStruct
    sub = lax.axis_index("sub").astype(jnp.int32).reshape(1)
    me = lax.axis_index("tile").astype(jnp.int32).reshape(1)

    samples = echoes.reshape(pulses, 2, pulse_len // LANES, LANES).transpose(0, 2, 1, 3)
    samples = samples.reshape(pulses, lines, LANES)
    weights = interp_weights.reshape(blocks, 2, band, image_rows, places, LANES)
    weights = weights.transpose(0, 1, 2, 4, 3, 5).reshape(
        blocks * 2 * band, places * image_rows, LANES
    )
    own = shape((near, 2 * pulses, band), jnp.bfloat16)
    extras = shape((blocks * count + near * 2 * pulses, LANES), jnp.float32)
    *bands, extra = call(
        compress_kernel,
        "compress",
        60,
        [own] * (far - 1) + [extras],
        [smem] * 3 + [anywhere] * 4,
        [
            pltpu.VMEM((2, chirp_len), jnp.bfloat16),
            pltpu.VMEM((1, blocks * count), jnp.float32),
            pltpu.VMEM((blocks, count), jnp.int32),
            pltpu.VMEM((pulses, lines, LANES), jnp.bfloat16),
            pltpu.VMEM((lines // 2 + span // LANES, 2 * pulses, LANES), jnp.bfloat16),
            pltpu.VMEM((2 * LANES, span), jnp.bfloat16),
        ]
        + [pltpu.VMEM((near * 2 * pulses, span), jnp.bfloat16)] * far
        + [
            pltpu.SemaphoreType.DMA((4,)),
        ],
        flops=6 * 10**9,
    )(me, sub, band_starts, chirp_ref, doppler_rates, slot_pulse.reshape(blocks, count), samples)

    subs = lax.axis_size("sub")

    def swap(value, by_core):
        pairs = [
            (one * tiles + tile, one * tiles + (tile ^ by_core[one & 1]))
            for one in range(subs)
            for tile in range(tiles)
        ]
        return lax.ppermute(value, ("sub", "tile"), pairs)

    table = shape((parts, 2 * count, 2 * LANES), jnp.bfloat16)
    turned = shape((2, places // 2 * image_rows, band, LANES), jnp.bfloat16)

    def turn(far, after):
        return call(
            functools.partial(turn_kernel, far),
            "turn",
            12,
            [turned, turned],
            [smem, vmem(), anywhere],
            flops=2 * 10**9,
        )(sub, weights, after)

    first_table, second_table, mine = call(phase_kernel, "phase", 12, [table, table, own], [vmem()], flops=4 * 10**9)(extra)
    bands = [mine] + [
        swap(bands[dy - 1], (FIRST_Z[dy], FIRST_Y[dy] * near)) for dy in range(1, far)
    ]
    passed = call(
        relay_kernel,
        "relay",
        16,
        [shape((far, 2 * pulses, band), jnp.bfloat16)] * (near - 1),
        [anywhere] + [vmem()] * far,
    )(first_table, *bands)
    far_weights = turn(1, passed[0])
    passed = [swap(passed[dz - 1], (SECOND_Y[dz] * near, SECOND_Z[dz])) for dz in range(1, near)]
    sources = bands + passed
    half = shape((places // 2, 2 * image_rows, LANES), jnp.float32)
    focused = [pltpu.VMEM((2 * band, 2 * LANES), jnp.float32)] * (2 * blocks)
    far_image, left = call(
        far_image_kernel,
        "far_image",
        12,
        [half, shape((blocks, 2 * band, 2 * count), jnp.bfloat16)],
        [smem, smem] + [vmem()] * (4 + len(sources)),
        [pltpu.VMEM((tiles, 2 * pulses, band), jnp.bfloat16)] + focused,
        flops=3 * 10**9,
    )(me, sub, first_table, second_table, *far_weights, *sources)
    near_weights = turn(0, far_image)
    near_image = call(
        near_image_kernel, "near_image", 12, half, [smem] + [vmem()] * 5 + [anywhere], focused, flops=3 * 10**9
    )(sub, first_table, second_table, *near_weights, left, far_image)
    return sub, far_image, near_image


def shards(*args):
    _, far_image, near_image = partial_image(*args)
    size = 16
    half = size // 2
    came = lax.ppermute(far_image, "sub", [(one, one ^ half) for one in range(size)])
    groups = [list(range(half)), list(range(half, size))]
    pieces = lax.all_to_all(near_image + came, "sub", 0, 0, axis_index_groups=groups, tiled=True)
    return jnp.sum(pieces, 0).reshape(2, -1, LANES)


def solution(mesh):
    in_specs = (
        P(("sub", "tile"), None, None),
        P(),
        P("sub", None),
        P("sub", None),
        P("sub", None, None),
        P("sub", None, None, "tile", None),
    )
    out_specs = P(None, "tile", "sub")
    return jax.shard_map(shards, mesh=mesh, in_specs=in_specs, out_specs=out_specs, check_vma=False)
```

```python
import jax
import jax.numpy as jnp
import numpy as np
from jax import lax
from jax.experimental import pallas as pl
from jax.experimental.pallas import tpu as pltpu
from jax.sharding import PartitionSpec as P

LANES = 128


def compress_kernel(
    me_ref, sub_ref, starts_ref, chirp_hbm, rates_hbm, slots_hbm, echoes_ref, *rest
):
    (
        *bands_refs, extra_ref, chirp_ref, rates_ref, slots_ref, raw_ref, samples_ref, toeplitz_ref,
        lhs_a, lhs_b, lhs_c, lhs_d, sems,
    ) = rest
    fetches = [
        pltpu.make_async_copy(source, target, sems.at[index])
        for index, (source, target) in enumerate(
            (
                (chirp_hbm, chirp_ref),
                (rates_hbm, rates_ref),
                (slots_hbm, slots_ref),
                (echoes_ref, raw_ref),
            )
        )
    ]
    for fetch in fetches:
        fetch.start()
    span = toeplitz_ref.shape[1]
    blocks, tiles = starts_ref.shape
    near = tiles // (len(bands_refs) + 1)
    pulses, lines, _ = raw_ref.shape
    half = pulses // blocks
    rows = 2 * half
    chunks = span // LANES
    samples_ref[lines // 2 :] = jnp.zeros(
        (samples_ref.shape[0] - lines // 2, 2 * pulses, LANES), jnp.bfloat16
    )
    piece = 16
    side = half * piece
    row = lax.broadcasted_iota(jnp.int32, (side, side), 0)
    col = lax.broadcasted_iota(jnp.int32, (side, side), 1)
    order = jnp.where(col == (row & (half - 1)) * piece + (row >> 4), 1.0, 0.0).astype(jnp.bfloat16)
    for fetch in fetches[:3]:
        fetch.wait()
    chirp = chirp_ref[...].astype(jnp.float32)
    pad = jnp.zeros((1, span - chirp.shape[1]), jnp.float32)
    for part in range(2):
        line = jnp.concatenate([chirp[part : part + 1], pad], 1)
        shifted = pltpu.roll(
            jnp.broadcast_to(line, (16, span)), 0, 1, stride=1, stride_axis=0
        ).astype(jnp.bfloat16)
        for first in range(0, LANES, 16):
            toeplitz_ref[part * LANES + first : part * LANES + first + 16, :] = (
                pltpu.roll(shifted, first, 1) if first > 0 else shifted
            )
    count = slots_ref.shape[1]
    row = lax.broadcasted_iota(jnp.int32, (count, count), 0)
    col = lax.broadcasted_iota(jnp.int32, (count, count), 1)
    for block in range(blocks):
        slots = slots_ref[block : block + 1, :].astype(jnp.float32)
        slot = jnp.sum(jnp.where(row == col, slots, 0.0), 1, keepdims=True)
        rates = rates_ref[:, block * count : (block + 1) * count]
        rate = jnp.sum(jnp.where(slot == col.astype(jnp.float32), rates, 0.0), 1, keepdims=True)
        extra_ref[block * count : (block + 1) * count, :] = jnp.broadcast_to(rate, (count, LANES))
    fetches[3].wait()
    for group in range(lines // piece):
        block_rows = jnp.concatenate(
            [
                raw_ref[block * half : (block + 1) * half, group * piece : (group + 1) * piece, :].reshape(
                    side, LANES
                )
                for block in range(blocks)
            ],
            1,
        )
        moved = jnp.dot(order, block_rows, preferred_element_type=jnp.float32).astype(jnp.bfloat16)
        for block in range(blocks):
            samples_ref[
                group * piece // 2 : (group + 1) * piece // 2, block * rows : (block + 1) * rows, :
            ] = moved[:, block * LANES : (block + 1) * LANES].reshape(piece // 2, rows, LANES)
    lane = lax.broadcasted_iota(jnp.int32, (rows, LANES), 1)
    lhs_refs = (lhs_a, lhs_b, lhs_c, lhs_d)

    def gather(dy):
        for dz in range(near):
            for block in range(blocks):
                start = starts_ref[block, me_ref[0] ^ distance_of(sub_ref[0], dy, dz, near)]
                first = start >> 7
                shift = start & (LANES - 1)
                turn = (LANES - shift) & (LANES - 1)
                keep = lane < LANES - shift
                place = (dz * blocks + block) * rows

                def rolled(chunk):
                    line = samples_ref[first + chunk, block * rows : (block + 1) * rows, :]
                    return pltpu.roll(line, turn, 1)

                low = rolled(0)
                for chunk in range(chunks):
                    high = rolled(chunk + 1)
                    lhs_refs[dy][place : place + rows, chunk * LANES : (chunk + 1) * LANES] = jnp.where(
                        keep, low, high
                    )
                    low = high

    def correlate(dy):
        return lax.dot_general(
            lhs_refs[dy][...],
            toeplitz_ref[...],
            (((1,), (1,)), ((), ())),
            preferred_element_type=jnp.float32,
        )

    def cut(dy, product):
        for dz in range(near):
            for block in range(blocks):
                place = (dz * blocks + block) * rows
                real = product[place : place + half]
                imag = product[place + half : place + rows]
                for part, band in enumerate(
                    (real[:, :LANES] + imag[:, LANES:], imag[:, :LANES] - real[:, LANES:])
                ):
                    band = band.astype(jnp.bfloat16)
                    top = block * rows + part * half
                    if dy == 0:
                        top += blocks * count + dz * 2 * pulses
                        extra_ref[top : top + half, :] = band.astype(jnp.float32)
                    else:
                        bands_refs[dy - 1][dz, top : top + half, :] = band

    gather(0)
    for dy in range(len(lhs_refs)):
        if dy + 1 < len(lhs_refs):
            gather(dy + 1)
        cut(dy, correlate(dy))


FIRST_Z, FIRST_Y = (0, 3, 2, 1), (0, 2, 1, 3)
SECOND_Z, SECOND_Y = (0, 1, 3, 2), (0, 3, 2, 1)


def distance_of(sub, first, second, near):
    return jnp.where(
        (sub & 1) == 1,
        FIRST_Y[first] * near + SECOND_Z[second],
        SECOND_Y[second] * near + FIRST_Z[first],
    )


def sine_cosine(angle):
    turns = jnp.round(angle * np.float32(2 / np.pi))
    rest = (angle - turns * np.float32(1.5703125)) - turns * np.float32(np.pi / 2 - 1.5703125)
    quarter = turns.astype(jnp.int32)
    sq = rest * rest
    sine = np.float32(1 / 362880) * sq + np.float32(-1 / 5040)
    sine = sine * sq + np.float32(1 / 120)
    sine = sine * sq + np.float32(-1 / 6)
    sine = sine * sq * rest + rest
    cosine = np.float32(1 / 40320) * sq + np.float32(-1 / 720)
    cosine = cosine * sq + np.float32(1 / 24)
    cosine = cosine * sq + np.float32(-1 / 2)
    cosine = cosine * sq + np.float32(1)
    odd = (quarter & 1) == 1
    sin_out = jnp.where(odd, cosine, sine)
    cos_out = jnp.where(odd, sine, cosine)
    sin_out = jnp.where((quarter & 2) == 2, -sin_out, sin_out)
    cos_out = jnp.where(((quarter + 1) & 2) == 2, -cos_out, cos_out)
    return sin_out, cos_out


def phase_kernel(extra_ref, first_table_ref, second_table_ref, bands_ref):
    count = first_table_ref.shape[1] // 2
    bands_ref[...] = extra_ref[2 * count :].astype(jnp.bfloat16).reshape(bands_ref.shape)
    phase_table(0, extra_ref, first_table_ref)
    phase_table(1, extra_ref, second_table_ref)


def turn_kernel(weights_ref, after_ref, first_ref, second_ref):
    band = first_ref.shape[2]
    lines = first_ref.shape[1]
    size = 16
    side = size * size
    row = lax.broadcasted_iota(jnp.int32, (side, side), 0)
    col = lax.broadcasted_iota(jnp.int32, (side, side), 1)
    order = jnp.where(col == (row & (size - 1)) * size + (row >> 4), 1.0, 0.0).astype(jnp.bfloat16)
    for block, out_ref in enumerate((first_ref, second_ref)):
        for part in range(2):

            def step(chunk, carry, block=block, part=part, out_ref=out_ref):
                first = pl.multiple_of(chunk * size, size)
                for pair in range(lines // (2 * size)):
                    tops = [(2 * pair + one) * size for one in range(2)]
                    block_rows = jnp.concatenate(
                        [
                            weights_ref[
                                pl.ds((block * 2 + part) * band + first, size), top : top + size, :
                            ].reshape(side, LANES)
                            for top in tops
                        ],
                        1,
                    )
                    moved = jnp.dot(order, block_rows, preferred_element_type=jnp.float32).astype(
                        jnp.bfloat16
                    )
                    for one, top in enumerate(tops):
                        out_ref[part, top : top + size, pl.ds(first, size), :] = moved[
                            :, one * LANES : (one + 1) * LANES
                        ].reshape(size, size, LANES)
                return carry

            lax.fori_loop(0, band // size, step, 0, unroll=True)


def phase_table(block, rate_ref, table_ref):
    count = table_ref.shape[1] // 2
    columns = table_ref.shape[0] * table_ref.shape[2]
    lane = lax.broadcasted_iota(jnp.int32, (32, LANES), 1).astype(jnp.float32)
    place = (lane + 0.5) * np.float32(1 / columns) - 0.5
    for group in range(count // 32):
        span = slice(group * 32, group * 32 + 32)
        rate = rate_ref[block * count + group * 32 : block * count + group * 32 + 32, :]
        sine, cosine = sine_cosine(rate * place)
        step_sine, step_cosine = sine_cosine(rate * np.float32(LANES / columns))
        for chunk in range(columns // LANES):
            if chunk > 0:
                sine, cosine = (
                    sine * step_cosine + cosine * step_sine,
                    cosine * step_cosine - sine * step_sine,
                )
            lanes = slice(chunk % 2 * LANES, (chunk % 2 + 1) * LANES)
            table_ref[chunk // 2, span, lanes] = cosine.astype(jnp.bfloat16)
            table_ref[chunk // 2, count + group * 32 : count + group * 32 + 32, lanes] = (
                sine.astype(jnp.bfloat16)
            )


def relay_kernel(after_ref, *refs):
    near = refs[0].shape[0]
    far = len(refs) - near + 1
    for dz in range(1, near):
        for dy in range(far):
            refs[far + dz - 1][dy] = refs[dy][dz]


def weighted_sum(side, table_refs, weights_refs, image_ref, left_ref, focused_refs):
    blocks = len(table_refs)
    pairs, lines, _ = image_ref.shape
    places = 2 * pairs
    image_rows = lines // 4
    band = weights_refs[0].shape[2]

    def focus(pair):
        for block in range(blocks):
            focused_refs[pair % 2 * blocks + block][...] = jnp.dot(
                left_ref[block], table_refs[block][side * pairs + pair], preferred_element_type=jnp.float32
            )

    focus(0)
    for pair in range(pairs):
        if pair + 1 < pairs:
            focus(pair + 1)
        sums = []
        for place in range(2):
            lanes = slice(place * LANES, (place + 1) * LANES)
            real = [jnp.zeros((8, LANES), jnp.float32)] * image_rows
            imag = [jnp.zeros((8, LANES), jnp.float32)] * image_rows
            for block in range(blocks):
                focused_ref = focused_refs[pair % 2 * blocks + block]
                for k in range(0, band, 16):
                    focus_real = focused_ref[k : k + 16, lanes]
                    focus_imag = focused_ref[band + k : band + k + 16, lanes]
                    for row in range(image_rows):
                        line = (side * places + 2 * pair + place) * image_rows + row
                        weight_real = weights_refs[block][0, line, k : k + 16, :].astype(jnp.float32)
                        weight_imag = weights_refs[block][1, line, k : k + 16, :].astype(jnp.float32)
                        for first in (0, 8):
                            part = slice(first, first + 8)
                            wr, wi = weight_real[part], weight_imag[part]
                            fr, fi = focus_real[part], focus_imag[part]
                            real[row] = real[row] + (wr * fr - wi * fi)
                            imag[row] = imag[row] + (wr * fi + wi * fr)
            sums.append(
                jnp.concatenate([jnp.sum(one, 0, keepdims=True) for one in real + imag], 0)
            )
        image_ref[pair] = jnp.concatenate(sums, 0).astype(image_ref.dtype)


def far_image_kernel(
    me_ref, sub_ref, first_table_ref, second_table_ref, first_weights_ref, second_weights_ref, *rest
):
    *sources_refs, image_ref, left_ref, bands_ref, one_ref, two_ref, three_ref, four_ref = rest
    sources, band_rows, band = bands_ref.shape
    far_count = len(sources_refs) // 2 + 1
    near_refs, far_refs = sources_refs[:far_count], sources_refs[far_count:]
    near = sources // far_count
    blocks = left_ref.shape[0]
    rows = band_rows // blocks
    half = rows // 2
    count = sources * half
    for dy in range(far_count):
        bands_ref[me_ref[0] ^ distance_of(sub_ref[0], dy, 0, near)] = near_refs[dy][0]
        for dz in range(1, near):
            bands_ref[me_ref[0] ^ distance_of(sub_ref[0], dy, dz, near)] = far_refs[dz - 1][dy]
    for block in range(blocks):
        real = bands_ref[:, block * rows : block * rows + half, :].reshape(count, band)
        imag = bands_ref[:, block * rows + half : (block + 1) * rows, :].reshape(count, band)
        top = jnp.concatenate([real, imag], 1)
        bottom = jnp.concatenate([-imag, real], 1)
        left_ref[block] = jnp.concatenate([top, bottom], 0).T
    weighted_sum(
        1 - (sub_ref[0] >> 3),
        (first_table_ref, second_table_ref),
        (first_weights_ref, second_weights_ref),
        image_ref,
        left_ref,
        (one_ref, two_ref, three_ref, four_ref),
    )


def near_image_kernel(
    sub_ref, first_table_ref, second_table_ref, first_weights_ref, second_weights_ref, left_ref, after_ref,
    image_ref, one_ref, two_ref, three_ref, four_ref,
):
    weighted_sum(
        sub_ref[0] >> 3,
        (first_table_ref, second_table_ref),
        (first_weights_ref, second_weights_ref),
        image_ref,
        left_ref,
        (one_ref, two_ref, three_ref, four_ref),
    )


def params(mib):
    return pltpu.CompilerParams(vmem_limit_bytes=mib * 1024 * 1024)


def vmem():
    return pl.BlockSpec(memory_space=pltpu.VMEM)


def call(kernel, name, mib, out_shape, in_specs, scratch=(), flops=0):
    multiple = isinstance(out_shape, list)
    return pl.pallas_call(
        kernel,
        out_shape=out_shape,
        in_specs=in_specs,
        out_specs=[vmem()] * len(out_shape) if multiple else vmem(),
        scratch_shapes=list(scratch),
        compiler_params=params(mib),
        cost_estimate=pl.CostEstimate(flops=flops, bytes_accessed=0, transcendentals=0),
        name=name,
    )


def partial_image(echoes, chirp_ref, band_starts, doppler_rates, slot_pulse, interp_weights):
    pulses, _, pulse_len = echoes.shape
    chirp_len = chirp_ref.shape[1]
    blocks, tiles = band_starts.shape
    _, _, band, image_rows, columns = interp_weights.shape
    count = slot_pulse.shape[2]
    lines = 2 * pulse_len // LANES
    span = chirp_len + LANES
    places = columns // LANES
    parts = places // 2
    near = 4
    far = tiles // near
    smem = pl.BlockSpec(memory_space=pltpu.SMEM)
    anywhere = pl.BlockSpec(memory_space=pl.ANY)
    shape = jax.ShapeDtypeStruct
    sub = lax.axis_index("sub").astype(jnp.int32).reshape(1)
    me = lax.axis_index("tile").astype(jnp.int32).reshape(1)

    samples = echoes.reshape(pulses, 2, pulse_len // LANES, LANES).transpose(0, 2, 1, 3)
    samples = samples.reshape(pulses, lines, LANES)
    weights = interp_weights.reshape(blocks, 2, band, image_rows, places, LANES)
    weights = weights.transpose(0, 1, 2, 4, 3, 5).reshape(
        blocks * 2 * band, places * image_rows, LANES
    )
    own = shape((near, 2 * pulses, band), jnp.bfloat16)
    extras = shape((blocks * count + near * 2 * pulses, LANES), jnp.float32)
    *bands, extra = call(
        compress_kernel,
        "compress",
        60,
        [own] * (far - 1) + [extras],
        [smem] * 3 + [anywhere] * 4,
        [
            pltpu.VMEM((2, chirp_len), jnp.bfloat16),
            pltpu.VMEM((1, blocks * count), jnp.float32),
            pltpu.VMEM((blocks, count), jnp.int32),
            pltpu.VMEM((pulses, lines, LANES), jnp.bfloat16),
            pltpu.VMEM((lines // 2 + span // LANES, 2 * pulses, LANES), jnp.bfloat16),
            pltpu.VMEM((2 * LANES, span), jnp.bfloat16),
        ]
        + [pltpu.VMEM((near * 2 * pulses, span), jnp.bfloat16)] * far
        + [
            pltpu.SemaphoreType.DMA((4,)),
        ],
        flops=6 * 10**9,
    )(me, sub, band_starts, chirp_ref, doppler_rates, slot_pulse.reshape(blocks, count), samples)

    subs = lax.axis_size("sub")

    def swap(value, by_core):
        pairs = [
            (one * tiles + tile, one * tiles + (tile ^ by_core[one & 1]))
            for one in range(subs)
            for tile in range(tiles)
        ]
        return lax.ppermute(value, ("sub", "tile"), pairs)

    table = shape((parts, 2 * count, 2 * LANES), jnp.bfloat16)
    turned = shape((2, places * image_rows, band, LANES), jnp.bfloat16)
    first_table, second_table, mine = call(phase_kernel, "phase", 12, [table, table, own], [vmem()], flops=4 * 10**9)(extra)
    bands = [mine] + [
        swap(bands[dy - 1], (FIRST_Z[dy], FIRST_Y[dy] * near)) for dy in range(1, far)
    ]
    passed = call(
        relay_kernel,
        "relay",
        16,
        [shape((far, 2 * pulses, band), jnp.bfloat16)] * (near - 1),
        [anywhere] + [vmem()] * far,
    )(first_table, *bands)
    first_weights, second_weights = call(turn_kernel, "turn", 12, [turned, turned], [vmem(), anywhere], flops=4 * 10**9)(
        weights, passed[0]
    )
    passed = [swap(passed[dz - 1], (SECOND_Y[dz] * near, SECOND_Z[dz])) for dz in range(1, near)]
    sources = bands + passed
    half = (places // 4, 4 * image_rows, LANES)
    focused = [pltpu.VMEM((2 * band, 2 * LANES), jnp.float32)] * (2 * blocks)
    far_image, left = call(
        far_image_kernel,
        "far_image",
        12,
        [shape(half, jnp.bfloat16), shape((blocks, 2 * band, 2 * count), jnp.bfloat16)],
        [smem, smem] + [vmem()] * (4 + len(sources)),
        [pltpu.VMEM((tiles, 2 * pulses, band), jnp.bfloat16)] + focused,
        flops=3 * 10**9,
    )(me, sub, first_table, second_table, first_weights, second_weights, *sources)
    near_image = call(
        near_image_kernel, "near_image", 12, shape(half, jnp.float32), [smem] + [vmem()] * 5 + [anywhere], focused, flops=3 * 10**9
    )(sub, first_table, second_table, first_weights, second_weights, left, far_image)
    return sub, far_image, near_image


def shards(*args):
    _, far_image, near_image = partial_image(*args)
    size = 16
    half = size // 2
    came = lax.ppermute(far_image, "sub", [(one, one ^ half) for one in range(size)])
    groups = [list(range(half)), list(range(half, size))]
    held = (near_image + came.astype(jnp.float32)).reshape(half, -1, LANES)
    pieces = lax.all_to_all(held, "sub", 0, 0, axis_index_groups=groups, tiled=True)
    return jnp.sum(pieces, 0).reshape(2, -1, LANES)


def solution(mesh):
    in_specs = (
        P(("sub", "tile"), None, None),
        P(),
        P("sub", None),
        P("sub", None),
        P("sub", None, None),
        P("sub", None, None, "tile", None),
    )
    out_specs = P(None, "tile", "sub")
    return jax.shard_map(shards, mesh=mesh, in_specs=in_specs, out_specs=out_specs, check_vma=False)
```

```python
import jax
import jax.numpy as jnp
import numpy as np
from jax import lax
from jax.experimental import pallas as pl
from jax.experimental.pallas import tpu as pltpu
from jax.sharding import PartitionSpec as P

LANES = 128


def compress_kernel(
    me_ref, sub_ref, starts_ref, chirp_hbm, rates_hbm, slots_hbm, echoes_ref, *rest
):
    (
        *bands_refs, extra_ref, chirp_ref, rates_ref, slots_ref, raw_ref, samples_ref, toeplitz_ref,
        lhs_a, lhs_b, lhs_c, lhs_d, sems,
    ) = rest
    fetches = [
        pltpu.make_async_copy(source, target, sems.at[index])
        for index, (source, target) in enumerate(
            (
                (chirp_hbm, chirp_ref),
                (rates_hbm, rates_ref),
                (slots_hbm, slots_ref),
                (echoes_ref, raw_ref),
            )
        )
    ]
    for fetch in fetches:
        fetch.start()
    span = toeplitz_ref.shape[1]
    blocks, tiles = starts_ref.shape
    near = tiles // (len(bands_refs) + 1)
    pulses, lines, _ = raw_ref.shape
    half = pulses // blocks
    rows = 2 * half
    chunks = span // LANES
    samples_ref[lines // 2 :] = jnp.zeros(
        (samples_ref.shape[0] - lines // 2, 2 * pulses, LANES), jnp.bfloat16
    )
    piece = 16
    side = half * piece
    row = lax.broadcasted_iota(jnp.int32, (side, side), 0)
    col = lax.broadcasted_iota(jnp.int32, (side, side), 1)
    order = jnp.where(col == (row & (half - 1)) * piece + (row >> 4), 1.0, 0.0).astype(jnp.bfloat16)
    for fetch in fetches:
        fetch.wait()
    chirp = chirp_ref[...].astype(jnp.float32)
    pad = jnp.zeros((1, span - chirp.shape[1]), jnp.float32)
    for part in range(2):
        line = jnp.concatenate([chirp[part : part + 1], pad], 1)
        shifted = pltpu.roll(
            jnp.broadcast_to(line, (LANES, span)), 0, 1, stride=1, stride_axis=0
        ).astype(jnp.bfloat16)
        toeplitz_ref[part * LANES : (part + 1) * LANES, :] = shifted
    count = slots_ref.shape[1]
    row = lax.broadcasted_iota(jnp.int32, (count, count), 0)
    col = lax.broadcasted_iota(jnp.int32, (count, count), 1)
    for block in range(blocks):
        slots = slots_ref[block : block + 1, :].astype(jnp.float32)
        slot = jnp.sum(jnp.where(row == col, slots, 0.0), 1, keepdims=True)
        rates = rates_ref[:, block * count : (block + 1) * count]
        rate = jnp.sum(jnp.where(slot == col.astype(jnp.float32), rates, 0.0), 1, keepdims=True)
        extra_ref[block * count : (block + 1) * count, :] = jnp.broadcast_to(rate, (count, LANES))
    for group in range(lines // piece):
        block_rows = jnp.concatenate(
            [
                raw_ref[block * half : (block + 1) * half, group * piece : (group + 1) * piece, :].reshape(
                    side, LANES
                )
                for block in range(blocks)
            ],
            1,
        )
        moved = jnp.dot(order, block_rows, preferred_element_type=jnp.float32).astype(jnp.bfloat16)
        for block in range(blocks):
            samples_ref[
                group * piece // 2 : (group + 1) * piece // 2, block * rows : (block + 1) * rows, :
            ] = moved[:, block * LANES : (block + 1) * LANES].reshape(piece // 2, rows, LANES)
    lane = lax.broadcasted_iota(jnp.int32, (rows, LANES), 1)
    lhs_refs = (lhs_a, lhs_b, lhs_c, lhs_d)

    def gather(dy):
        for dz in range(near):
            for block in range(blocks):
                start = starts_ref[block, me_ref[0] ^ distance_of(sub_ref[0], dy, dz, near)]
                first = start >> 7
                shift = start & (LANES - 1)
                turn = (LANES - shift) & (LANES - 1)
                keep = lane < LANES - shift
                place = (dz * blocks + block) * rows

                def rolled(chunk):
                    line = samples_ref[first + chunk, block * rows : (block + 1) * rows, :]
                    return pltpu.roll(line, turn, 1)

                low = rolled(0)
                for chunk in range(chunks):
                    high = rolled(chunk + 1)
                    lhs_refs[dy][place : place + rows, chunk * LANES : (chunk + 1) * LANES] = jnp.where(
                        keep, low, high
                    )
                    low = high

    def correlate(dy):
        return lax.dot_general(
            lhs_refs[dy][...],
            toeplitz_ref[...],
            (((1,), (1,)), ((), ())),
            preferred_element_type=jnp.float32,
        )

    def cut(dy, product):
        for dz in range(near):
            for block in range(blocks):
                place = (dz * blocks + block) * rows
                real = product[place : place + half]
                imag = product[place + half : place + rows]
                for part, band in enumerate(
                    (real[:, :LANES] + imag[:, LANES:], imag[:, :LANES] - real[:, LANES:])
                ):
                    band = band.astype(jnp.bfloat16)
                    top = block * rows + part * half
                    if dy == 0:
                        top += blocks * count + dz * 2 * pulses
                        extra_ref[top : top + half, :] = band.astype(jnp.float32)
                    else:
                        bands_refs[dy - 1][dz, top : top + half, :] = band

    gather(0)
    for dy in range(len(lhs_refs)):
        if dy + 1 < len(lhs_refs):
            gather(dy + 1)
        cut(dy, correlate(dy))


FIRST_Z, FIRST_Y = (0, 3, 2, 1), (0, 2, 1, 3)
SECOND_Z, SECOND_Y = (0, 1, 3, 2), (0, 3, 2, 1)


def distance_of(sub, first, second, near):
    return jnp.where(
        (sub & 1) == 0,
        FIRST_Y[first] * near + SECOND_Z[second],
        SECOND_Y[second] * near + FIRST_Z[first],
    )


def sine_cosine(angle):
    turns = jnp.round(angle * np.float32(2 / np.pi))
    rest = (angle - turns * np.float32(1.5703125)) - turns * np.float32(np.pi / 2 - 1.5703125)
    quarter = turns.astype(jnp.int32)
    sq = rest * rest
    sine = np.float32(1 / 362880) * sq + np.float32(-1 / 5040)
    sine = sine * sq + np.float32(1 / 120)
    sine = sine * sq + np.float32(-1 / 6)
    sine = sine * sq * rest + rest
    cosine = np.float32(1 / 40320) * sq + np.float32(-1 / 720)
    cosine = cosine * sq + np.float32(1 / 24)
    cosine = cosine * sq + np.float32(-1 / 2)
    cosine = cosine * sq + np.float32(1)
    odd = (quarter & 1) == 1
    sin_out = jnp.where(odd, cosine, sine)
    cos_out = jnp.where(odd, sine, cosine)
    sin_out = jnp.where((quarter & 2) == 2, -sin_out, sin_out)
    cos_out = jnp.where(((quarter + 1) & 2) == 2, -cos_out, cos_out)
    return sin_out, cos_out


def phase_kernel(extra_ref, first_table_ref, second_table_ref, bands_ref):
    count = first_table_ref.shape[1] // 2
    bands_ref[...] = extra_ref[2 * count :].astype(jnp.bfloat16).reshape(bands_ref.shape)
    phase_table(0, extra_ref, first_table_ref)
    phase_table(1, extra_ref, second_table_ref)


def turn_kernel(weights_ref, after_ref, first_ref, second_ref):
    band = first_ref.shape[2]
    lines = first_ref.shape[1]
    size = 16
    side = size * size
    row = lax.broadcasted_iota(jnp.int32, (side, side), 0)
    col = lax.broadcasted_iota(jnp.int32, (side, side), 1)
    order = jnp.where(col == (row & (size - 1)) * size + (row >> 4), 1.0, 0.0).astype(jnp.bfloat16)
    for block, out_ref in enumerate((first_ref, second_ref)):
        for part in range(2):

            def step(chunk, carry, block=block, part=part, out_ref=out_ref):
                first = pl.multiple_of(chunk * size, size)
                for pair in range(lines // (2 * size)):
                    tops = [(2 * pair + one) * size for one in range(2)]
                    block_rows = jnp.concatenate(
                        [
                            weights_ref[
                                pl.ds((block * 2 + part) * band + first, size), top : top + size, :
                            ].reshape(side, LANES)
                            for top in tops
                        ],
                        1,
                    )
                    moved = jnp.dot(order, block_rows, preferred_element_type=jnp.float32).astype(
                        jnp.bfloat16
                    )
                    for one, top in enumerate(tops):
                        out_ref[part, top : top + size, pl.ds(first, size), :] = moved[
                            :, one * LANES : (one + 1) * LANES
                        ].reshape(size, size, LANES)
                return carry

            lax.fori_loop(0, band // size, step, 0, unroll=True)


def phase_table(block, rate_ref, table_ref):
    count = table_ref.shape[1] // 2
    columns = table_ref.shape[0] * table_ref.shape[2]
    lane = lax.broadcasted_iota(jnp.int32, (32, LANES), 1).astype(jnp.float32)
    place = (lane + 0.5) * np.float32(1 / columns) - 0.5
    for group in range(count // 32):
        span = slice(group * 32, group * 32 + 32)
        rate = rate_ref[block * count + group * 32 : block * count + group * 32 + 32, :]
        sine, cosine = sine_cosine(rate * place)
        step_sine, step_cosine = sine_cosine(rate * np.float32(LANES / columns))
        for chunk in range(columns // LANES):
            if chunk > 0:
                sine, cosine = (
                    sine * step_cosine + cosine * step_sine,
                    cosine * step_cosine - sine * step_sine,
                )
            lanes = slice(chunk % 2 * LANES, (chunk % 2 + 1) * LANES)
            table_ref[chunk // 2, span, lanes] = cosine.astype(jnp.bfloat16)
            table_ref[chunk // 2, count + group * 32 : count + group * 32 + 32, lanes] = (
                sine.astype(jnp.bfloat16)
            )


def relay_kernel(after_ref, *refs):
    near = refs[0].shape[0]
    far = len(refs) - near + 1
    for dz in range(1, near):
        for dy in range(far):
            refs[far + dz - 1][dy] = refs[dy][dz]


def weighted_sum(side, table_refs, weights_refs, image_ref, left_ref, focused_refs):
    blocks = len(table_refs)
    pairs, lines, _ = image_ref.shape
    places = 2 * pairs
    image_rows = lines // 4
    band = weights_refs[0].shape[2]

    def focus(pair):
        for block in range(blocks):
            focused_refs[pair % 2 * blocks + block][...] = jnp.dot(
                left_ref[block], table_refs[block][side * pairs + pair], preferred_element_type=jnp.float32
            )

    focus(0)
    for pair in range(pairs):
        if pair + 1 < pairs:
            focus(pair + 1)
        sums = []
        for place in range(2):
            lanes = slice(place * LANES, (place + 1) * LANES)
            real = [jnp.zeros((8, LANES), jnp.float32)] * image_rows
            imag = [jnp.zeros((8, LANES), jnp.float32)] * image_rows
            for block in range(blocks):
                focused_ref = focused_refs[pair % 2 * blocks + block]
                for k in range(0, band, 16):
                    focus_real = focused_ref[k : k + 16, lanes]
                    focus_imag = focused_ref[band + k : band + k + 16, lanes]
                    for row in range(image_rows):
                        line = (side * places + 2 * pair + place) * image_rows + row
                        weight_real = weights_refs[block][0, line, k : k + 16, :].astype(jnp.float32)
                        weight_imag = weights_refs[block][1, line, k : k + 16, :].astype(jnp.float32)
                        for first in (0, 8):
                            part = slice(first, first + 8)
                            wr, wi = weight_real[part], weight_imag[part]
                            fr, fi = focus_real[part], focus_imag[part]
                            real[row] = real[row] + (wr * fr - wi * fi)
                            imag[row] = imag[row] + (wr * fi + wi * fr)
            sums.append(
                jnp.concatenate([jnp.sum(one, 0, keepdims=True) for one in real + imag], 0)
            )
        image_ref[pair] = jnp.concatenate(sums, 0).astype(image_ref.dtype)


def far_image_kernel(
    me_ref, sub_ref, first_table_ref, second_table_ref, first_weights_ref, second_weights_ref, *rest
):
    *sources_refs, image_ref, left_ref, bands_ref, one_ref, two_ref, three_ref, four_ref = rest
    sources, band_rows, band = bands_ref.shape
    far_count = len(sources_refs) // 2 + 1
    near_refs, far_refs = sources_refs[:far_count], sources_refs[far_count:]
    near = sources // far_count
    blocks = left_ref.shape[0]
    rows = band_rows // blocks
    half = rows // 2
    count = sources * half
    for dy in range(far_count):
        bands_ref[me_ref[0] ^ distance_of(sub_ref[0], dy, 0, near)] = near_refs[dy][0]
        for dz in range(1, near):
            bands_ref[me_ref[0] ^ distance_of(sub_ref[0], dy, dz, near)] = far_refs[dz - 1][dy]
    for block in range(blocks):
        real = bands_ref[:, block * rows : block * rows + half, :].reshape(count, band)
        imag = bands_ref[:, block * rows + half : (block + 1) * rows, :].reshape(count, band)
        top = jnp.concatenate([real, imag], 1)
        bottom = jnp.concatenate([-imag, real], 1)
        left_ref[block] = jnp.concatenate([top, bottom], 0).T
    weighted_sum(
        1 - (sub_ref[0] >> 3),
        (first_table_ref, second_table_ref),
        (first_weights_ref, second_weights_ref),
        image_ref,
        left_ref,
        (one_ref, two_ref, three_ref, four_ref),
    )


def near_image_kernel(
    sub_ref, first_table_ref, second_table_ref, first_weights_ref, second_weights_ref, left_ref, after_ref,
    image_ref, one_ref, two_ref, three_ref, four_ref,
):
    weighted_sum(
        sub_ref[0] >> 3,
        (first_table_ref, second_table_ref),
        (first_weights_ref, second_weights_ref),
        image_ref,
        left_ref,
        (one_ref, two_ref, three_ref, four_ref),
    )


def params(mib):
    return pltpu.CompilerParams(vmem_limit_bytes=mib * 1024 * 1024)


def vmem():
    return pl.BlockSpec(memory_space=pltpu.VMEM)


def call(kernel, name, mib, out_shape, in_specs, scratch=(), flops=0):
    multiple = isinstance(out_shape, list)
    return pl.pallas_call(
        kernel,
        out_shape=out_shape,
        in_specs=in_specs,
        out_specs=[vmem()] * len(out_shape) if multiple else vmem(),
        scratch_shapes=list(scratch),
        compiler_params=params(mib),
        cost_estimate=pl.CostEstimate(flops=flops, bytes_accessed=0, transcendentals=0),
        name=name,
    )


def partial_image(echoes, chirp_ref, band_starts, doppler_rates, slot_pulse, interp_weights):
    pulses, _, pulse_len = echoes.shape
    chirp_len = chirp_ref.shape[1]
    blocks, tiles = band_starts.shape
    _, _, band, image_rows, columns = interp_weights.shape
    count = slot_pulse.shape[2]
    lines = 2 * pulse_len // LANES
    span = chirp_len + LANES
    places = columns // LANES
    parts = places // 2
    near = 4
    far = tiles // near
    smem = pl.BlockSpec(memory_space=pltpu.SMEM)
    anywhere = pl.BlockSpec(memory_space=pl.ANY)
    shape = jax.ShapeDtypeStruct
    sub = lax.axis_index("sub").astype(jnp.int32).reshape(1)
    me = lax.axis_index("tile").astype(jnp.int32).reshape(1)

    samples = echoes.reshape(pulses, 2, pulse_len // LANES, LANES).transpose(0, 2, 1, 3)
    samples = samples.reshape(pulses, lines, LANES)
    weights = interp_weights.reshape(blocks, 2, band, image_rows, places, LANES)
    weights = weights.transpose(0, 1, 2, 4, 3, 5).reshape(
        blocks * 2 * band, places * image_rows, LANES
    )
    own = shape((near, 2 * pulses, band), jnp.bfloat16)
    extras = shape((blocks * count + near * 2 * pulses, LANES), jnp.float32)
    *bands, extra = call(
        compress_kernel,
        "compress",
        60,
        [own] * (far - 1) + [extras],
        [smem] * 3 + [anywhere] * 4,
        [
            pltpu.VMEM((2, chirp_len), jnp.bfloat16),
            pltpu.VMEM((1, blocks * count), jnp.float32),
            pltpu.VMEM((blocks, count), jnp.int32),
            pltpu.VMEM((pulses, lines, LANES), jnp.bfloat16),
            pltpu.VMEM((lines // 2 + span // LANES, 2 * pulses, LANES), jnp.bfloat16),
            pltpu.VMEM((2 * LANES, span), jnp.bfloat16),
        ]
        + [pltpu.VMEM((near * 2 * pulses, span), jnp.bfloat16)] * far
        + [
            pltpu.SemaphoreType.DMA((4,)),
        ],
        flops=6 * 10**9,
    )(me, sub, band_starts, chirp_ref, doppler_rates, slot_pulse.reshape(blocks, count), samples)

    subs = lax.axis_size("sub")

    def swap(value, by_core):
        pairs = [
            (one * tiles + tile, one * tiles + (tile ^ by_core[1 - (one & 1)]))
            for one in range(subs)
            for tile in range(tiles)
        ]
        return lax.ppermute(value, ("sub", "tile"), pairs)

    table = shape((parts, 2 * count, 2 * LANES), jnp.bfloat16)
    turned = shape((2, places * image_rows, band, LANES), jnp.bfloat16)
    first_table, second_table, mine = call(phase_kernel, "phase", 12, [table, table, own], [vmem()], flops=4 * 10**9)(extra)
    bands = [mine] + [
        swap(bands[dy - 1], (FIRST_Z[dy], FIRST_Y[dy] * near)) for dy in range(1, far)
    ]
    passed = call(
        relay_kernel,
        "relay",
        16,
        [shape((far, 2 * pulses, band), jnp.bfloat16)] * (near - 1),
        [anywhere] + [vmem()] * far,
    )(first_table, *bands)
    first_weights, second_weights = call(turn_kernel, "turn", 12, [turned, turned], [vmem(), anywhere], flops=4 * 10**9)(
        weights, passed[0]
    )
    passed = [swap(passed[dz - 1], (SECOND_Y[dz] * near, SECOND_Z[dz])) for dz in range(1, near)]
    sources = bands + passed
    half = (places // 4, 4 * image_rows, LANES)
    focused = [pltpu.VMEM((2 * band, 2 * LANES), jnp.float32)] * (2 * blocks)
    far_image, left = call(
        far_image_kernel,
        "far_image",
        12,
        [shape(half, jnp.bfloat16), shape((blocks, 2 * band, 2 * count), jnp.bfloat16)],
        [smem, smem] + [vmem()] * (4 + len(sources)),
        [pltpu.VMEM((tiles, 2 * pulses, band), jnp.bfloat16)] + focused,
        flops=3 * 10**9,
    )(me, sub, first_table, second_table, first_weights, second_weights, *sources)
    near_image = call(
        near_image_kernel, "near_image", 12, shape(half, jnp.float32), [smem] + [vmem()] * 5 + [anywhere], focused, flops=3 * 10**9
    )(sub, first_table, second_table, first_weights, second_weights, left, far_image)
    return sub, far_image, near_image


def shards(*args):
    _, far_image, near_image = partial_image(*args)
    size = 16
    half = size // 2
    came = lax.ppermute(far_image, "sub", [(one, one ^ half) for one in range(size)])
    groups = [list(range(half)), list(range(half, size))]
    held = (near_image + came.astype(jnp.float32)).reshape(half, -1, LANES)
    pieces = lax.all_to_all(held, "sub", 0, 0, axis_index_groups=groups, tiled=True)
    return jnp.sum(pieces, 0).reshape(2, -1, LANES)


def solution(mesh):
    in_specs = (
        P(("sub", "tile"), None, None),
        P(),
        P("sub", None),
        P("sub", None),
        P("sub", None, None),
        P("sub", None, None, "tile", None),
    )
    out_specs = P(None, "tile", "sub")
    return jax.shard_map(shards, mesh=mesh, in_specs=in_specs, out_specs=out_specs, check_vma=False)
```

```python
import jax
import jax.numpy as jnp
import numpy as np
from jax import lax
from jax.experimental import pallas as pl
from jax.experimental.pallas import tpu as pltpu
from jax.sharding import PartitionSpec as P

LANES = 128


def compress_kernel(
    me_ref, sub_ref, starts_ref, chirp_hbm, rates_hbm, slots_hbm, echoes_ref, *rest
):
    (
        *bands_refs, extra_ref, chirp_ref, rates_ref, slots_ref, raw_ref, samples_ref, toeplitz_ref,
        lhs_a, lhs_b, lhs_c, lhs_d, sems,
    ) = rest
    fetches = [
        pltpu.make_async_copy(source, target, sems.at[index])
        for index, (source, target) in enumerate(
            (
                (chirp_hbm, chirp_ref),
                (rates_hbm, rates_ref),
                (slots_hbm, slots_ref),
                (echoes_ref, raw_ref),
            )
        )
    ]
    for fetch in fetches:
        fetch.start()
    span = toeplitz_ref.shape[1]
    blocks, tiles = starts_ref.shape
    near = tiles // (len(bands_refs) + 1)
    pulses, lines, _ = raw_ref.shape
    half = pulses // blocks
    rows = 2 * half
    chunks = span // LANES
    samples_ref[lines // 2 :] = jnp.zeros(
        (samples_ref.shape[0] - lines // 2, 2 * pulses, LANES), jnp.bfloat16
    )
    piece = 16
    side = half * piece
    row = lax.broadcasted_iota(jnp.int32, (side, side), 0)
    col = lax.broadcasted_iota(jnp.int32, (side, side), 1)
    order = jnp.where(col == (row & (half - 1)) * piece + (row >> 4), 1.0, 0.0).astype(jnp.bfloat16)
    for fetch in fetches:
        fetch.wait()
    chirp = chirp_ref[...].astype(jnp.float32)
    pad = jnp.zeros((1, span - chirp.shape[1]), jnp.float32)
    for part in range(2):
        line = jnp.concatenate([chirp[part : part + 1], pad], 1)
        shifted = pltpu.roll(
            jnp.broadcast_to(line, (LANES, span)), 0, 1, stride=1, stride_axis=0
        ).astype(jnp.bfloat16)
        toeplitz_ref[part * LANES : (part + 1) * LANES, :] = shifted
    count = slots_ref.shape[1]
    row = lax.broadcasted_iota(jnp.int32, (count, count), 0)
    col = lax.broadcasted_iota(jnp.int32, (count, count), 1)
    for block in range(blocks):
        slots = slots_ref[block : block + 1, :].astype(jnp.float32)
        slot = jnp.sum(jnp.where(row == col, slots, 0.0), 1, keepdims=True)
        rates = rates_ref[:, block * count : (block + 1) * count]
        rate = jnp.sum(jnp.where(slot == col.astype(jnp.float32), rates, 0.0), 1, keepdims=True)
        extra_ref[block * count : (block + 1) * count, :] = jnp.broadcast_to(rate, (count, LANES))
    for group in range(lines // piece):
        block_rows = jnp.concatenate(
            [
                raw_ref[block * half : (block + 1) * half, group * piece : (group + 1) * piece, :].reshape(
                    side, LANES
                )
                for block in range(blocks)
            ],
            1,
        )
        moved = jnp.dot(order, block_rows, preferred_element_type=jnp.float32).astype(jnp.bfloat16)
        for block in range(blocks):
            samples_ref[
                group * piece // 2 : (group + 1) * piece // 2, block * rows : (block + 1) * rows, :
            ] = moved[:, block * LANES : (block + 1) * LANES].reshape(piece // 2, rows, LANES)
    lane = lax.broadcasted_iota(jnp.int32, (rows, LANES), 1)
    lhs_refs = (lhs_a, lhs_b, lhs_c, lhs_d)

    def gather(dy):
        for dz in range(near):
            for block in range(blocks):
                start = starts_ref[block, me_ref[0] ^ distance_of(sub_ref[0], dy, dz, near)]
                first = start >> 7
                shift = start & (LANES - 1)
                turn = (LANES - shift) & (LANES - 1)
                keep = lane < LANES - shift
                place = (dz * blocks + block) * rows

                def rolled(chunk):
                    line = samples_ref[first + chunk, block * rows : (block + 1) * rows, :]
                    return pltpu.roll(line, turn, 1)

                low = rolled(0)
                for chunk in range(chunks):
                    high = rolled(chunk + 1)
                    lhs_refs[dy][place : place + rows, chunk * LANES : (chunk + 1) * LANES] = jnp.where(
                        keep, low, high
                    )
                    low = high

    def correlate(dy):
        return lax.dot_general(
            lhs_refs[dy][...],
            toeplitz_ref[...],
            (((1,), (1,)), ((), ())),
            preferred_element_type=jnp.float32,
        )

    def cut(dy, product):
        for dz in range(near):
            for block in range(blocks):
                place = (dz * blocks + block) * rows
                real = product[place : place + half]
                imag = product[place + half : place + rows]
                for part, band in enumerate(
                    (real[:, :LANES] + imag[:, LANES:], imag[:, :LANES] - real[:, LANES:])
                ):
                    band = band.astype(jnp.bfloat16)
                    top = block * rows + part * half
                    if dy == 0:
                        top += blocks * count + dz * 2 * pulses
                        extra_ref[top : top + half, :] = band.astype(jnp.float32)
                    else:
                        bands_refs[dy - 1][dz, top : top + half, :] = band

    gather(0)
    for dy in range(len(lhs_refs)):
        if dy + 1 < len(lhs_refs):
            gather(dy + 1)
        cut(dy, correlate(dy))


FIRST_Z, FIRST_Y = (0, 3, 2, 1), (0, 2, 1, 3)
SECOND_Z, SECOND_Y = (0, 1, 3, 2), (0, 3, 2, 1)


def distance_of(sub, first, second, near):
    return jnp.where(
        (sub & 1) == 0,
        FIRST_Y[first] * near + SECOND_Z[second],
        SECOND_Y[second] * near + FIRST_Z[first],
    )


def sine_cosine(angle):
    turns = jnp.round(angle * np.float32(2 / np.pi))
    rest = (angle - turns * np.float32(1.5703125)) - turns * np.float32(np.pi / 2 - 1.5703125)
    quarter = turns.astype(jnp.int32)
    sq = rest * rest
    sine = np.float32(1 / 362880) * sq + np.float32(-1 / 5040)
    sine = sine * sq + np.float32(1 / 120)
    sine = sine * sq + np.float32(-1 / 6)
    sine = sine * sq * rest + rest
    cosine = np.float32(1 / 40320) * sq + np.float32(-1 / 720)
    cosine = cosine * sq + np.float32(1 / 24)
    cosine = cosine * sq + np.float32(-1 / 2)
    cosine = cosine * sq + np.float32(1)
    odd = (quarter & 1) == 1
    sin_out = jnp.where(odd, cosine, sine)
    cos_out = jnp.where(odd, sine, cosine)
    sin_out = jnp.where((quarter & 2) == 2, -sin_out, sin_out)
    cos_out = jnp.where(((quarter + 1) & 2) == 2, -cos_out, cos_out)
    return sin_out, cos_out


def phase_kernel(extra_ref, first_table_ref, second_table_ref, bands_ref):
    count = first_table_ref.shape[1] // 2
    bands_ref[...] = extra_ref[2 * count :].astype(jnp.bfloat16).reshape(bands_ref.shape)
    phase_table(0, extra_ref, first_table_ref)
    phase_table(1, extra_ref, second_table_ref)


def turn_kernel(weights_ref, after_ref, first_ref, second_ref):
    band = first_ref.shape[2]
    lines = first_ref.shape[1]
    size = 16
    side = size * size
    row = lax.broadcasted_iota(jnp.int32, (side, side), 0)
    col = lax.broadcasted_iota(jnp.int32, (side, side), 1)
    order = jnp.where(col == (row & (size - 1)) * size + (row >> 4), 1.0, 0.0).astype(jnp.bfloat16)
    for block, out_ref in enumerate((first_ref, second_ref)):
        for part in range(2):

            def step(chunk, carry, block=block, part=part, out_ref=out_ref):
                first = pl.multiple_of(chunk * size, size)
                for pair in range(lines // (2 * size)):
                    tops = [(2 * pair + one) * size for one in range(2)]
                    block_rows = jnp.concatenate(
                        [
                            weights_ref[
                                pl.ds((block * 2 + part) * band + first, size), top : top + size, :
                            ].reshape(side, LANES)
                            for top in tops
                        ],
                        1,
                    )
                    moved = jnp.dot(order, block_rows, preferred_element_type=jnp.float32)
                    for one, top in enumerate(tops):
                        out_ref[part, top : top + size, pl.ds(first, size), :] = moved[
                            :, one * LANES : (one + 1) * LANES
                        ].reshape(size, size, LANES)
                return carry

            lax.fori_loop(0, band // size, step, 0, unroll=True)


def phase_table(block, rate_ref, table_ref):
    count = table_ref.shape[1] // 2
    columns = table_ref.shape[0] * table_ref.shape[2]
    per_half = table_ref.shape[2] // LANES
    lane = lax.broadcasted_iota(jnp.int32, (32, LANES), 1).astype(jnp.float32)
    place = (lane + 0.5) * np.float32(1 / columns) - 0.5
    for group in range(count // 32):
        span = slice(group * 32, group * 32 + 32)
        rate = rate_ref[block * count + group * 32 : block * count + group * 32 + 32, :]
        sine, cosine = sine_cosine(rate * place)
        step_sine, step_cosine = sine_cosine(rate * np.float32(LANES / columns))
        for chunk in range(columns // LANES):
            if chunk > 0:
                sine, cosine = (
                    sine * step_cosine + cosine * step_sine,
                    cosine * step_cosine - sine * step_sine,
                )
            side, place_of = chunk // per_half, chunk % per_half
            lanes = slice(place_of * LANES, (place_of + 1) * LANES)
            table_ref[side, span, lanes] = cosine.astype(jnp.bfloat16)
            table_ref[side, count + group * 32 : count + group * 32 + 32, lanes] = sine.astype(
                jnp.bfloat16
            )


def relay_kernel(after_ref, *refs):
    near = refs[0].shape[0]
    far = len(refs) - near + 1
    for dz in range(1, near):
        for dy in range(far):
            refs[far + dz - 1][dy] = refs[dy][dz]


def weighted_sum(side, table_refs, weights_refs, image_ref, left_ref, focused_refs, partial_ref):
    blocks = len(table_refs)
    pairs, lines, _ = image_ref.shape
    places = 2 * pairs
    image_rows = lines // 4
    band = weights_refs[0].shape[2]
    for block in range(blocks):
        focused_refs[block][...] = jnp.dot(
            left_ref[block], table_refs[block][side], preferred_element_type=jnp.float32
        )
    for block in range(blocks):
        for place in range(places):
            lanes = slice(place * LANES, (place + 1) * LANES)
            if block == 0:
                sums = [jnp.zeros((8, LANES), jnp.float32)] * (2 * image_rows)
            else:
                sums = [partial_ref[place, one] for one in range(2 * image_rows)]
            for k in range(0, band, 8):
                fr = focused_refs[block][k : k + 8, lanes]
                fi = focused_refs[block][band + k : band + k + 8, lanes]
                for row in range(image_rows):
                    line = (side * places + place) * image_rows + row
                    wr = weights_refs[block][0, line, k : k + 8, :]
                    wi = weights_refs[block][1, line, k : k + 8, :]
                    sums[row] = sums[row] + (wr * fr - wi * fi)
                    sums[image_rows + row] = sums[image_rows + row] + (wr * fi + wi * fr)
            if block + 1 < blocks:
                for one in range(2 * image_rows):
                    partial_ref[place, one] = sums[one]
            else:
                rows = jnp.concatenate([jnp.sum(one, 0, keepdims=True) for one in sums], 0)
                if place % 2 == 0:
                    upper = rows
                else:
                    image_ref[place // 2] = jnp.concatenate([upper, rows], 0).astype(image_ref.dtype)


def far_image_kernel(
    me_ref, sub_ref, first_table_ref, second_table_ref, first_weights_ref, second_weights_ref, *rest
):
    *sources_refs, image_ref, left_ref, bands_ref, one_ref, two_ref, partial_ref = rest
    sources, band_rows, band = bands_ref.shape
    far_count = len(sources_refs) // 2 + 1
    near_refs, far_refs = sources_refs[:far_count], sources_refs[far_count:]
    near = sources // far_count
    blocks = left_ref.shape[0]
    rows = band_rows // blocks
    half = rows // 2
    count = sources * half
    for dy in range(far_count):
        bands_ref[me_ref[0] ^ distance_of(sub_ref[0], dy, 0, near)] = near_refs[dy][0]
        for dz in range(1, near):
            bands_ref[me_ref[0] ^ distance_of(sub_ref[0], dy, dz, near)] = far_refs[dz - 1][dy]
    for block in range(blocks):
        real = bands_ref[:, block * rows : block * rows + half, :].reshape(count, band)
        imag = bands_ref[:, block * rows + half : (block + 1) * rows, :].reshape(count, band)
        top = jnp.concatenate([real, imag], 1)
        bottom = jnp.concatenate([-imag, real], 1)
        left_ref[block] = jnp.concatenate([top, bottom], 0).T
    weighted_sum(
        1 - (sub_ref[0] >> 3),
        (first_table_ref, second_table_ref),
        (first_weights_ref, second_weights_ref),
        image_ref,
        left_ref,
        (one_ref, two_ref),
        partial_ref,
    )


def near_image_kernel(
    sub_ref, first_table_ref, second_table_ref, first_weights_ref, second_weights_ref, left_ref, after_ref,
    image_ref, one_ref, two_ref, partial_ref,
):
    weighted_sum(
        sub_ref[0] >> 3,
        (first_table_ref, second_table_ref),
        (first_weights_ref, second_weights_ref),
        image_ref,
        left_ref,
        (one_ref, two_ref),
        partial_ref,
    )


def params(mib):
    return pltpu.CompilerParams(vmem_limit_bytes=mib * 1024 * 1024)


def vmem():
    return pl.BlockSpec(memory_space=pltpu.VMEM)


def call(kernel, name, mib, out_shape, in_specs, scratch=(), flops=0):
    multiple = isinstance(out_shape, list)
    return pl.pallas_call(
        kernel,
        out_shape=out_shape,
        in_specs=in_specs,
        out_specs=[vmem()] * len(out_shape) if multiple else vmem(),
        scratch_shapes=list(scratch),
        compiler_params=params(mib),
        cost_estimate=pl.CostEstimate(flops=flops, bytes_accessed=0, transcendentals=0),
        name=name,
    )


def partial_image(echoes, chirp_ref, band_starts, doppler_rates, slot_pulse, interp_weights):
    pulses, _, pulse_len = echoes.shape
    chirp_len = chirp_ref.shape[1]
    blocks, tiles = band_starts.shape
    _, _, band, image_rows, columns = interp_weights.shape
    count = slot_pulse.shape[2]
    lines = 2 * pulse_len // LANES
    span = chirp_len + LANES
    places = columns // LANES
    parts = places // 2
    near = 4
    far = tiles // near
    smem = pl.BlockSpec(memory_space=pltpu.SMEM)
    anywhere = pl.BlockSpec(memory_space=pl.ANY)
    shape = jax.ShapeDtypeStruct
    sub = lax.axis_index("sub").astype(jnp.int32).reshape(1)
    me = lax.axis_index("tile").astype(jnp.int32).reshape(1)

    samples = echoes.reshape(pulses, 2, pulse_len // LANES, LANES).transpose(0, 2, 1, 3)
    samples = samples.reshape(pulses, lines, LANES)
    weights = interp_weights.reshape(blocks, 2, band, image_rows, places, LANES)
    weights = weights.transpose(0, 1, 2, 4, 3, 5).reshape(
        blocks * 2 * band, places * image_rows, LANES
    )
    own = shape((near, 2 * pulses, band), jnp.bfloat16)
    extras = shape((blocks * count + near * 2 * pulses, LANES), jnp.float32)
    *bands, extra = call(
        compress_kernel,
        "compress",
        60,
        [own] * (far - 1) + [extras],
        [smem] * 3 + [anywhere] * 4,
        [
            pltpu.VMEM((2, chirp_len), jnp.bfloat16),
            pltpu.VMEM((1, blocks * count), jnp.float32),
            pltpu.VMEM((blocks, count), jnp.int32),
            pltpu.VMEM((pulses, lines, LANES), jnp.bfloat16),
            pltpu.VMEM((lines // 2 + span // LANES, 2 * pulses, LANES), jnp.bfloat16),
            pltpu.VMEM((2 * LANES, span), jnp.bfloat16),
        ]
        + [pltpu.VMEM((near * 2 * pulses, span), jnp.bfloat16)] * far
        + [
            pltpu.SemaphoreType.DMA((4,)),
        ],
        flops=6 * 10**9,
    )(me, sub, band_starts, chirp_ref, doppler_rates, slot_pulse.reshape(blocks, count), samples)

    subs = lax.axis_size("sub")

    def swap(value, by_core):
        pairs = [
            (one * tiles + tile, one * tiles + (tile ^ by_core[1 - (one & 1)]))
            for one in range(subs)
            for tile in range(tiles)
        ]
        return lax.ppermute(value, ("sub", "tile"), pairs)

    table = shape((2, 2 * count, columns // 2), jnp.bfloat16)
    turned = shape((2, places * image_rows, band, LANES), jnp.float32)
    first_table, second_table, mine = call(phase_kernel, "phase", 12, [table, table, own], [vmem()], flops=4 * 10**9)(extra)
    bands = [mine] + [
        swap(bands[dy - 1], (FIRST_Z[dy], FIRST_Y[dy] * near)) for dy in range(1, far)
    ]
    passed = call(
        relay_kernel,
        "relay",
        16,
        [shape((far, 2 * pulses, band), jnp.bfloat16)] * (near - 1),
        [anywhere] + [vmem()] * far,
    )(first_table, *bands)
    first_weights, second_weights = call(turn_kernel, "turn", 12, [turned, turned], [vmem(), anywhere], flops=4 * 10**9)(
        weights, passed[0]
    )
    passed = [swap(passed[dz - 1], (SECOND_Y[dz] * near, SECOND_Z[dz])) for dz in range(1, near)]
    sources = bands + passed
    half = (places // 4, 4 * image_rows, LANES)
    focused = [pltpu.VMEM((2 * band, columns // 2), jnp.float32)] * blocks + [
        pltpu.VMEM((places // 2, 2 * image_rows, 8, LANES), jnp.float32)
    ]
    far_image, left = call(
        far_image_kernel,
        "far_image",
        12,
        [shape(half, jnp.bfloat16), shape((blocks, 2 * band, 2 * count), jnp.bfloat16)],
        [smem, smem] + [vmem()] * (4 + len(sources)),
        [pltpu.VMEM((tiles, 2 * pulses, band), jnp.bfloat16)] + focused,
        flops=3 * 10**9,
    )(me, sub, first_table, second_table, first_weights, second_weights, *sources)
    near_image = call(
        near_image_kernel, "near_image", 12, shape(half, jnp.float32), [smem] + [vmem()] * 5 + [anywhere], focused, flops=3 * 10**9
    )(sub, first_table, second_table, first_weights, second_weights, left, far_image)
    return sub, far_image, near_image


def shards(*args):
    _, far_image, near_image = partial_image(*args)
    size = 16
    half = size // 2
    came = lax.ppermute(far_image, "sub", [(one, one ^ half) for one in range(size)])
    groups = [list(range(half)), list(range(half, size))]
    held = (near_image + came.astype(jnp.float32)).reshape(half, -1, LANES)
    pieces = lax.all_to_all(held, "sub", 0, 0, axis_index_groups=groups, tiled=True)
    return jnp.sum(pieces, 0).reshape(2, -1, LANES)


def solution(mesh):
    in_specs = (
        P(("sub", "tile"), None, None),
        P(),
        P("sub", None),
        P("sub", None),
        P("sub", None, None),
        P("sub", None, None, "tile", None),
    )
    out_specs = P(None, "tile", "sub")
    return jax.shard_map(shards, mesh=mesh, in_specs=in_specs, out_specs=out_specs, check_vma=False)
```

```python
import jax
import jax.numpy as jnp
import numpy as np
from jax import lax
from jax.experimental import pallas as pl
from jax.experimental.pallas import tpu as pltpu
from jax.sharding import PartitionSpec as P

LANES = 128


def compress_kernel(
    me_ref, sub_ref, starts_ref, chirp_hbm, rates_hbm, slots_hbm, echoes_ref, *rest
):
    (
        *bands_refs, extra_ref, chirp_ref, rates_ref, slots_ref, raw_ref, samples_ref, toeplitz_ref,
        lhs_a, lhs_b, lhs_c, lhs_d, sems,
    ) = rest
    fetches = [
        pltpu.make_async_copy(source, target, sems.at[index])
        for index, (source, target) in enumerate(
            (
                (chirp_hbm, chirp_ref),
                (rates_hbm, rates_ref),
                (slots_hbm, slots_ref),
                (echoes_ref, raw_ref),
            )
        )
    ]
    for fetch in fetches:
        fetch.start()
    span = toeplitz_ref.shape[1]
    blocks, tiles = starts_ref.shape
    near = tiles // (len(bands_refs) + 1)
    pulses, lines, _ = raw_ref.shape
    half = pulses // blocks
    rows = 2 * half
    chunks = span // LANES
    samples_ref[lines // 2 :] = jnp.zeros(
        (samples_ref.shape[0] - lines // 2, 2 * pulses, LANES), jnp.bfloat16
    )
    piece = 16
    side = half * piece
    row = lax.broadcasted_iota(jnp.int32, (side, side), 0)
    col = lax.broadcasted_iota(jnp.int32, (side, side), 1)
    order = jnp.where(col == (row & (half - 1)) * piece + (row >> 4), 1.0, 0.0).astype(jnp.bfloat16)
    for fetch in fetches:
        fetch.wait()
    chirp = chirp_ref[...].astype(jnp.float32)
    pad = jnp.zeros((1, span - chirp.shape[1]), jnp.float32)
    for part in range(2):
        line = jnp.concatenate([chirp[part : part + 1], pad], 1)
        shifted = pltpu.roll(
            jnp.broadcast_to(line, (LANES, span)), 0, 1, stride=1, stride_axis=0
        ).astype(jnp.bfloat16)
        toeplitz_ref[part * LANES : (part + 1) * LANES, :] = shifted
    count = slots_ref.shape[1]
    row = lax.broadcasted_iota(jnp.int32, (count, count), 0)
    col = lax.broadcasted_iota(jnp.int32, (count, count), 1)
    for block in range(blocks):
        slots = slots_ref[block : block + 1, :].astype(jnp.float32)
        slot = jnp.sum(jnp.where(row == col, slots, 0.0), 1, keepdims=True)
        rates = rates_ref[:, block * count : (block + 1) * count]
        rate = jnp.sum(jnp.where(slot == col.astype(jnp.float32), rates, 0.0), 1, keepdims=True)
        extra_ref[block * count : (block + 1) * count, :] = jnp.broadcast_to(rate, (count, LANES))
    for group in range(lines // piece):
        block_rows = jnp.concatenate(
            [
                raw_ref[block * half : (block + 1) * half, group * piece : (group + 1) * piece, :].reshape(
                    side, LANES
                )
                for block in range(blocks)
            ],
            1,
        )
        moved = jnp.dot(order, block_rows, preferred_element_type=jnp.float32).astype(jnp.bfloat16)
        for block in range(blocks):
            samples_ref[
                group * piece // 2 : (group + 1) * piece // 2, block * rows : (block + 1) * rows, :
            ] = moved[:, block * LANES : (block + 1) * LANES].reshape(piece // 2, rows, LANES)
    lane = lax.broadcasted_iota(jnp.int32, (rows, LANES), 1)
    lhs_refs = (lhs_a, lhs_b, lhs_c, lhs_d)

    def gather(dy):
        for dz in range(near):
            for block in range(blocks):
                start = starts_ref[block, me_ref[0] ^ distance_of(sub_ref[0], dy, dz, near)]
                first = start >> 7
                shift = start & (LANES - 1)
                turn = (LANES - shift) & (LANES - 1)
                keep = lane < LANES - shift
                place = (dz * blocks + block) * rows

                def rolled(chunk):
                    line = samples_ref[first + chunk, block * rows : (block + 1) * rows, :]
                    return pltpu.roll(line, turn, 1)

                low = rolled(0)
                for chunk in range(chunks):
                    high = rolled(chunk + 1)
                    lhs_refs[dy][place : place + rows, chunk * LANES : (chunk + 1) * LANES] = jnp.where(
                        keep, low, high
                    )
                    low = high

    def correlate(dy):
        return lax.dot_general(
            lhs_refs[dy][...],
            toeplitz_ref[...],
            (((1,), (1,)), ((), ())),
            preferred_element_type=jnp.float32,
        )

    def cut(dy, product):
        for dz in range(near):
            for block in range(blocks):
                place = (dz * blocks + block) * rows
                real = product[place : place + half]
                imag = product[place + half : place + rows]
                for part, band in enumerate(
                    (real[:, :LANES] + imag[:, LANES:], imag[:, :LANES] - real[:, LANES:])
                ):
                    band = band.astype(jnp.bfloat16)
                    top = block * rows + part * half
                    if dy == 0:
                        top += blocks * count + dz * 2 * pulses
                        extra_ref[top : top + half, :] = band.astype(jnp.float32)
                    else:
                        bands_refs[dy - 1][dz, top : top + half, :] = band

    gather(0)
    for dy in range(len(lhs_refs)):
        if dy + 1 < len(lhs_refs):
            gather(dy + 1)
        cut(dy, correlate(dy))


FIRST_Z, FIRST_Y = (0, 3, 2, 1), (0, 2, 1, 3)
SECOND_Z, SECOND_Y = (0, 1, 3, 2), (0, 3, 2, 1)


def distance_of(sub, first, second, near):
    return jnp.where(
        (sub & 1) == 0,
        FIRST_Y[first] * near + SECOND_Z[second],
        SECOND_Y[second] * near + FIRST_Z[first],
    )


def sine_cosine(angle):
    turns = jnp.round(angle * np.float32(2 / np.pi))
    rest = (angle - turns * np.float32(1.5703125)) - turns * np.float32(np.pi / 2 - 1.5703125)
    quarter = turns.astype(jnp.int32)
    sq = rest * rest
    sine = np.float32(1 / 362880) * sq + np.float32(-1 / 5040)
    sine = sine * sq + np.float32(1 / 120)
    sine = sine * sq + np.float32(-1 / 6)
    sine = sine * sq * rest + rest
    cosine = np.float32(1 / 40320) * sq + np.float32(-1 / 720)
    cosine = cosine * sq + np.float32(1 / 24)
    cosine = cosine * sq + np.float32(-1 / 2)
    cosine = cosine * sq + np.float32(1)
    odd = (quarter & 1) == 1
    sin_out = jnp.where(odd, cosine, sine)
    cos_out = jnp.where(odd, sine, cosine)
    sin_out = jnp.where((quarter & 2) == 2, -sin_out, sin_out)
    cos_out = jnp.where(((quarter + 1) & 2) == 2, -cos_out, cos_out)
    return sin_out, cos_out


def phase_kernel(extra_ref, first_table_ref, second_table_ref, bands_ref):
    count = first_table_ref.shape[1] // 2
    bands_ref[...] = extra_ref[2 * count :].astype(jnp.bfloat16).reshape(bands_ref.shape)
    phase_table(0, extra_ref, first_table_ref)
    phase_table(1, extra_ref, second_table_ref)


def turn_kernel(weights_ref, after_ref, first_ref, second_ref):
    band = first_ref.shape[2]
    lines = first_ref.shape[1]
    size = 16
    side = size * size
    row = lax.broadcasted_iota(jnp.int32, (side, side), 0)
    col = lax.broadcasted_iota(jnp.int32, (side, side), 1)
    order = jnp.where(col == (row & (size - 1)) * size + (row >> 4), 1.0, 0.0).astype(jnp.bfloat16)
    for block, out_ref in enumerate((first_ref, second_ref)):
        for part in range(2):

            def step(chunk, carry, block=block, part=part, out_ref=out_ref):
                first = pl.multiple_of(chunk * size, size)
                for pair in range(lines // (2 * size)):
                    tops = [(2 * pair + one) * size for one in range(2)]
                    block_rows = jnp.concatenate(
                        [
                            weights_ref[
                                pl.ds((block * 2 + part) * band + first, size), top : top + size, :
                            ].reshape(side, LANES)
                            for top in tops
                        ],
                        1,
                    )
                    moved = jnp.dot(order, block_rows, preferred_element_type=jnp.float32)
                    for one, top in enumerate(tops):
                        out_ref[part, top : top + size, pl.ds(first, size), :] = moved[
                            :, one * LANES : (one + 1) * LANES
                        ].reshape(size, size, LANES)
                return carry

            lax.fori_loop(0, band // size, step, 0, unroll=True)


def phase_table(block, rate_ref, table_ref):
    count = table_ref.shape[1] // 2
    columns = table_ref.shape[0] * table_ref.shape[2]
    lane = lax.broadcasted_iota(jnp.int32, (32, LANES), 1).astype(jnp.float32)
    place = (lane + 0.5) * np.float32(1 / columns) - 0.5
    for group in range(count // 32):
        span = slice(group * 32, group * 32 + 32)
        rate = rate_ref[block * count + group * 32 : block * count + group * 32 + 32, :]
        sine, cosine = sine_cosine(rate * place)
        step_sine, step_cosine = sine_cosine(rate * np.float32(LANES / columns))
        for chunk in range(columns // LANES):
            if chunk > 0:
                sine, cosine = (
                    sine * step_cosine + cosine * step_sine,
                    cosine * step_cosine - sine * step_sine,
                )
            side, place_of = chunk % 2, chunk // 2
            lanes = slice(place_of * LANES, (place_of + 1) * LANES)
            table_ref[side, span, lanes] = cosine.astype(jnp.bfloat16)
            table_ref[side, count + group * 32 : count + group * 32 + 32, lanes] = sine.astype(
                jnp.bfloat16
            )


def relay_kernel(after_ref, *refs):
    near = refs[0].shape[0]
    far = len(refs) - near + 1
    for dz in range(1, near):
        for dy in range(far):
            refs[far + dz - 1][dy] = refs[dy][dz]


def weighted_sum(side, table_refs, weights_refs, image_ref, left_ref, focused_refs, partial_ref):
    blocks = len(table_refs)
    pairs, lines, _ = image_ref.shape
    places = 2 * pairs
    image_rows = lines // 4
    band = weights_refs[0].shape[2]
    for block in range(blocks):
        focused_refs[block][...] = jnp.dot(
            left_ref[block], table_refs[block][side], preferred_element_type=jnp.float32
        )
    for block in range(blocks):
        for place in range(places):
            lanes = slice(place * LANES, (place + 1) * LANES)
            if block == 0:
                sums = [jnp.zeros((8, LANES), jnp.float32)] * (2 * image_rows)
            else:
                sums = [partial_ref[place, one] for one in range(2 * image_rows)]
            for k in range(0, band, 8):
                fr = focused_refs[block][k : k + 8, lanes]
                fi = focused_refs[block][band + k : band + k + 8, lanes]
                for row in range(image_rows):
                    line = (2 * place + side) * image_rows + row
                    wr = weights_refs[block][0, line, k : k + 8, :]
                    wi = weights_refs[block][1, line, k : k + 8, :]
                    sums[row] = sums[row] + (wr * fr - wi * fi)
                    sums[image_rows + row] = sums[image_rows + row] + (wr * fi + wi * fr)
            if block + 1 < blocks:
                for one in range(2 * image_rows):
                    partial_ref[place, one] = sums[one]
            else:
                rows = jnp.concatenate([jnp.sum(one, 0, keepdims=True) for one in sums], 0)
                if place % 2 == 0:
                    upper = rows
                else:
                    image_ref[place // 2] = jnp.concatenate([upper, rows], 0).astype(image_ref.dtype)


def far_image_kernel(
    me_ref, sub_ref, first_table_ref, second_table_ref, first_weights_ref, second_weights_ref, *rest
):
    *sources_refs, image_ref, left_ref, bands_ref, one_ref, two_ref, partial_ref = rest
    sources, band_rows, band = bands_ref.shape
    far_count = len(sources_refs) // 2 + 1
    near_refs, far_refs = sources_refs[:far_count], sources_refs[far_count:]
    near = sources // far_count
    blocks = left_ref.shape[0]
    rows = band_rows // blocks
    half = rows // 2
    count = sources * half
    for dy in range(far_count):
        bands_ref[me_ref[0] ^ distance_of(sub_ref[0], dy, 0, near)] = near_refs[dy][0]
        for dz in range(1, near):
            bands_ref[me_ref[0] ^ distance_of(sub_ref[0], dy, dz, near)] = far_refs[dz - 1][dy]
    for block in range(blocks):
        real = bands_ref[:, block * rows : block * rows + half, :].reshape(count, band)
        imag = bands_ref[:, block * rows + half : (block + 1) * rows, :].reshape(count, band)
        top = jnp.concatenate([real, imag], 1)
        bottom = jnp.concatenate([-imag, real], 1)
        left_ref[block] = jnp.concatenate([top, bottom], 0).T
    weighted_sum(
        1 - (sub_ref[0] & 1),
        (first_table_ref, second_table_ref),
        (first_weights_ref, second_weights_ref),
        image_ref,
        left_ref,
        (one_ref, two_ref),
        partial_ref,
    )


def near_image_kernel(
    sub_ref, first_table_ref, second_table_ref, first_weights_ref, second_weights_ref, left_ref, after_ref,
    image_ref, one_ref, two_ref, partial_ref,
):
    weighted_sum(
        sub_ref[0] & 1,
        (first_table_ref, second_table_ref),
        (first_weights_ref, second_weights_ref),
        image_ref,
        left_ref,
        (one_ref, two_ref),
        partial_ref,
    )


def params(mib):
    return pltpu.CompilerParams(vmem_limit_bytes=mib * 1024 * 1024)


def vmem():
    return pl.BlockSpec(memory_space=pltpu.VMEM)


def call(kernel, name, mib, out_shape, in_specs, scratch=(), flops=0):
    multiple = isinstance(out_shape, list)
    return pl.pallas_call(
        kernel,
        out_shape=out_shape,
        in_specs=in_specs,
        out_specs=[vmem()] * len(out_shape) if multiple else vmem(),
        scratch_shapes=list(scratch),
        compiler_params=params(mib),
        cost_estimate=pl.CostEstimate(flops=flops, bytes_accessed=0, transcendentals=0),
        name=name,
    )


def partial_image(echoes, chirp_ref, band_starts, doppler_rates, slot_pulse, interp_weights):
    pulses, _, pulse_len = echoes.shape
    chirp_len = chirp_ref.shape[1]
    blocks, tiles = band_starts.shape
    _, _, band, image_rows, columns = interp_weights.shape
    count = slot_pulse.shape[2]
    lines = 2 * pulse_len // LANES
    span = chirp_len + LANES
    places = columns // LANES
    parts = places // 2
    near = 4
    far = tiles // near
    smem = pl.BlockSpec(memory_space=pltpu.SMEM)
    anywhere = pl.BlockSpec(memory_space=pl.ANY)
    shape = jax.ShapeDtypeStruct
    sub = lax.axis_index("sub").astype(jnp.int32).reshape(1)
    me = lax.axis_index("tile").astype(jnp.int32).reshape(1)

    samples = echoes.reshape(pulses, 2, pulse_len // LANES, LANES).transpose(0, 2, 1, 3)
    samples = samples.reshape(pulses, lines, LANES)
    weights = interp_weights.reshape(blocks, 2, band, image_rows, places, LANES)
    weights = weights.transpose(0, 1, 2, 4, 3, 5).reshape(
        blocks * 2 * band, places * image_rows, LANES
    )
    own = shape((near, 2 * pulses, band), jnp.bfloat16)
    extras = shape((blocks * count + near * 2 * pulses, LANES), jnp.float32)
    *bands, extra = call(
        compress_kernel,
        "compress",
        60,
        [own] * (far - 1) + [extras],
        [smem] * 3 + [anywhere] * 4,
        [
            pltpu.VMEM((2, chirp_len), jnp.bfloat16),
            pltpu.VMEM((1, blocks * count), jnp.float32),
            pltpu.VMEM((blocks, count), jnp.int32),
            pltpu.VMEM((pulses, lines, LANES), jnp.bfloat16),
            pltpu.VMEM((lines // 2 + span // LANES, 2 * pulses, LANES), jnp.bfloat16),
            pltpu.VMEM((2 * LANES, span), jnp.bfloat16),
        ]
        + [pltpu.VMEM((near * 2 * pulses, span), jnp.bfloat16)] * far
        + [
            pltpu.SemaphoreType.DMA((4,)),
        ],
        flops=6 * 10**9,
    )(me, sub, band_starts, chirp_ref, doppler_rates, slot_pulse.reshape(blocks, count), samples)

    subs = lax.axis_size("sub")

    def swap(value, by_core):
        pairs = [
            (one * tiles + tile, one * tiles + (tile ^ by_core[1 - (one & 1)]))
            for one in range(subs)
            for tile in range(tiles)
        ]
        return lax.ppermute(value, ("sub", "tile"), pairs)

    table = shape((2, 2 * count, columns // 2), jnp.bfloat16)
    turned = shape((2, places * image_rows, band, LANES), jnp.float32)
    first_table, second_table, mine = call(phase_kernel, "phase", 12, [table, table, own], [vmem()], flops=4 * 10**9)(extra)
    bands = [mine] + [
        swap(bands[dy - 1], (FIRST_Z[dy], FIRST_Y[dy] * near)) for dy in range(1, far)
    ]
    passed = call(
        relay_kernel,
        "relay",
        16,
        [shape((far, 2 * pulses, band), jnp.bfloat16)] * (near - 1),
        [anywhere] + [vmem()] * far,
    )(first_table, *bands)
    first_weights, second_weights = call(turn_kernel, "turn", 12, [turned, turned], [vmem(), anywhere], flops=4 * 10**9)(
        weights, passed[0]
    )
    passed = [swap(passed[dz - 1], (SECOND_Y[dz] * near, SECOND_Z[dz])) for dz in range(1, near)]
    sources = bands + passed
    half = (places // 4, 4 * image_rows, LANES)
    focused = [pltpu.VMEM((2 * band, columns // 2), jnp.float32)] * blocks + [
        pltpu.VMEM((places // 2, 2 * image_rows, 8, LANES), jnp.float32)
    ]
    far_image, left = call(
        far_image_kernel,
        "far_image",
        12,
        [shape(half, jnp.float32), shape((blocks, 2 * band, 2 * count), jnp.bfloat16)],
        [smem, smem] + [vmem()] * (4 + len(sources)),
        [pltpu.VMEM((tiles, 2 * pulses, band), jnp.bfloat16)] + focused,
        flops=3 * 10**9,
    )(me, sub, first_table, second_table, first_weights, second_weights, *sources)
    near_image = call(
        near_image_kernel, "near_image", 12, shape(half, jnp.float32), [smem] + [vmem()] * 5 + [anywhere], focused, flops=3 * 10**9
    )(sub, first_table, second_table, first_weights, second_weights, left, far_image)
    return sub, far_image, near_image


def shards(*args):
    _, far_image, near_image = partial_image(*args)
    size = 16
    half = size // 2
    came = lax.ppermute(far_image, "sub", [(one, one ^ 1) for one in range(size)])
    groups = [list(range(0, size, 2)), list(range(1, size, 2))]
    held = (near_image + came).reshape(half, -1, LANES)
    pieces = lax.all_to_all(held, "sub", 0, 0, axis_index_groups=groups, tiled=True)
    return jnp.sum(pieces, 0).reshape(2, -1, LANES)


def solution(mesh):
    in_specs = (
        P(("sub", "tile"), None, None),
        P(),
        P("sub", None),
        P("sub", None),
        P("sub", None, None),
        P("sub", None, None, "tile", None),
    )
    out_specs = P(None, "tile", "sub")
    return jax.shard_map(shards, mesh=mesh, in_specs=in_specs, out_specs=out_specs, check_vma=False)
```

```python
import jax
import jax.numpy as jnp
import numpy as np
from jax import lax
from jax.experimental import pallas as pl
from jax.experimental.pallas import tpu as pltpu
from jax.sharding import PartitionSpec as P

LANES = 128


def compress_kernel(
    me_ref, sub_ref, starts_ref, chirp_hbm, rates_hbm, slots_hbm, echoes_ref, *rest
):
    (
        *bands_refs, extra_ref, chirp_ref, rates_ref, slots_ref, raw_ref, samples_ref, toeplitz_ref,
        lhs_a, lhs_b, lhs_c, lhs_d, sems,
    ) = rest
    fetches = [
        pltpu.make_async_copy(source, target, sems.at[index])
        for index, (source, target) in enumerate(
            (
                (chirp_hbm, chirp_ref),
                (rates_hbm, rates_ref),
                (slots_hbm, slots_ref),
                (echoes_ref, raw_ref),
            )
        )
    ]
    for fetch in fetches:
        fetch.start()
    span = toeplitz_ref.shape[1]
    blocks, tiles = starts_ref.shape
    near = tiles // (len(bands_refs) + 1)
    pulses, lines, _ = raw_ref.shape
    half = pulses // blocks
    rows = 2 * half
    chunks = span // LANES
    samples_ref[lines // 2 :] = jnp.zeros(
        (samples_ref.shape[0] - lines // 2, 2 * pulses, LANES), jnp.bfloat16
    )
    piece = 16
    side = half * piece
    row = lax.broadcasted_iota(jnp.int32, (side, side), 0)
    col = lax.broadcasted_iota(jnp.int32, (side, side), 1)
    order = jnp.where(col == (row & (half - 1)) * piece + (row >> 4), 1.0, 0.0).astype(jnp.bfloat16)
    for fetch in fetches:
        fetch.wait()
    chirp = chirp_ref[...].astype(jnp.float32)
    pad = jnp.zeros((1, span - chirp.shape[1]), jnp.float32)
    for part in range(2):
        line = jnp.concatenate([chirp[part : part + 1], pad], 1)
        shifted = pltpu.roll(
            jnp.broadcast_to(line, (LANES, span)), 0, 1, stride=1, stride_axis=0
        ).astype(jnp.bfloat16)
        toeplitz_ref[part * LANES : (part + 1) * LANES, :] = shifted
    count = slots_ref.shape[1]
    row = lax.broadcasted_iota(jnp.int32, (count, count), 0)
    col = lax.broadcasted_iota(jnp.int32, (count, count), 1)
    for block in range(blocks):
        slots = slots_ref[block : block + 1, :].astype(jnp.float32)
        slot = jnp.sum(jnp.where(row == col, slots, 0.0), 1, keepdims=True)
        rates = rates_ref[:, block * count : (block + 1) * count]
        rate = jnp.sum(jnp.where(slot == col.astype(jnp.float32), rates, 0.0), 1, keepdims=True)
        extra_ref[block * count : (block + 1) * count, :] = jnp.broadcast_to(rate, (count, LANES))
    for group in range(lines // piece):
        block_rows = jnp.concatenate(
            [
                raw_ref[block * half : (block + 1) * half, group * piece : (group + 1) * piece, :].reshape(
                    side, LANES
                )
                for block in range(blocks)
            ],
            1,
        )
        moved = jnp.dot(order, block_rows, preferred_element_type=jnp.float32).astype(jnp.bfloat16)
        for block in range(blocks):
            samples_ref[
                group * piece // 2 : (group + 1) * piece // 2, block * rows : (block + 1) * rows, :
            ] = moved[:, block * LANES : (block + 1) * LANES].reshape(piece // 2, rows, LANES)
    lane = lax.broadcasted_iota(jnp.int32, (rows, LANES), 1)
    lhs_refs = (lhs_a, lhs_b, lhs_c, lhs_d)

    def gather(dy):
        for dz in range(near):
            for block in range(blocks):
                start = starts_ref[block, me_ref[0] ^ distance_of(sub_ref[0], dy, dz, near)]
                first = start >> 7
                shift = start & (LANES - 1)
                turn = (LANES - shift) & (LANES - 1)
                keep = lane < LANES - shift
                place = (dz * blocks + block) * rows

                def rolled(chunk):
                    line = samples_ref[first + chunk, block * rows : (block + 1) * rows, :]
                    return pltpu.roll(line, turn, 1)

                low = rolled(0)
                for chunk in range(chunks):
                    high = rolled(chunk + 1)
                    lhs_refs[dy][place : place + rows, chunk * LANES : (chunk + 1) * LANES] = jnp.where(
                        keep, low, high
                    )
                    low = high

    def correlate(dy):
        return lax.dot_general(
            lhs_refs[dy][...],
            toeplitz_ref[...],
            (((1,), (1,)), ((), ())),
            preferred_element_type=jnp.float32,
        )

    def cut(dy, product):
        for dz in range(near):
            for block in range(blocks):
                place = (dz * blocks + block) * rows
                real = product[place : place + half]
                imag = product[place + half : place + rows]
                for part, band in enumerate(
                    (real[:, :LANES] + imag[:, LANES:], imag[:, :LANES] - real[:, LANES:])
                ):
                    band = band.astype(jnp.bfloat16)
                    top = block * rows + part * half
                    if dy == 0:
                        top += blocks * count + dz * 2 * pulses
                        extra_ref[top : top + half, :] = band.astype(jnp.float32)
                    else:
                        bands_refs[dy - 1][dz, top : top + half, :] = band

    gather(0)
    for dy in range(len(lhs_refs)):
        if dy + 1 < len(lhs_refs):
            gather(dy + 1)
        cut(dy, correlate(dy))


FIRST_Z, FIRST_Y = (0, 3, 2, 1), (0, 2, 1, 3)
SECOND_Z, SECOND_Y = (0, 1, 3, 2), (0, 3, 2, 1)


def distance_of(sub, first, second, near):
    return jnp.where(
        (sub & 1) == 0,
        FIRST_Y[first] * near + SECOND_Z[second],
        SECOND_Y[second] * near + FIRST_Z[first],
    )


def sine_cosine(angle):
    turns = jnp.round(angle * np.float32(2 / np.pi))
    rest = (angle - turns * np.float32(1.5703125)) - turns * np.float32(np.pi / 2 - 1.5703125)
    quarter = turns.astype(jnp.int32)
    sq = rest * rest
    sine = np.float32(1 / 362880) * sq + np.float32(-1 / 5040)
    sine = sine * sq + np.float32(1 / 120)
    sine = sine * sq + np.float32(-1 / 6)
    sine = sine * sq * rest + rest
    cosine = np.float32(1 / 40320) * sq + np.float32(-1 / 720)
    cosine = cosine * sq + np.float32(1 / 24)
    cosine = cosine * sq + np.float32(-1 / 2)
    cosine = cosine * sq + np.float32(1)
    odd = (quarter & 1) == 1
    sin_out = jnp.where(odd, cosine, sine)
    cos_out = jnp.where(odd, sine, cosine)
    sin_out = jnp.where((quarter & 2) == 2, -sin_out, sin_out)
    cos_out = jnp.where(((quarter + 1) & 2) == 2, -cos_out, cos_out)
    return sin_out, cos_out


def phase_kernel(extra_ref, first_table_ref, second_table_ref, bands_ref):
    count = first_table_ref.shape[1] // 2
    bands_ref[...] = extra_ref[2 * count :].astype(jnp.bfloat16).reshape(bands_ref.shape)
    phase_table(0, extra_ref, first_table_ref)
    phase_table(1, extra_ref, second_table_ref)


def turn_kernel(weights_ref, after_ref, first_ref, second_ref):
    band = first_ref.shape[2]
    lines = first_ref.shape[1]
    size = 16
    side = size * size
    row = lax.broadcasted_iota(jnp.int32, (side, side), 0)
    col = lax.broadcasted_iota(jnp.int32, (side, side), 1)
    order = jnp.where(col == (row & (size - 1)) * size + (row >> 4), 1.0, 0.0).astype(jnp.bfloat16)
    for block, out_ref in enumerate((first_ref, second_ref)):
        for part in range(2):

            def step(chunk, carry, block=block, part=part, out_ref=out_ref):
                first = pl.multiple_of(chunk * size, size)
                for pair in range(lines // (2 * size)):
                    tops = [(2 * pair + one) * size for one in range(2)]
                    block_rows = jnp.concatenate(
                        [
                            weights_ref[
                                pl.ds((block * 2 + part) * band + first, size), top : top + size, :
                            ].reshape(side, LANES)
                            for top in tops
                        ],
                        1,
                    )
                    moved = jnp.dot(order, block_rows, preferred_element_type=jnp.float32).astype(
                        jnp.bfloat16
                    )
                    for one, top in enumerate(tops):
                        out_ref[part, top : top + size, pl.ds(first, size), :] = moved[
                            :, one * LANES : (one + 1) * LANES
                        ].reshape(size, size, LANES)
                return carry

            lax.fori_loop(0, band // size, step, 0, unroll=True)


def phase_table(block, rate_ref, table_ref):
    count = table_ref.shape[1] // 2
    columns = table_ref.shape[0] * table_ref.shape[2]
    lane = lax.broadcasted_iota(jnp.int32, (32, LANES), 1).astype(jnp.float32)
    place = (lane + 0.5) * np.float32(1 / columns) - 0.5
    for group in range(count // 32):
        span = slice(group * 32, group * 32 + 32)
        rate = rate_ref[block * count + group * 32 : block * count + group * 32 + 32, :]
        sine, cosine = sine_cosine(rate * place)
        step_sine, step_cosine = sine_cosine(rate * np.float32(LANES / columns))
        for chunk in range(columns // LANES):
            if chunk > 0:
                sine, cosine = (
                    sine * step_cosine + cosine * step_sine,
                    cosine * step_cosine - sine * step_sine,
                )
            lanes = slice(chunk % 2 * LANES, (chunk % 2 + 1) * LANES)
            table_ref[chunk // 2, span, lanes] = cosine.astype(jnp.bfloat16)
            table_ref[chunk // 2, count + group * 32 : count + group * 32 + 32, lanes] = (
                sine.astype(jnp.bfloat16)
            )


def relay_kernel(after_ref, *refs):
    near = refs[0].shape[0]
    far = len(refs) - near + 1
    for dz in range(1, near):
        for dy in range(far):
            refs[far + dz - 1][dy] = refs[dy][dz]


def fold_rows(values):
    row = lax.broadcasted_iota(jnp.int32, values[0].shape, 0)
    shift = 1
    while len(values) > 1:
        low = (row & shift) == 0
        values = [
            jnp.where(low, first, second) + pltpu.roll(jnp.where(low, second, first), 8 - shift, 0)
            for first, second in zip(values[::2], values[1::2])
        ]
        shift *= 2
    return values[0]


def weighted_sum(side, table_refs, weights_refs, image_ref, left_ref, focused_refs):
    blocks = len(table_refs)
    pairs, lines, _ = image_ref.shape
    places = 2 * pairs
    image_rows = lines // 4
    band = weights_refs[0].shape[2]

    def focus(pair):
        for block in range(blocks):
            focused_refs[pair % 2 * blocks + block][...] = jnp.dot(
                left_ref[block], table_refs[block][side * pairs + pair], preferred_element_type=jnp.float32
            )

    focus(0)
    for pair in range(pairs):
        if pair + 1 < pairs:
            focus(pair + 1)
        sums = []
        for place in range(2):
            lanes = slice(place * LANES, (place + 1) * LANES)
            real = [jnp.zeros((8, LANES), jnp.float32)] * image_rows
            imag = [jnp.zeros((8, LANES), jnp.float32)] * image_rows
            for block in range(blocks):
                focused_ref = focused_refs[pair % 2 * blocks + block]
                for k in range(0, band, 16):
                    focus_real = focused_ref[k : k + 16, lanes]
                    focus_imag = focused_ref[band + k : band + k + 16, lanes]
                    for row in range(image_rows):
                        line = (side * places + 2 * pair + place) * image_rows + row
                        weight_real = weights_refs[block][0, line, k : k + 16, :].astype(jnp.float32)
                        weight_imag = weights_refs[block][1, line, k : k + 16, :].astype(jnp.float32)
                        for first in (0, 8):
                            part = slice(first, first + 8)
                            wr, wi = weight_real[part], weight_imag[part]
                            fr, fi = focus_real[part], focus_imag[part]
                            real[row] = real[row] + (wr * fr - wi * fi)
                            imag[row] = imag[row] + (wr * fi + wi * fr)
            sums.append(fold_rows(real + imag))
        image_ref[pair] = jnp.concatenate(sums, 0).astype(image_ref.dtype)


def far_image_kernel(
    me_ref, sub_ref, first_table_ref, second_table_ref, first_weights_ref, second_weights_ref, *rest
):
    *sources_refs, image_ref, left_ref, bands_ref, one_ref, two_ref, three_ref, four_ref = rest
    sources, band_rows, band = bands_ref.shape
    far_count = len(sources_refs) // 2 + 1
    near_refs, far_refs = sources_refs[:far_count], sources_refs[far_count:]
    near = sources // far_count
    blocks = left_ref.shape[0]
    rows = band_rows // blocks
    half = rows // 2
    count = sources * half
    for dy in range(far_count):
        bands_ref[me_ref[0] ^ distance_of(sub_ref[0], dy, 0, near)] = near_refs[dy][0]
        for dz in range(1, near):
            bands_ref[me_ref[0] ^ distance_of(sub_ref[0], dy, dz, near)] = far_refs[dz - 1][dy]
    for block in range(blocks):
        real = bands_ref[:, block * rows : block * rows + half, :].reshape(count, band)
        imag = bands_ref[:, block * rows + half : (block + 1) * rows, :].reshape(count, band)
        top = jnp.concatenate([real, imag], 1)
        bottom = jnp.concatenate([-imag, real], 1)
        left_ref[block] = jnp.concatenate([top, bottom], 0).T
    weighted_sum(
        1 - (sub_ref[0] >> 3),
        (first_table_ref, second_table_ref),
        (first_weights_ref, second_weights_ref),
        image_ref,
        left_ref,
        (one_ref, two_ref, three_ref, four_ref),
    )


def near_image_kernel(
    sub_ref, first_table_ref, second_table_ref, first_weights_ref, second_weights_ref, left_ref, after_ref,
    image_ref, one_ref, two_ref, three_ref, four_ref,
):
    weighted_sum(
        sub_ref[0] >> 3,
        (first_table_ref, second_table_ref),
        (first_weights_ref, second_weights_ref),
        image_ref,
        left_ref,
        (one_ref, two_ref, three_ref, four_ref),
    )


def params(mib):
    return pltpu.CompilerParams(vmem_limit_bytes=mib * 1024 * 1024)


def vmem():
    return pl.BlockSpec(memory_space=pltpu.VMEM)


def call(kernel, name, mib, out_shape, in_specs, scratch=(), flops=0):
    multiple = isinstance(out_shape, list)
    return pl.pallas_call(
        kernel,
        out_shape=out_shape,
        in_specs=in_specs,
        out_specs=[vmem()] * len(out_shape) if multiple else vmem(),
        scratch_shapes=list(scratch),
        compiler_params=params(mib),
        cost_estimate=pl.CostEstimate(flops=flops, bytes_accessed=0, transcendentals=0),
        name=name,
    )


def partial_image(echoes, chirp_ref, band_starts, doppler_rates, slot_pulse, interp_weights):
    pulses, _, pulse_len = echoes.shape
    chirp_len = chirp_ref.shape[1]
    blocks, tiles = band_starts.shape
    _, _, band, image_rows, columns = interp_weights.shape
    count = slot_pulse.shape[2]
    lines = 2 * pulse_len // LANES
    span = chirp_len + LANES
    places = columns // LANES
    parts = places // 2
    near = 4
    far = tiles // near
    smem = pl.BlockSpec(memory_space=pltpu.SMEM)
    anywhere = pl.BlockSpec(memory_space=pl.ANY)
    shape = jax.ShapeDtypeStruct
    sub = lax.axis_index("sub").astype(jnp.int32).reshape(1)
    me = lax.axis_index("tile").astype(jnp.int32).reshape(1)

    samples = echoes.reshape(pulses, 2, pulse_len // LANES, LANES).transpose(0, 2, 1, 3)
    samples = samples.reshape(pulses, lines, LANES)
    weights = interp_weights.reshape(blocks, 2, band, image_rows, places, LANES)
    weights = weights.transpose(0, 1, 2, 4, 3, 5).reshape(
        blocks * 2 * band, places * image_rows, LANES
    )
    own = shape((near, 2 * pulses, band), jnp.bfloat16)
    extras = shape((blocks * count + near * 2 * pulses, LANES), jnp.float32)
    *bands, extra = call(
        compress_kernel,
        "compress",
        60,
        [own] * (far - 1) + [extras],
        [smem] * 3 + [anywhere] * 4,
        [
            pltpu.VMEM((2, chirp_len), jnp.bfloat16),
            pltpu.VMEM((1, blocks * count), jnp.float32),
            pltpu.VMEM((blocks, count), jnp.int32),
            pltpu.VMEM((pulses, lines, LANES), jnp.bfloat16),
            pltpu.VMEM((lines // 2 + span // LANES, 2 * pulses, LANES), jnp.bfloat16),
            pltpu.VMEM((2 * LANES, span), jnp.bfloat16),
        ]
        + [pltpu.VMEM((near * 2 * pulses, span), jnp.bfloat16)] * far
        + [
            pltpu.SemaphoreType.DMA((4,)),
        ],
        flops=6 * 10**9,
    )(me, sub, band_starts, chirp_ref, doppler_rates, slot_pulse.reshape(blocks, count), samples)

    subs = lax.axis_size("sub")

    def swap(value, by_core):
        pairs = [
            (one * tiles + tile, one * tiles + (tile ^ by_core[1 - (one & 1)]))
            for one in range(subs)
            for tile in range(tiles)
        ]
        return lax.ppermute(value, ("sub", "tile"), pairs)

    table = shape((parts, 2 * count, 2 * LANES), jnp.bfloat16)
    turned = shape((2, places * image_rows, band, LANES), jnp.bfloat16)
    first_table, second_table, mine = call(phase_kernel, "phase", 12, [table, table, own], [vmem()], flops=4 * 10**9)(extra)
    bands = [mine] + [
        swap(bands[dy - 1], (FIRST_Z[dy], FIRST_Y[dy] * near)) for dy in range(1, far)
    ]
    passed = call(
        relay_kernel,
        "relay",
        16,
        [shape((far, 2 * pulses, band), jnp.bfloat16)] * (near - 1),
        [anywhere] + [vmem()] * far,
    )(first_table, *bands)
    first_weights, second_weights = call(turn_kernel, "turn", 12, [turned, turned], [vmem(), anywhere], flops=4 * 10**9)(
        weights, passed[0]
    )
    passed = [swap(passed[dz - 1], (SECOND_Y[dz] * near, SECOND_Z[dz])) for dz in range(1, near)]
    sources = bands + passed
    half = (places // 4, 4 * image_rows, LANES)
    focused = [pltpu.VMEM((2 * band, 2 * LANES), jnp.float32)] * (2 * blocks)
    far_image, left = call(
        far_image_kernel,
        "far_image",
        12,
        [shape(half, jnp.bfloat16), shape((blocks, 2 * band, 2 * count), jnp.bfloat16)],
        [smem, smem] + [vmem()] * (4 + len(sources)),
        [pltpu.VMEM((tiles, 2 * pulses, band), jnp.bfloat16)] + focused,
        flops=3 * 10**9,
    )(me, sub, first_table, second_table, first_weights, second_weights, *sources)
    near_image = call(
        near_image_kernel, "near_image", 12, shape(half, jnp.float32), [smem] + [vmem()] * 5 + [anywhere], focused, flops=3 * 10**9
    )(sub, first_table, second_table, first_weights, second_weights, left, far_image)
    return sub, far_image, near_image


def shards(*args):
    _, far_image, near_image = partial_image(*args)
    size = 16
    half = size // 2
    came = lax.ppermute(far_image, "sub", [(one, one ^ half) for one in range(size)])
    groups = [list(range(half)), list(range(half, size))]
    held = (near_image + came.astype(jnp.float32)).reshape(half, -1, LANES)
    pieces = lax.all_to_all(held, "sub", 0, 0, axis_index_groups=groups, tiled=True)
    return jnp.sum(pieces, 0).reshape(2, -1, LANES)


def solution(mesh):
    in_specs = (
        P(("sub", "tile"), None, None),
        P(),
        P("sub", None),
        P("sub", None),
        P("sub", None, None),
        P("sub", None, None, "tile", None),
    )
    out_specs = P(None, "tile", "sub")
    return jax.shard_map(shards, mesh=mesh, in_specs=in_specs, out_specs=out_specs, check_vma=False)
```

```python
import jax
import jax.numpy as jnp
import numpy as np
from jax import lax
from jax.experimental import pallas as pl
from jax.experimental.pallas import tpu as pltpu
from jax.sharding import PartitionSpec as P

LANES = 128


def compress_kernel(
    me_ref, sub_ref, starts_ref, chirp_hbm, rates_hbm, slots_hbm, echoes_ref, *rest
):
    (
        *bands_refs, extra_ref, chirp_ref, rates_ref, slots_ref, raw_ref, samples_ref, toeplitz_ref,
        lhs_a, lhs_b, lhs_c, lhs_d, sems,
    ) = rest
    fetches = [
        pltpu.make_async_copy(source, target, sems.at[index])
        for index, (source, target) in enumerate(
            (
                (chirp_hbm, chirp_ref),
                (rates_hbm, rates_ref),
                (slots_hbm, slots_ref),
                (echoes_ref, raw_ref),
            )
        )
    ]
    for fetch in fetches:
        fetch.start()
    span = toeplitz_ref.shape[1]
    blocks, tiles = starts_ref.shape
    near = tiles // (len(bands_refs) + 1)
    pulses, lines, _ = raw_ref.shape
    half = pulses // blocks
    rows = 2 * half
    chunks = span // LANES
    samples_ref[lines // 2 :] = jnp.zeros(
        (samples_ref.shape[0] - lines // 2, 2 * pulses, LANES), jnp.bfloat16
    )
    piece = 16
    side = half * piece
    row = lax.broadcasted_iota(jnp.int32, (side, side), 0)
    col = lax.broadcasted_iota(jnp.int32, (side, side), 1)
    order = jnp.where(col == (row & (half - 1)) * piece + (row >> 4), 1.0, 0.0).astype(jnp.bfloat16)
    for fetch in fetches:
        fetch.wait()
    chirp = chirp_ref[...].astype(jnp.float32)
    pad = jnp.zeros((1, span - chirp.shape[1]), jnp.float32)
    for part in range(2):
        line = jnp.concatenate([chirp[part : part + 1], pad], 1)
        shifted = pltpu.roll(
            jnp.broadcast_to(line, (LANES, span)), 0, 1, stride=1, stride_axis=0
        ).astype(jnp.bfloat16)
        toeplitz_ref[part * LANES : (part + 1) * LANES, :] = shifted
    count = slots_ref.shape[1]
    row = lax.broadcasted_iota(jnp.int32, (count, count), 0)
    col = lax.broadcasted_iota(jnp.int32, (count, count), 1)
    for block in range(blocks):
        slots = slots_ref[block : block + 1, :].astype(jnp.float32)
        slot = jnp.sum(jnp.where(row == col, slots, 0.0), 1, keepdims=True)
        rates = rates_ref[:, block * count : (block + 1) * count]
        rate = jnp.sum(jnp.where(slot == col.astype(jnp.float32), rates, 0.0), 1, keepdims=True)
        extra_ref[block * count : (block + 1) * count, :] = jnp.broadcast_to(rate, (count, LANES))
    for group in range(lines // piece):
        block_rows = jnp.concatenate(
            [
                raw_ref[block * half : (block + 1) * half, group * piece : (group + 1) * piece, :].reshape(
                    side, LANES
                )
                for block in range(blocks)
            ],
            1,
        )
        moved = jnp.dot(order, block_rows, preferred_element_type=jnp.float32).astype(jnp.bfloat16)
        for block in range(blocks):
            samples_ref[
                group * piece // 2 : (group + 1) * piece // 2, block * rows : (block + 1) * rows, :
            ] = moved[:, block * LANES : (block + 1) * LANES].reshape(piece // 2, rows, LANES)
    lane = lax.broadcasted_iota(jnp.int32, (rows, LANES), 1)
    lhs_refs = (lhs_a, lhs_b, lhs_c, lhs_d)

    def gather(dy):
        for dz in range(near):
            for block in range(blocks):
                start = starts_ref[block, me_ref[0] ^ distance_of(sub_ref[0], dy, dz, near)]
                first = start >> 7
                shift = start & (LANES - 1)
                turn = (LANES - shift) & (LANES - 1)
                keep = lane < LANES - shift
                place = (dz * blocks + block) * rows

                def rolled(chunk):
                    line = samples_ref[first + chunk, block * rows : (block + 1) * rows, :]
                    return pltpu.roll(line, turn, 1)

                low = rolled(0)
                for chunk in range(chunks):
                    high = rolled(chunk + 1)
                    lhs_refs[dy][place : place + rows, chunk * LANES : (chunk + 1) * LANES] = jnp.where(
                        keep, low, high
                    )
                    low = high

    def correlate(dy):
        return lax.dot_general(
            lhs_refs[dy][...],
            toeplitz_ref[...],
            (((1,), (1,)), ((), ())),
            preferred_element_type=jnp.float32,
        )

    def cut(dy, product):
        for dz in range(near):
            for block in range(blocks):
                place = (dz * blocks + block) * rows
                real = product[place : place + half]
                imag = product[place + half : place + rows]
                for part, band in enumerate(
                    (real[:, :LANES] + imag[:, LANES:], imag[:, :LANES] - real[:, LANES:])
                ):
                    band = band.astype(jnp.bfloat16)
                    top = block * rows + part * half
                    if dy == 0:
                        top += blocks * count + dz * 2 * pulses
                        extra_ref[top : top + half, :] = band.astype(jnp.float32)
                    else:
                        bands_refs[dy - 1][dz, top : top + half, :] = band

    gather(0)
    for dy in range(len(lhs_refs)):
        if dy + 1 < len(lhs_refs):
            gather(dy + 1)
        cut(dy, correlate(dy))


FIRST_Z, FIRST_Y = (0, 3, 2, 1), (0, 2, 1, 3)
SECOND_Z, SECOND_Y = (0, 1, 3, 2), (0, 3, 2, 1)


def distance_of(sub, first, second, near):
    return jnp.where(
        (sub & 1) == 0,
        FIRST_Y[first] * near + SECOND_Z[second],
        SECOND_Y[second] * near + FIRST_Z[first],
    )


def sine_cosine(angle):
    turns = jnp.round(angle * np.float32(2 / np.pi))
    rest = (angle - turns * np.float32(1.5703125)) - turns * np.float32(np.pi / 2 - 1.5703125)
    quarter = turns.astype(jnp.int32)
    sq = rest * rest
    sine = np.float32(1 / 362880) * sq + np.float32(-1 / 5040)
    sine = sine * sq + np.float32(1 / 120)
    sine = sine * sq + np.float32(-1 / 6)
    sine = sine * sq * rest + rest
    cosine = np.float32(1 / 40320) * sq + np.float32(-1 / 720)
    cosine = cosine * sq + np.float32(1 / 24)
    cosine = cosine * sq + np.float32(-1 / 2)
    cosine = cosine * sq + np.float32(1)
    odd = (quarter & 1) == 1
    sin_out = jnp.where(odd, cosine, sine)
    cos_out = jnp.where(odd, sine, cosine)
    sin_out = jnp.where((quarter & 2) == 2, -sin_out, sin_out)
    cos_out = jnp.where(((quarter + 1) & 2) == 2, -cos_out, cos_out)
    return sin_out, cos_out


def phase_kernel(extra_ref, first_table_ref, second_table_ref, bands_ref):
    count = first_table_ref.shape[1] // 2
    bands_ref[...] = extra_ref[2 * count :].astype(jnp.bfloat16).reshape(bands_ref.shape)
    phase_table(0, extra_ref, first_table_ref)
    phase_table(1, extra_ref, second_table_ref)


def turn_kernel(weights_ref, after_ref, first_ref, second_ref):
    band = first_ref.shape[2]
    lines = first_ref.shape[1]
    size = 16
    side = size * size
    row = lax.broadcasted_iota(jnp.int32, (side, side), 0)
    col = lax.broadcasted_iota(jnp.int32, (side, side), 1)
    order = jnp.where(col == (row & (size - 1)) * size + (row >> 4), 1.0, 0.0).astype(jnp.bfloat16)
    for block, out_ref in enumerate((first_ref, second_ref)):
        for part in range(2):

            def step(chunk, carry, block=block, part=part, out_ref=out_ref):
                first = pl.multiple_of(chunk * size, size)
                for pair in range(lines // (2 * size)):
                    tops = [(2 * pair + one) * size for one in range(2)]
                    block_rows = jnp.concatenate(
                        [
                            weights_ref[
                                pl.ds((block * 2 + part) * band + first, size), top : top + size, :
                            ].reshape(side, LANES)
                            for top in tops
                        ],
                        1,
                    )
                    moved = jnp.dot(order, block_rows, preferred_element_type=jnp.float32).astype(
                        jnp.bfloat16
                    )
                    for one, top in enumerate(tops):
                        out_ref[part, top : top + size, pl.ds(first, size), :] = moved[
                            :, one * LANES : (one + 1) * LANES
                        ].reshape(size, size, LANES)
                return carry

            lax.fori_loop(0, band // size, step, 0, unroll=True)


def phase_table(block, rate_ref, table_ref):
    count = table_ref.shape[1] // 2
    columns = table_ref.shape[0] * table_ref.shape[2]
    lane = lax.broadcasted_iota(jnp.int32, (32, LANES), 1).astype(jnp.float32)
    place = (lane + 0.5) * np.float32(1 / columns) - 0.5
    for group in range(count // 32):
        span = slice(group * 32, group * 32 + 32)
        rate = rate_ref[block * count + group * 32 : block * count + group * 32 + 32, :]
        sine, cosine = sine_cosine(rate * place)
        step_sine, step_cosine = sine_cosine(rate * np.float32(LANES / columns))
        for chunk in range(columns // LANES):
            if chunk > 0:
                sine, cosine = (
                    sine * step_cosine + cosine * step_sine,
                    cosine * step_cosine - sine * step_sine,
                )
            lanes = slice(chunk % 2 * LANES, (chunk % 2 + 1) * LANES)
            table_ref[chunk // 2, span, lanes] = cosine.astype(jnp.bfloat16)
            table_ref[chunk // 2, count + group * 32 : count + group * 32 + 32, lanes] = (
                sine.astype(jnp.bfloat16)
            )


def relay_kernel(after_ref, *refs):
    near = refs[0].shape[0]
    far = len(refs) - near + 1
    for dz in range(1, near):
        for dy in range(far):
            refs[far + dz - 1][dy] = refs[dy][dz]


def fold_rows(values):
    row = lax.broadcasted_iota(jnp.int32, values[0].shape, 0)
    shift = 1
    while len(values) > 1:
        low = (row & shift) == 0
        values = [
            jnp.where(low, first, second) + pltpu.roll(jnp.where(low, second, first), 8 - shift, 0)
            for first, second in zip(values[::2], values[1::2])
        ]
        shift *= 2
    return values[0]


def weighted_sum(side, table_refs, weights_refs, image_ref, left_ref, focused_refs):
    blocks = len(table_refs)
    pairs, lines, _ = image_ref.shape
    places = 2 * pairs
    image_rows = lines // 4
    band = weights_refs[0].shape[2]

    def focus(pair):
        for block in range(blocks):
            focused_refs[pair % 2 * blocks + block][...] = jnp.dot(
                left_ref[block], table_refs[block][side * pairs + pair], preferred_element_type=jnp.float32
            )

    focus(0)
    for pair in range(pairs):
        if pair + 1 < pairs:
            focus(pair + 1)
        sums = []
        for place in range(2):
            lanes = slice(place * LANES, (place + 1) * LANES)
            real = [jnp.zeros((8, LANES), jnp.float32)] * image_rows
            imag = [jnp.zeros((8, LANES), jnp.float32)] * image_rows
            for block in range(blocks):
                focused_ref = focused_refs[pair % 2 * blocks + block]
                for k in range(0, band, 16):
                    focus_real = focused_ref[k : k + 16, lanes]
                    focus_imag = focused_ref[band + k : band + k + 16, lanes]
                    for row in range(image_rows):
                        line = (side * places + 2 * pair + place) * image_rows + row
                        weight_real = weights_refs[block][0, line, k : k + 16, :].astype(jnp.float32)
                        weight_imag = weights_refs[block][1, line, k : k + 16, :].astype(jnp.float32)
                        for first in (0, 8):
                            part = slice(first, first + 8)
                            wr, wi = weight_real[part], weight_imag[part]
                            fr, fi = focus_real[part], focus_imag[part]
                            real[row] = real[row] + (wr * fr - wi * fi)
                            imag[row] = imag[row] + (wr * fi + wi * fr)
            sums.append(fold_rows(real + imag))
        image_ref[pair] = jnp.concatenate(sums, 0).astype(image_ref.dtype)


def far_image_kernel(
    me_ref, sub_ref, first_table_ref, second_table_ref, first_weights_ref, second_weights_ref, *rest
):
    *sources_refs, image_ref, left_ref, bands_ref, one_ref, two_ref, three_ref, four_ref = rest
    sources, band_rows, band = bands_ref.shape
    far_count = len(sources_refs) // 2 + 1
    near_refs, far_refs = sources_refs[:far_count], sources_refs[far_count:]
    near = sources // far_count
    blocks = left_ref.shape[0]
    rows = band_rows // blocks
    half = rows // 2
    count = sources * half
    for dy in range(far_count):
        bands_ref[me_ref[0] ^ distance_of(sub_ref[0], dy, 0, near)] = near_refs[dy][0]
        for dz in range(1, near):
            bands_ref[me_ref[0] ^ distance_of(sub_ref[0], dy, dz, near)] = far_refs[dz - 1][dy]
    for block in range(blocks):
        real = bands_ref[:, block * rows : block * rows + half, :].reshape(count, band)
        imag = bands_ref[:, block * rows + half : (block + 1) * rows, :].reshape(count, band)
        top = jnp.concatenate([real, imag], 1)
        bottom = jnp.concatenate([-imag, real], 1)
        left_ref[block] = jnp.concatenate([top, bottom], 0).T
    weighted_sum(
        1 - (sub_ref[0] >> 3),
        (first_table_ref, second_table_ref),
        (first_weights_ref, second_weights_ref),
        image_ref,
        left_ref,
        (one_ref, two_ref, three_ref, four_ref),
    )


def near_image_kernel(
    sub_ref, first_table_ref, second_table_ref, first_weights_ref, second_weights_ref, left_ref, after_ref,
    image_ref, one_ref, two_ref, three_ref, four_ref,
):
    weighted_sum(
        sub_ref[0] >> 3,
        (first_table_ref, second_table_ref),
        (first_weights_ref, second_weights_ref),
        image_ref,
        left_ref,
        (one_ref, two_ref, three_ref, four_ref),
    )


def params(mib):
    return pltpu.CompilerParams(vmem_limit_bytes=mib * 1024 * 1024)


def vmem():
    return pl.BlockSpec(memory_space=pltpu.VMEM)


def call(kernel, name, mib, out_shape, in_specs, scratch=(), flops=0):
    multiple = isinstance(out_shape, list)
    return pl.pallas_call(
        kernel,
        out_shape=out_shape,
        in_specs=in_specs,
        out_specs=[vmem()] * len(out_shape) if multiple else vmem(),
        scratch_shapes=list(scratch),
        compiler_params=params(mib),
        cost_estimate=pl.CostEstimate(flops=flops, bytes_accessed=0, transcendentals=0),
        name=name,
    )


def partial_image(echoes, chirp_ref, band_starts, doppler_rates, slot_pulse, interp_weights):
    pulses, _, pulse_len = echoes.shape
    chirp_len = chirp_ref.shape[1]
    blocks, tiles = band_starts.shape
    _, _, band, image_rows, columns = interp_weights.shape
    count = slot_pulse.shape[2]
    lines = 2 * pulse_len // LANES
    span = chirp_len + LANES
    places = columns // LANES
    parts = places // 2
    near = 4
    far = tiles // near
    smem = pl.BlockSpec(memory_space=pltpu.SMEM)
    anywhere = pl.BlockSpec(memory_space=pl.ANY)
    shape = jax.ShapeDtypeStruct
    sub = lax.axis_index("sub").astype(jnp.int32).reshape(1)
    me = lax.axis_index("tile").astype(jnp.int32).reshape(1)

    samples = echoes.reshape(pulses, 2, pulse_len // LANES, LANES).transpose(0, 2, 1, 3)
    samples = samples.reshape(pulses, lines, LANES)
    weights = interp_weights.reshape(blocks, 2, band, image_rows, places, LANES)
    weights = weights.transpose(0, 1, 2, 4, 3, 5).reshape(
        blocks * 2 * band, places * image_rows, LANES
    )
    own = shape((near, 2 * pulses, band), jnp.bfloat16)
    extras = shape((blocks * count + near * 2 * pulses, LANES), jnp.float32)
    *bands, extra = call(
        compress_kernel,
        "compress",
        60,
        [own] * (far - 1) + [extras],
        [smem] * 3 + [anywhere] * 4,
        [
            pltpu.VMEM((2, chirp_len), jnp.bfloat16),
            pltpu.VMEM((1, blocks * count), jnp.float32),
            pltpu.VMEM((blocks, count), jnp.int32),
            pltpu.VMEM((pulses, lines, LANES), jnp.bfloat16),
            pltpu.VMEM((lines // 2 + span // LANES, 2 * pulses, LANES), jnp.bfloat16),
            pltpu.VMEM((2 * LANES, span), jnp.bfloat16),
        ]
        + [pltpu.VMEM((near * 2 * pulses, span), jnp.bfloat16)] * far
        + [
            pltpu.SemaphoreType.DMA((4,)),
        ],
        flops=6 * 10**9,
    )(me, sub, band_starts, chirp_ref, doppler_rates, slot_pulse.reshape(blocks, count), samples)

    subs = lax.axis_size("sub")

    def swap(value, by_core):
        pairs = [
            (one * tiles + tile, one * tiles + (tile ^ by_core[1 - (one & 1)]))
            for one in range(subs)
            for tile in range(tiles)
        ]
        return lax.ppermute(value, ("sub", "tile"), pairs)

    table = shape((parts, 2 * count, 2 * LANES), jnp.bfloat16)
    turned = shape((2, places * image_rows, band, LANES), jnp.bfloat16)
    first_table, second_table, mine = call(phase_kernel, "phase", 12, [table, table, own], [vmem()], flops=4 * 10**9)(extra)
    bands = [mine] + [
        swap(bands[dy - 1], (FIRST_Z[dy], FIRST_Y[dy] * near)) for dy in range(1, far)
    ]
    passed = call(
        relay_kernel,
        "relay",
        16,
        [shape((far, 2 * pulses, band), jnp.bfloat16)] * (near - 1),
        [anywhere] + [vmem()] * far,
    )(first_table, *bands)
    first_weights, second_weights = call(turn_kernel, "turn", 12, [turned, turned], [vmem(), anywhere], flops=4 * 10**9)(
        weights, passed[0]
    )
    passed = [swap(passed[dz - 1], (SECOND_Y[dz] * near, SECOND_Z[dz])) for dz in range(1, near)]
    sources = bands + passed
    half = (places // 4, 4 * image_rows, LANES)
    focused = [pltpu.VMEM((2 * band, 2 * LANES), jnp.float32)] * (2 * blocks)
    far_image, left = call(
        far_image_kernel,
        "far_image",
        12,
        [shape(half, jnp.float32), shape((blocks, 2 * band, 2 * count), jnp.bfloat16)],
        [smem, smem] + [vmem()] * (4 + len(sources)),
        [pltpu.VMEM((tiles, 2 * pulses, band), jnp.bfloat16)] + focused,
        flops=3 * 10**9,
    )(me, sub, first_table, second_table, first_weights, second_weights, *sources)
    near_image = call(
        near_image_kernel, "near_image", 12, shape(half, jnp.float32), [smem] + [vmem()] * 5 + [anywhere], focused, flops=3 * 10**9
    )(sub, first_table, second_table, first_weights, second_weights, left, far_image)
    return sub, far_image, near_image


def shards(*args):
    _, far_image, near_image = partial_image(*args)
    size = 16
    half = size // 2
    came = lax.ppermute(far_image, "sub", [(one, one ^ half) for one in range(size)])
    groups = [list(range(half)), list(range(half, size))]
    held = (near_image + came).reshape(half, -1, LANES)
    pieces = lax.all_to_all(held, "sub", 0, 0, axis_index_groups=groups, tiled=True)
    return jnp.sum(pieces, 0).reshape(2, -1, LANES)


def solution(mesh):
    in_specs = (
        P(("sub", "tile"), None, None),
        P(),
        P("sub", None),
        P("sub", None),
        P("sub", None, None),
        P("sub", None, None, "tile", None),
    )
    out_specs = P(None, "tile", "sub")
    return jax.shard_map(shards, mesh=mesh, in_specs=in_specs, out_specs=out_specs, check_vma=False)
```

```python
import jax
import jax.numpy as jnp
import numpy as np
from jax import lax
from jax.experimental import pallas as pl
from jax.experimental.pallas import tpu as pltpu
from jax.sharding import PartitionSpec as P

LANES = 128


def compress_kernel(
    me_ref, sub_ref, starts_ref, chirp_hbm, rates_hbm, slots_hbm, echoes_ref, *rest
):
    (
        *bands_refs, extra_ref, chirp_ref, rates_ref, slots_ref, raw_ref, samples_ref, toeplitz_ref,
        lhs_a, lhs_b, lhs_c, lhs_d, sems,
    ) = rest
    fetches = [
        pltpu.make_async_copy(source, target, sems.at[index])
        for index, (source, target) in enumerate(
            (
                (chirp_hbm, chirp_ref),
                (rates_hbm, rates_ref),
                (slots_hbm, slots_ref),
                (echoes_ref, raw_ref),
            )
        )
    ]
    for fetch in fetches:
        fetch.start()
    span = toeplitz_ref.shape[1]
    blocks, tiles = starts_ref.shape
    near = tiles // (len(bands_refs) + 1)
    pulses, lines, _ = raw_ref.shape
    half = pulses // blocks
    rows = 2 * half
    chunks = span // LANES
    samples_ref[lines // 2 :] = jnp.zeros(
        (samples_ref.shape[0] - lines // 2, 2 * pulses, LANES), jnp.bfloat16
    )
    piece = 16
    side = half * piece
    row = lax.broadcasted_iota(jnp.int32, (side, side), 0)
    col = lax.broadcasted_iota(jnp.int32, (side, side), 1)
    order = jnp.where(col == (row & (half - 1)) * piece + (row >> 4), 1.0, 0.0).astype(jnp.bfloat16)
    for fetch in fetches:
        fetch.wait()
    chirp = chirp_ref[...].astype(jnp.float32)
    pad = jnp.zeros((1, span - chirp.shape[1]), jnp.float32)
    for part in range(2):
        line = jnp.concatenate([chirp[part : part + 1], pad], 1)
        shifted = pltpu.roll(
            jnp.broadcast_to(line, (LANES, span)), 0, 1, stride=1, stride_axis=0
        ).astype(jnp.bfloat16)
        toeplitz_ref[part * LANES : (part + 1) * LANES, :] = shifted
    count = slots_ref.shape[1]
    row = lax.broadcasted_iota(jnp.int32, (count, count), 0)
    col = lax.broadcasted_iota(jnp.int32, (count, count), 1)
    for block in range(blocks):
        slots = slots_ref[block : block + 1, :].astype(jnp.float32)
        slot = jnp.sum(jnp.where(row == col, slots, 0.0), 1, keepdims=True)
        rates = rates_ref[:, block * count : (block + 1) * count]
        rate = jnp.sum(jnp.where(slot == col.astype(jnp.float32), rates, 0.0), 1, keepdims=True)
        extra_ref[block * count : (block + 1) * count, :] = jnp.broadcast_to(rate, (count, LANES))
    for group in range(lines // piece):
        block_rows = jnp.concatenate(
            [
                raw_ref[block * half : (block + 1) * half, group * piece : (group + 1) * piece, :].reshape(
                    side, LANES
                )
                for block in range(blocks)
            ],
            1,
        )
        moved = jnp.dot(order, block_rows, preferred_element_type=jnp.float32).astype(jnp.bfloat16)
        for block in range(blocks):
            samples_ref[
                group * piece // 2 : (group + 1) * piece // 2, block * rows : (block + 1) * rows, :
            ] = moved[:, block * LANES : (block + 1) * LANES].reshape(piece // 2, rows, LANES)
    lane = lax.broadcasted_iota(jnp.int32, (rows, LANES), 1)
    lhs_refs = (lhs_a, lhs_b, lhs_c, lhs_d)

    def gather(dy):
        for dz in range(near):
            for block in range(blocks):
                start = starts_ref[block, me_ref[0] ^ distance_of(sub_ref[0], dy, dz, near)]
                first = start >> 7
                shift = start & (LANES - 1)
                turn = (LANES - shift) & (LANES - 1)
                keep = lane < LANES - shift
                place = (dz * blocks + block) * rows

                def rolled(chunk):
                    line = samples_ref[first + chunk, block * rows : (block + 1) * rows, :]
                    return pltpu.roll(line, turn, 1)

                low = rolled(0)
                for chunk in range(chunks):
                    high = rolled(chunk + 1)
                    lhs_refs[dy][place : place + rows, chunk * LANES : (chunk + 1) * LANES] = jnp.where(
                        keep, low, high
                    )
                    low = high

    def correlate(dy):
        return lax.dot_general(
            lhs_refs[dy][...],
            toeplitz_ref[...],
            (((1,), (1,)), ((), ())),
            preferred_element_type=jnp.float32,
        )

    def cut(dy, product):
        for dz in range(near):
            for block in range(blocks):
                place = (dz * blocks + block) * rows
                real = product[place : place + half]
                imag = product[place + half : place + rows]
                for part, band in enumerate(
                    (real[:, :LANES] + imag[:, LANES:], imag[:, :LANES] - real[:, LANES:])
                ):
                    band = band.astype(jnp.bfloat16)
                    top = block * rows + part * half
                    if dy == 0:
                        top += blocks * count + dz * 2 * pulses
                        extra_ref[top : top + half, :] = band.astype(jnp.float32)
                    else:
                        bands_refs[dy - 1][dz, top : top + half, :] = band

    gather(0)
    for dy in range(len(lhs_refs)):
        if dy + 1 < len(lhs_refs):
            gather(dy + 1)
        cut(dy, correlate(dy))


FIRST_Z, FIRST_Y = (0, 3, 2, 1), (0, 2, 1, 3)
SECOND_Z, SECOND_Y = (0, 1, 3, 2), (0, 3, 2, 1)


def distance_of(sub, first, second, near):
    return jnp.where(
        (sub & 1) == 0,
        FIRST_Y[first] * near + SECOND_Z[second],
        SECOND_Y[second] * near + FIRST_Z[first],
    )


def sine_cosine(angle):
    turns = jnp.round(angle * np.float32(2 / np.pi))
    rest = (angle - turns * np.float32(1.5703125)) - turns * np.float32(np.pi / 2 - 1.5703125)
    quarter = turns.astype(jnp.int32)
    sq = rest * rest
    sine = np.float32(1 / 362880) * sq + np.float32(-1 / 5040)
    sine = sine * sq + np.float32(1 / 120)
    sine = sine * sq + np.float32(-1 / 6)
    sine = sine * sq * rest + rest
    cosine = np.float32(1 / 40320) * sq + np.float32(-1 / 720)
    cosine = cosine * sq + np.float32(1 / 24)
    cosine = cosine * sq + np.float32(-1 / 2)
    cosine = cosine * sq + np.float32(1)
    odd = (quarter & 1) == 1
    sin_out = jnp.where(odd, cosine, sine)
    cos_out = jnp.where(odd, sine, cosine)
    sin_out = jnp.where((quarter & 2) == 2, -sin_out, sin_out)
    cos_out = jnp.where(((quarter + 1) & 2) == 2, -cos_out, cos_out)
    return sin_out, cos_out


def phase_kernel(extra_ref, first_table_ref, second_table_ref, bands_ref):
    count = first_table_ref.shape[1] // 2
    bands_ref[...] = extra_ref[2 * count :].astype(jnp.bfloat16).reshape(bands_ref.shape)
    phase_table(0, extra_ref, first_table_ref)
    phase_table(1, extra_ref, second_table_ref)


def turn_kernel(weights_ref, after_ref, first_ref, second_ref):
    band = first_ref.shape[2]
    lines = first_ref.shape[1]
    size = 16
    side = size * size
    row = lax.broadcasted_iota(jnp.int32, (side, side), 0)
    col = lax.broadcasted_iota(jnp.int32, (side, side), 1)
    order = jnp.where(col == (row & (size - 1)) * size + (row >> 4), 1.0, 0.0).astype(jnp.bfloat16)
    for block, out_ref in enumerate((first_ref, second_ref)):
        for part in range(2):

            def step(chunk, carry, block=block, part=part, out_ref=out_ref):
                first = pl.multiple_of(chunk * size, size)
                for pair in range(lines // (2 * size)):
                    tops = [(2 * pair + one) * size for one in range(2)]
                    block_rows = jnp.concatenate(
                        [
                            weights_ref[
                                pl.ds((block * 2 + part) * band + first, size), top : top + size, :
                            ].reshape(side, LANES)
                            for top in tops
                        ],
                        1,
                    )
                    moved = jnp.dot(order, block_rows, preferred_element_type=jnp.float32).astype(
                        jnp.bfloat16
                    )
                    for one, top in enumerate(tops):
                        out_ref[part, top : top + size, pl.ds(first, size), :] = moved[
                            :, one * LANES : (one + 1) * LANES
                        ].reshape(size, size, LANES)
                return carry

            lax.fori_loop(0, band // size, step, 0, unroll=True)


def phase_table(block, rate_ref, table_ref):
    count = table_ref.shape[1] // 2
    columns = table_ref.shape[0] * table_ref.shape[2]
    lane = lax.broadcasted_iota(jnp.int32, (32, LANES), 1).astype(jnp.float32)
    place = (lane + 0.5) * np.float32(1 / columns) - 0.5
    for group in range(count // 32):
        span = slice(group * 32, group * 32 + 32)
        rate = rate_ref[block * count + group * 32 : block * count + group * 32 + 32, :]
        sine, cosine = sine_cosine(rate * place)
        step_sine, step_cosine = sine_cosine(rate * np.float32(LANES / columns))
        for chunk in range(columns // LANES):
            if chunk > 0:
                sine, cosine = (
                    sine * step_cosine + cosine * step_sine,
                    cosine * step_cosine - sine * step_sine,
                )
            lanes = slice(chunk % 2 * LANES, (chunk % 2 + 1) * LANES)
            table_ref[chunk // 2, span, lanes] = cosine.astype(jnp.bfloat16)
            table_ref[chunk // 2, count + group * 32 : count + group * 32 + 32, lanes] = (
                sine.astype(jnp.bfloat16)
            )


def relay_kernel(after_ref, *refs):
    near = refs[0].shape[0]
    far = len(refs) - near + 1
    for dz in range(1, near):
        for dy in range(far):
            refs[far + dz - 1][dy] = refs[dy][dz]


def fold_rows(values):
    row = lax.broadcasted_iota(jnp.int32, values[0].shape, 0)
    shift = 1
    while len(values) > 1:
        low = (row & shift) == 0
        values = [
            jnp.where(low, first, second) + pltpu.roll(jnp.where(low, second, first), 8 - shift, 0)
            for first, second in zip(values[::2], values[1::2])
        ]
        shift *= 2
    return values[0]


def weighted_sum(side, table_refs, weights_refs, image_ref, left_ref, focused_refs):
    blocks = len(table_refs)
    pairs, lines, _ = image_ref.shape
    places = 2 * pairs
    image_rows = lines // 4
    band = weights_refs[0].shape[2]

    def focus(pair):
        for block in range(blocks):
            focused_refs[pair % 2 * blocks + block][...] = jnp.dot(
                left_ref[block], table_refs[block][side * pairs + pair], preferred_element_type=jnp.float32
            )

    focus(0)
    for pair in range(pairs):
        if pair + 1 < pairs:
            focus(pair + 1)
        sums = []
        for place in range(2):
            lanes = slice(place * LANES, (place + 1) * LANES)
            real = [jnp.zeros((8, LANES), jnp.float32)] * image_rows
            imag = [jnp.zeros((8, LANES), jnp.float32)] * image_rows
            for block in range(blocks):
                focused_ref = focused_refs[pair % 2 * blocks + block]
                for k in range(0, band, 16):
                    focus_real = focused_ref[k : k + 16, lanes]
                    focus_imag = focused_ref[band + k : band + k + 16, lanes]
                    for row in range(image_rows):
                        line = (side * places + 2 * pair + place) * image_rows + row
                        weight_real = weights_refs[block][0, line, k : k + 16, :].astype(jnp.float32)
                        weight_imag = weights_refs[block][1, line, k : k + 16, :].astype(jnp.float32)
                        for first in (0, 8):
                            part = slice(first, first + 8)
                            wr, wi = weight_real[part], weight_imag[part]
                            fr, fi = focus_real[part], focus_imag[part]
                            real[row] = real[row] + (wr * fr - wi * fi)
                            imag[row] = imag[row] + (wr * fi + wi * fr)
            sums.append(fold_rows(real + imag))
        image_ref[pair] = jnp.concatenate(sums, 0).astype(image_ref.dtype)


def far_image_kernel(
    me_ref, sub_ref, first_table_ref, second_table_ref, first_weights_ref, second_weights_ref, *rest
):
    *sources_refs, image_ref, left_ref, bands_ref, one_ref, two_ref, three_ref, four_ref = rest
    sources, band_rows, band = bands_ref.shape
    far_count = len(sources_refs) // 2 + 1
    near_refs, far_refs = sources_refs[:far_count], sources_refs[far_count:]
    near = sources // far_count
    blocks = left_ref.shape[0]
    rows = band_rows // blocks
    half = rows // 2
    count = sources * half
    for dy in range(far_count):
        bands_ref[me_ref[0] ^ distance_of(sub_ref[0], dy, 0, near)] = near_refs[dy][0]
        for dz in range(1, near):
            bands_ref[me_ref[0] ^ distance_of(sub_ref[0], dy, dz, near)] = far_refs[dz - 1][dy]
    for block in range(blocks):
        real = bands_ref[:, block * rows : block * rows + half, :].reshape(count, band)
        imag = bands_ref[:, block * rows + half : (block + 1) * rows, :].reshape(count, band)
        top = jnp.concatenate([real, imag], 1)
        bottom = jnp.concatenate([-imag, real], 1)
        left_ref[block] = jnp.concatenate([top, bottom], 0).T
    weighted_sum(
        1 - (sub_ref[0] >> 3),
        (first_table_ref, second_table_ref),
        (first_weights_ref, second_weights_ref),
        image_ref,
        left_ref,
        (one_ref, two_ref, three_ref, four_ref),
    )


def near_image_kernel(
    sub_ref, first_table_ref, second_table_ref, first_weights_ref, second_weights_ref, left_ref, after_ref,
    image_ref, one_ref, two_ref, three_ref, four_ref,
):
    weighted_sum(
        sub_ref[0] >> 3,
        (first_table_ref, second_table_ref),
        (first_weights_ref, second_weights_ref),
        image_ref,
        left_ref,
        (one_ref, two_ref, three_ref, four_ref),
    )


ACROSS = (0, 2, 1, 3)


def split_kernel(sub_ref, mine_ref, came_ref, *out_refs):
    for distance, out_ref in zip(ACROSS, out_refs):
        at = (sub_ref[0] >> 1 & 3) ^ distance
        out_ref[...] = mine_ref[at] + came_ref[at]


def join_kernel(sub_ref, *refs):
    *piece_refs, keep_ref, send_ref = refs
    total = (piece_refs[0][...] + piece_refs[1][...]) + (piece_refs[2][...] + piece_refs[3][...])
    own_first = (sub_ref[0] & 1) == 0
    keep_ref[...] = jnp.where(own_first, total[:8], total[8:])
    send_ref[...] = jnp.where(own_first, total[8:], total[:8])


def params(mib):
    return pltpu.CompilerParams(vmem_limit_bytes=mib * 1024 * 1024)


def vmem():
    return pl.BlockSpec(memory_space=pltpu.VMEM)


def call(kernel, name, mib, out_shape, in_specs, scratch=(), flops=0):
    multiple = isinstance(out_shape, list)
    return pl.pallas_call(
        kernel,
        out_shape=out_shape,
        in_specs=in_specs,
        out_specs=[vmem()] * len(out_shape) if multiple else vmem(),
        scratch_shapes=list(scratch),
        compiler_params=params(mib),
        cost_estimate=pl.CostEstimate(flops=flops, bytes_accessed=0, transcendentals=0),
        name=name,
    )


def partial_image(echoes, chirp_ref, band_starts, doppler_rates, slot_pulse, interp_weights):
    pulses, _, pulse_len = echoes.shape
    chirp_len = chirp_ref.shape[1]
    blocks, tiles = band_starts.shape
    _, _, band, image_rows, columns = interp_weights.shape
    count = slot_pulse.shape[2]
    lines = 2 * pulse_len // LANES
    span = chirp_len + LANES
    places = columns // LANES
    parts = places // 2
    near = 4
    far = tiles // near
    smem = pl.BlockSpec(memory_space=pltpu.SMEM)
    anywhere = pl.BlockSpec(memory_space=pl.ANY)
    shape = jax.ShapeDtypeStruct
    sub = lax.axis_index("sub").astype(jnp.int32).reshape(1)
    me = lax.axis_index("tile").astype(jnp.int32).reshape(1)

    samples = echoes.reshape(pulses, 2, pulse_len // LANES, LANES).transpose(0, 2, 1, 3)
    samples = samples.reshape(pulses, lines, LANES)
    weights = interp_weights.reshape(blocks, 2, band, image_rows, places, LANES)
    weights = weights.transpose(0, 1, 2, 4, 3, 5).reshape(
        blocks * 2 * band, places * image_rows, LANES
    )
    own = shape((near, 2 * pulses, band), jnp.bfloat16)
    extras = shape((blocks * count + near * 2 * pulses, LANES), jnp.float32)
    *bands, extra = call(
        compress_kernel,
        "compress",
        60,
        [own] * (far - 1) + [extras],
        [smem] * 3 + [anywhere] * 4,
        [
            pltpu.VMEM((2, chirp_len), jnp.bfloat16),
            pltpu.VMEM((1, blocks * count), jnp.float32),
            pltpu.VMEM((blocks, count), jnp.int32),
            pltpu.VMEM((pulses, lines, LANES), jnp.bfloat16),
            pltpu.VMEM((lines // 2 + span // LANES, 2 * pulses, LANES), jnp.bfloat16),
            pltpu.VMEM((2 * LANES, span), jnp.bfloat16),
        ]
        + [pltpu.VMEM((near * 2 * pulses, span), jnp.bfloat16)] * far
        + [
            pltpu.SemaphoreType.DMA((4,)),
        ],
        flops=6 * 10**9,
    )(me, sub, band_starts, chirp_ref, doppler_rates, slot_pulse.reshape(blocks, count), samples)

    subs = lax.axis_size("sub")

    def swap(value, by_core):
        pairs = [
            (one * tiles + tile, one * tiles + (tile ^ by_core[1 - (one & 1)]))
            for one in range(subs)
            for tile in range(tiles)
        ]
        return lax.ppermute(value, ("sub", "tile"), pairs)

    table = shape((parts, 2 * count, 2 * LANES), jnp.bfloat16)
    turned = shape((2, places * image_rows, band, LANES), jnp.bfloat16)
    first_table, second_table, mine = call(phase_kernel, "phase", 12, [table, table, own], [vmem()], flops=4 * 10**9)(extra)
    bands = [mine] + [
        swap(bands[dy - 1], (FIRST_Z[dy], FIRST_Y[dy] * near)) for dy in range(1, far)
    ]
    passed = call(
        relay_kernel,
        "relay",
        16,
        [shape((far, 2 * pulses, band), jnp.bfloat16)] * (near - 1),
        [anywhere] + [vmem()] * far,
    )(first_table, *bands)
    first_weights, second_weights = call(turn_kernel, "turn", 12, [turned, turned], [vmem(), anywhere], flops=4 * 10**9)(
        weights, passed[0]
    )
    passed = [swap(passed[dz - 1], (SECOND_Y[dz] * near, SECOND_Z[dz])) for dz in range(1, near)]
    sources = bands + passed
    half = (places // 4, 4 * image_rows, LANES)
    focused = [pltpu.VMEM((2 * band, 2 * LANES), jnp.float32)] * (2 * blocks)
    far_image, left = call(
        far_image_kernel,
        "far_image",
        12,
        [shape(half, jnp.float32), shape((blocks, 2 * band, 2 * count), jnp.bfloat16)],
        [smem, smem] + [vmem()] * (4 + len(sources)),
        [pltpu.VMEM((tiles, 2 * pulses, band), jnp.bfloat16)] + focused,
        flops=3 * 10**9,
    )(me, sub, first_table, second_table, first_weights, second_weights, *sources)
    near_image = call(
        near_image_kernel, "near_image", 12, shape(half, jnp.float32), [smem] + [vmem()] * 5 + [anywhere], focused, flops=3 * 10**9
    )(sub, first_table, second_table, first_weights, second_weights, left, far_image)
    return sub, far_image, near_image


def shards(*args):
    sub, far_image, near_image = partial_image(*args)
    size = 16

    def swap(value, distance):
        return lax.ppermute(value, "sub", [(one, one ^ distance) for one in range(size)])

    smem = pl.BlockSpec(memory_space=pltpu.SMEM)
    _, lines, _ = near_image.shape
    pair = jax.ShapeDtypeStruct((lines, LANES), jnp.float32)
    one = jax.ShapeDtypeStruct((lines // 2, LANES), jnp.float32)
    came = swap(far_image, size // 2)
    pieces = call(split_kernel, "split", 12, [pair] * 4, [smem, vmem(), vmem()])(sub, near_image, came)
    pieces = [pieces[0]] + [swap(pieces[slot], 2 * ACROSS[slot]) for slot in range(1, 4)]
    keep, send = call(join_kernel, "join", 12, [one, one], [smem] + [vmem()] * 4)(sub, *pieces)
    return (keep + swap(send, 1)).reshape(2, -1, LANES)


def solution(mesh):
    in_specs = (
        P(("sub", "tile"), None, None),
        P(),
        P("sub", None),
        P("sub", None),
        P("sub", None, None),
        P("sub", None, None, "tile", None),
    )
    out_specs = P(None, "tile", "sub")
    return jax.shard_map(shards, mesh=mesh, in_specs=in_specs, out_specs=out_specs, check_vma=False)
```
